32 devices in a mesh: lat: 4 (over y, x), lon: 8 (over z, core).
Axes of the slice: x: 2, y: 2, z: 4, core: 2. Of those that a mesh axis runs over, the one named last changes fastest.
Arguments:
- queries: float32 [16, 256, 512], P('lat', 'lon'), may hold values from -80 to 80
- key_rows: float32 [32, 512], P(('lat', 'lon')), may hold values from -8 to 8
- value_rows: float32 [32, 512], P(('lat', 'lon')), may hold values from -6 to 6
- cotangent: float32 [16, 256, 512], P('lat', 'lon'), may hold values from -25 to 25
- conv_taps: float32 [9, 512], replicated, may hold values from -1.75 to 1.75
Outputs:
- query_grad: float32 [16, 256, 512], P('lat', 'lon')
- key_grad: float32 [32, 512], P(('lat', 'lon'))
- value_grad: float32 [32, 512], P(('lat', 'lon'))
- tap_update: float32 [9, 512], replicated
The draws below stay inside these ranges and needn't reach their ends.
All inputs are finite; a program needn't handle non-finite values.
Results may differ from the reference program's by a relative error of at most 0.0003.
Values sent between devices are 32-bit elements; how exact they have to be, the bound alone decides.
No kernel may reach another device: no remote copies, remote signals or barrier semaphores. Data moves between devices by JAX's collectives and lax.ppermute only.
A program may use at most 64 MiB of HBM per device.

```python
import math
import jax
import jax.numpy as jnp
from jax import lax

HD = 64
CH = 512
NLAT = 16
NLON = 256
KEYS = 32


def attention_inputs(key):
    base_key = jax.random.fold_in(key, 7)
    key_keys, key_queries = jax.random.split(base_key, 2)
    key_table = 2.0 * jnp.clip(jax.random.normal(key_keys, (KEYS, CH), jnp.float32), -4.0, 4.0)
    query_table = jnp.clip(jax.random.normal(key_queries, (NLAT * NLON, CH), jnp.float32), -4.0, 4.0)
    return (query_table.reshape(NLAT, NLON, CH), key_table)


def draw_queries(key, part):
    return attention_inputs(key)[0]


def draw_key_rows(key, part):
    return attention_inputs(key)[1]


def draw_cotangent(key, part):
    key_scale, key_noise = jax.random.split(jax.random.fold_in(key, 11), 2)
    channel_scale = jnp.exp(jax.random.uniform(key_scale, (CH,), jnp.float32, math.log(0.3), math.log(3.0)))
    return jnp.clip(jax.random.normal(key_noise, (NLAT, NLON, CH), jnp.float32), -4.0, 4.0) * channel_scale


def levels(stream_key, extent, shards, low, largest):
    factor_of = 1.0
    for dim, parts in shards:
        draws = jax.random.uniform(jax.random.fold_in(jax.random.fold_in(stream_key, 6), dim), (parts,), jnp.float32, low / len(shards), largest / len(shards))
        factor_of = factor_of * jnp.repeat(jnp.exp(draws), extent[dim] // parts).reshape((-1,) + (1,) * (len(extent) - 1 - dim))
    return factor_of


def normal_values(stream_key, dims, spread, most, pieces=(), held_as=jnp.bfloat16):
    result = spread * jax.random.normal(stream_key, dims, jnp.float32)
    if pieces:
        result = result * levels(stream_key, dims, pieces, -0.22, 0.18)
    return jnp.clip(result, -most, most).astype(held_as)


def setup_inputs(seed: int = 0) -> dict:
    key_list = jax.random.split(jax.random.key(seed), 6)
    queries = draw_queries(jax.random.fold_in(key_list[5], 71), 0)
    key_rows = draw_key_rows(jax.random.fold_in(key_list[5], 71), 0)
    value_rows = normal_values(key_list[2], (KEYS, CH), 1.0, 6.0, ((0, 32),), jnp.float32)
    cotangent = draw_cotangent(jax.random.fold_in(key_list[5], 71), 0)
    conv_taps = normal_values(key_list[4], (9, CH), 0.35, 1.75, (), jnp.float32)
    return dict(queries=queries, key_rows=key_rows, value_rows=value_rows, cotangent=cotangent, conv_taps=conv_taps)


HIGH = lax.Precision.HIGHEST
OFFSETS = ((-1, -1), (-1, 0), (-1, 1), (0, -1), (0, 0), (0, 1), (1, -1), (1, 0), (1, 1))

def split_heads(matrix):
    return matrix.reshape(matrix.shape[0], -1, HD)

def soft_scores(query_part, key_part):
    logits = jnp.einsum('qhd,khd->hqk', split_heads(query_part), split_heads(key_part), precision=HIGH) * HD ** (-0.5)
    row_peak = lax.optimization_barrier(jnp.max(logits, -1, keepdims=True))
    raised = jnp.exp(logits - row_peak)
    return raised / lax.optimization_barrier(jnp.sum(raised, -1, keepdims=True))

def latitude_weights():
    centres = (jnp.arange(NLAT, dtype=jnp.float32) + 0.5) * (jnp.pi / NLAT)
    cosine = jnp.sin(centres)
    return cosine / (jnp.sum(cosine) / NLAT)

def pad_field(grid_field):
    wrapped = jnp.pad(grid_field, ((0, 0), (1, 1), (0, 0)), mode='wrap')
    return jnp.pad(wrapped, ((1, 1), (0, 0), (0, 0)))

def reference(queries, key_rows, value_rows, cotangent, conv_taps):
    value_heads = split_heads(value_rows)
    key_heads = split_heads(key_rows)

    def forward_row(query_row):
        soft_weights = soft_scores(query_row, key_rows)
        return jnp.einsum('hqk,khd->qhd', soft_weights, value_heads, precision=HIGH).reshape(query_row.shape)
    attn_out = lax.map(forward_row, queries)
    weighted = cotangent * latitude_weights()[:, None, None]
    grad_padded = pad_field(weighted)
    out_padded = pad_field(attn_out)
    out_grad = weighted
    tap_list = []
    for tap_index, (shift_row, shift_col) in enumerate(OFFSETS):
        out_grad = out_grad + conv_taps[tap_index] * grad_padded[1 - shift_row:1 - shift_row + NLAT, 1 - shift_col:1 - shift_col + NLON]
        tap_list.append(lax.optimization_barrier(jnp.sum(out_padded[1 + shift_row:1 + shift_row + NLAT, 1 + shift_col:1 + shift_col + NLON] * weighted, axis=(0, 1))))
    tap_sum = jnp.stack(tap_list)
    tap_update = tap_sum / jnp.sqrt(jnp.mean(tap_sum * tap_sum) + 1e-06)

    def backward_row(running, inputs):
        key_acc, value_acc = running
        query_row, grad_row, out_row = inputs
        soft_weights = soft_scores(query_row, key_rows)
        grad_heads = split_heads(grad_row)
        value_acc = value_acc + jnp.einsum('hqk,qhd->khd', soft_weights, grad_heads, precision=HIGH).reshape(key_rows.shape)
        prob_grad = jnp.einsum('qhd,khd->hqk', grad_heads, value_heads, precision=HIGH)
        row_dot = jnp.transpose(lax.optimization_barrier(jnp.sum(grad_heads * split_heads(out_row), -1)))[:, :, None]
        logit_grad = soft_weights * (prob_grad - row_dot)
        query_part = (jnp.einsum('hqk,khd->qhd', logit_grad, key_heads, precision=HIGH) * HD ** (-0.5)).reshape(query_row.shape)
        key_acc = key_acc + (jnp.einsum('hqk,qhd->khd', logit_grad, split_heads(query_row), precision=HIGH) * HD ** (-0.5)).reshape(key_rows.shape)
        return ((key_acc, value_acc), query_part)
    zeros_acc = jnp.zeros(key_rows.shape, jnp.float32)
    (key_grad, value_grad), query_grad = lax.scan(backward_row, (zeros_acc, zeros_acc), (queries, out_grad, attn_out))
    return (query_grad, key_grad, value_grad, tap_update)
```

```python
import functools

import jax
import jax.numpy as jnp
import numpy as np
from jax import lax
from jax.experimental import pallas as pl
from jax.experimental.pallas import tpu as pltpu
from jax.sharding import PartitionSpec as P

HD = 64
LANES = 128
SUBLANES = 8
VMEM_LIMIT = 16 * 1024 * 1024

HIGH = lax.Precision.HIGHEST
OFFSETS = ((-1, -1), (-1, 0), (-1, 1), (0, -1), (0, 0), (0, 1), (1, -1), (1, 0), (1, 1))


def partner(index, step, peers):
    if peers & (peers - 1) == 0:
        return index ^ step
    return lax.rem(index + step, peers) if not isinstance(index, int) else (index + step) % peers


def source(index, step, peers):
    if peers & (peers - 1) == 0:
        return index ^ step
    return lax.rem(index + (peers - step), peers)


def exchange(value, step, peers):
    return lax.ppermute(value, "lat", [(i, partner(i, step, peers)) for i in range(peers)])


def round_up(value, multiple):
    return -(-value // multiple) * multiple


def row_weights(line_total):
    cosine = np.sin((np.arange(line_total, dtype=np.float64) + 0.5) * (np.pi / line_total))
    return [float(w) for w in cosine / np.mean(cosine)]


def vmem_call(kernel, out_shapes, scratch=()):
    return pl.pallas_call(
        kernel,
        out_shape=[jax.ShapeDtypeStruct(s, jnp.float32) for s in out_shapes],
        scratch_shapes=[pltpu.VMEM(s, jnp.float32) for s in scratch],
        compiler_params=pltpu.CompilerParams(vmem_limit_bytes=VMEM_LIMIT),
    )


def rows_kernel(bands, sectors, width, key_ref, value_ref, first_ref, last_ref, out_ref):
    sector = lax.axis_index("lon")
    rows = first_ref.shape[0]
    keys = key_ref.shape[0]
    for band in range(bands):
        lanes = slice(band * width, (band + 1) * width)
        key = key_ref[:, lanes]
        value = value_ref[:, lanes]
        first = first_ref[:, lanes]
        last = last_ref[:, lanes]
        for other in range(sectors):
            device = band * sectors + other
            is_next = lax.rem(other - sector + sectors, sectors) == 1
            out_ref[device, 0:keys, :] = key
            out_ref[device, keys : 2 * keys, :] = value
            out_ref[device, 2 * keys : 2 * keys + rows, :] = jnp.where(is_next, last, first)


def tokens_kernel(bands, width, query_ref, cotangent_ref, *out_refs):
    band = lax.axis_index("lat")
    for step, out_ref in enumerate(out_refs):
        lanes = pl.ds(pl.multiple_of(partner(band, step, bands) * width, width), width)
        out_ref[0] = query_ref[:, :, lanes]
        out_ref[1] = cotangent_ref[:, :, lanes]


def heads_of(matrix, width):
    lane = lax.broadcasted_iota(jnp.int32, matrix.shape, 1)
    return jnp.concatenate(
        [
            jnp.where((lane >= h * HD) & (lane < (h + 1) * HD), matrix, 0.0)
            for h in range(width // HD)
        ],
        0,
    )


def own_heads(matrix, width, keys):
    lane = lax.broadcasted_iota(jnp.int32, (keys, width), 1)
    result = matrix[0:keys]
    for h in range(1, width // HD):
        result = jnp.where(lane >= h * HD, matrix[h * keys : (h + 1) * keys], result)
    return result


def dot(left, right, left_dim, right_dim):
    return lax.dot_general(
        left,
        right,
        (((left_dim,), (right_dim,)), ((), ())),
        precision=HIGH,
        preferred_element_type=jnp.float32,
    )


def attention_kernel(bands, sectors, width, keys, *refs):
    part_refs = refs[:bands]
    rows_ref, taps_ref, terms_ref = refs[bands : bands + 3]
    query_grad_refs = refs[bands + 3 : 2 * bands + 3]
    query_ref, weighted_ref, grad_ref, out_ref = refs[2 * bands + 3 :]
    band = lax.axis_index("lat")
    sector = lax.axis_index("lon")
    rows, columns = part_refs[0].shape[1:3]
    lines = rows * bands
    tokens = lines * columns
    edge = SUBLANES
    scale = HD ** (-0.5)
    weights = row_weights(lines)
    heads = width // HD
    key_total = bands * sectors * keys

    for step, part_ref in enumerate(part_refs):
        start = source(band, step, bands) * rows
        query_ref[pl.ds(start, rows)] = part_ref[0]
        weighted_ref[pl.ds(start + 1, rows), edge : edge + columns, :] = part_ref[1]
    before = lax.rem(sector + sectors - 1, sectors)
    after = lax.rem(sector + 1, sectors)
    for line in range(lines):
        b, r = divmod(line, rows)
        r = 2 * keys + r
        inner = weighted_ref[1 + line, edge : edge + columns, :]
        weighted_ref[1 + line, edge : edge + columns, :] = inner * weights[line]
        left = rows_ref[b * sectors + before, r : r + 1, :]
        right = rows_ref[b * sectors + after, r : r + 1, :]
        weighted_ref[1 + line, edge - 1 : edge, :] = left * weights[line]
        weighted_ref[1 + line, edge + columns : edge + columns + 1, :] = right * weights[line]
    zeros = jnp.zeros(weighted_ref.shape[1:], jnp.float32)
    weighted_ref[0] = zeros
    weighted_ref[lines + 1] = zeros

    own_lanes = pl.ds(pl.multiple_of(band * width, width), width)
    taps = [taps_ref[t : t + 1, own_lanes] for t in range(len(OFFSETS))]

    def shifted(line, offset):
        a, b = offset
        return weighted_ref[1 + line - a, edge - b : edge - b + columns, :]

    for line in range(lines):
        total = shifted(line, (0, 0))
        for tap, offset in zip(taps, OFFSETS):
            total = total + tap * shifted(line, offset)
        grad_ref[line] = total

    key_all = rows_ref[:, 0:keys, :].reshape(key_total, width)
    value_all = rows_ref[:, keys : 2 * keys, :].reshape(key_total, width)
    key_heads = heads_of(key_all, width)
    value_heads = heads_of(value_all, width)
    query = query_ref[...].reshape(tokens, width)
    grad = grad_ref[...].reshape(tokens, width)

    logits = dot(key_heads, query, 1, 1) * scale
    prob_list = []
    for h in range(heads):
        part = logits[h * key_total : (h + 1) * key_total]
        raised = jnp.exp(part - jnp.max(part, 0, keepdims=True))
        prob_list.append(raised / jnp.sum(raised, 0, keepdims=True))
    probs = jnp.concatenate(prob_list, 0)
    out_ref[...] = dot(probs, value_heads, 0, 0).reshape(lines, columns, width)
    prob_grad = dot(value_heads, grad, 1, 1)
    logit_grad_list = []
    for h in range(heads):
        part = prob_grad[h * key_total : (h + 1) * key_total]
        row_dot = jnp.sum(prob_list[h] * part, 0, keepdims=True)
        logit_grad_list.append(prob_list[h] * (part - row_dot))
    logit_grad = jnp.concatenate(logit_grad_list, 0)

    key_grad = own_heads(dot(logit_grad, query, 1, 0), width, key_total) * scale
    value_grad = own_heads(dot(probs, grad, 1, 0), width, key_total)

    sums = [jnp.zeros((SUBLANES, width), jnp.float32) for _ in OFFSETS]
    for line in range(lines):
        out_line = out_ref[line]
        for t, offset in enumerate(OFFSETS):
            product = out_line * shifted(line, offset)
            for c in range(0, columns, SUBLANES):
                sums[t] = sums[t] + product[c : c + SUBLANES]
    tap_sum = jnp.concatenate([jnp.sum(s, 0, keepdims=True) for s in sums], 0)
    used = 2 * keys + len(OFFSETS)
    filler = jnp.zeros((terms_ref.shape[1] - used, width), jnp.float32)
    for device in range(bands * sectors):
        mine = slice(device * keys, (device + 1) * keys)
        terms_ref[device, 0:keys, :] = key_grad[mine]
        terms_ref[device, keys : 2 * keys, :] = value_grad[mine]
        terms_ref[device, 2 * keys : used, :] = tap_sum
        if terms_ref.shape[1] > used:
            terms_ref[device, used:, :] = filler

    query_grad = (dot(logit_grad, key_heads, 0, 0) * scale).reshape(lines, columns, width)
    out_ref[...] = query_grad
    for step, query_grad_ref in enumerate(query_grad_refs):
        query_grad_ref[...] = out_ref[pl.ds(partner(band, step, bands) * rows, rows)]


def join_kernel(bands, width, *refs):
    band = lax.axis_index("lat")
    out_ref = refs[-1]
    for step, part_ref in enumerate(refs[:-1]):
        lanes = pl.ds(pl.multiple_of(source(band, step, bands) * width, width), width)
        out_ref[:, :, lanes] = part_ref[...]


def sums_kernel(bands, sectors, width, keys, terms_ref, key_ref, value_ref, taps_ref):
    used = 2 * keys + len(OFFSETS)
    total = jnp.zeros((), jnp.float32)
    parts = []
    for band in range(bands):
        lanes = slice(band * width, (band + 1) * width)
        part = terms_ref[band * sectors]
        for sector in range(1, sectors):
            part = part + terms_ref[band * sectors + sector]
        key_ref[:, lanes] = part[0:keys]
        value_ref[:, lanes] = part[keys : 2 * keys]
        parts.append(part[2 * keys : used])
    tap_sum = jnp.concatenate(parts, 1)
    mean = jnp.sum(tap_sum * tap_sum, keepdims=True) / (len(OFFSETS) * width * bands)
    taps_ref[...] = tap_sum / jnp.sqrt(mean + 1e-06)


def split_heads_body(queries, key_rows, value_rows, cotangent, conv_taps):
    rows, columns, channels = queries.shape
    bands = lax.axis_size("lat")
    sectors = lax.axis_size("lon")
    devices = bands * sectors
    keys = key_rows.shape[0]
    width = channels // bands
    lines = rows * bands

    sent_rows = round_up(2 * keys + rows, SUBLANES)
    (row_blocks,) = vmem_call(
        functools.partial(rows_kernel, bands, sectors, width), [(devices, sent_rows, width)]
    )(key_rows, value_rows, cotangent[:, 0, :], cotangent[:, columns - 1, :])
    row_blocks = lax.all_to_all(row_blocks, ("lat", "lon"), 0, 0, tiled=True)

    parts = vmem_call(
        functools.partial(tokens_kernel, bands, width), [(2, rows, columns, width)] * bands
    )(queries, cotangent)
    parts = [parts[0]] + [exchange(parts[s], s, bands) for s in range(1, bands)]

    sent_terms = round_up(2 * keys + len(OFFSETS), SUBLANES)
    grid = (lines, columns, width)
    terms, *grad_parts = vmem_call(
        functools.partial(attention_kernel, bands, sectors, width, keys),
        [(devices, sent_terms, width)] + [(rows, columns, width)] * bands,
        [grid, (lines + 2, columns + 2 * SUBLANES, width), grid, grid],
    )(*parts, row_blocks, conv_taps)

    terms = lax.all_to_all(terms, ("lat", "lon"), 0, 0, tiled=True)
    grad_parts = [grad_parts[0]] + [exchange(grad_parts[s], s, bands) for s in range(1, bands)]
    (query_grad,) = vmem_call(
        functools.partial(join_kernel, bands, width), [(rows, columns, channels)]
    )(*grad_parts)
    key_grad, value_grad, tap_update = vmem_call(
        functools.partial(sums_kernel, bands, sectors, width, keys),
        [(keys, channels), (keys, channels), (len(OFFSETS), channels)],
    )(terms)
    return (query_grad, key_grad, value_grad, tap_update)


def extended(value, sides, width):
    for axis, dim in sides:
        peers, length = (lax.axis_size(axis), value.shape[dim])
        up = [(i, (i + 1) % peers) for i in range(peers)]
        down = [(j, i) for i, j in up]
        last = lax.slice_in_dim(value, length - width, length, axis=dim)
        initial = lax.slice_in_dim(value, 0, width, axis=dim)
        before = lax.ppermute(last, axis, up)
        after = lax.ppermute(initial, axis, down)
        value = jnp.concatenate([before, value, after], axis=dim)
    return value


def split_heads(matrix):
    return matrix.reshape(matrix.shape[0], -1, HD)


def latitude_weights(row_count, band_index, band_count):
    line_total = row_count * band_count
    centres = (jnp.arange(line_total, dtype=jnp.float32) + 0.5) * (jnp.pi / line_total)
    mean_cosine = jnp.sum(jnp.sin(centres)) / line_total
    mine = (band_index * row_count + jnp.arange(row_count, dtype=jnp.int32)).astype(jnp.float32)
    return jnp.sin((mine + 0.5) * (jnp.pi / line_total)) / mean_cosine


def close_poles(padded, row_dim, band_index, band_count):
    height = padded.shape[row_dim]
    positions = jnp.arange(height)
    outside = (positions == 0) & (band_index == 0) | (positions == height - 1) & (
        band_index == band_count - 1
    )
    shape_mask = [1] * padded.ndim
    shape_mask[row_dim] = height
    return jnp.where(outside.reshape(shape_mask), 0.0, padded)


def spread_taps(weighted, grad_padded, conv_taps):
    row_count, col_count = (weighted.shape[0], weighted.shape[1])
    result = weighted
    for tap_index, (shift_row, shift_col) in enumerate(OFFSETS):
        result = (
            result
            + conv_taps[tap_index]
            * grad_padded[
                1 - shift_row : 1 - shift_row + row_count, 1 - shift_col : 1 - shift_col + col_count
            ]
        )
    return result


def tap_terms(weighted, out_padded):
    row_count, col_count = (weighted.shape[0], weighted.shape[1])
    term_list = []
    for shift_row, shift_col in OFFSETS:
        term_list.append(
            jnp.sum(
                out_padded[
                    1 + shift_row : 1 + shift_row + row_count,
                    1 + shift_col : 1 + shift_col + col_count,
                ]
                * weighted,
                axis=(0, 1),
            )
        )
    return jnp.stack(term_list)


def group_logits(query_part, key_part):
    return jnp.einsum(
        "qhd,khd->hqk", split_heads(query_part), split_heads(key_part), precision=HIGH
    ) * HD ** (-0.5)


def whole_rows_body(queries, key_rows, value_rows, cotangent, conv_taps):
    row_count, col_count, channels = queries.shape
    band_count = lax.axis_size("lat")
    band_index = lax.axis_index("lat")
    weighted = cotangent * latitude_weights(row_count, band_index, band_count)[:, None, None]
    paired_rows = jnp.concatenate([key_rows, value_rows], 1)
    paired_all = lax.all_gather(paired_rows, ("lat", "lon"), axis=0, tiled=True)
    key_all = paired_all[:, :channels]
    value_all = paired_all[:, channels:]
    token_count = row_count * col_count
    key_count = key_all.shape[0]
    query_flat = queries.reshape(token_count, channels)
    group_width = 2 * HD
    group_count = channels // group_width
    outputs = []
    peaks = []
    sums_soft = []
    for group_index in range(group_count):
        col_start = group_index * group_width
        col_stop = col_start + group_width
        logits = group_logits(query_flat[:, col_start:col_stop], key_all[:, col_start:col_stop])
        row_peak = jnp.max(logits, -1, keepdims=True)
        raised = jnp.exp(logits - row_peak)
        normaliser = jnp.sum(raised, -1, keepdims=True)
        soft_weights = raised / normaliser
        outputs.append(
            jnp.einsum(
                "hqk,khd->qhd",
                soft_weights,
                split_heads(value_all[:, col_start:col_stop]),
                precision=HIGH,
            ).reshape(token_count, group_width)
        )
        peaks.append(row_peak)
        sums_soft.append(normaliser)
    out_flat = jnp.concatenate(outputs, 1)
    out_grid = out_flat.reshape(row_count, col_count, channels)
    both_padded = close_poles(
        extended(jnp.stack([weighted, out_grid]), (("lat", 1), ("lon", 2)), 1),
        1,
        band_index,
        band_count,
    )
    grad_padded = both_padded[0]
    out_padded = both_padded[1]
    out_grad = spread_taps(weighted, grad_padded, conv_taps)
    tap_sum = lax.psum(tap_terms(weighted, out_padded), ("lat", "lon"))
    tap_update = tap_sum / jnp.sqrt(jnp.mean(tap_sum * tap_sum) + 1e-06)
    grad_flat = out_grad.reshape(token_count, channels)
    query_parts = []
    key_parts = []
    value_parts = []
    for group_index in range(group_count):
        col_start = group_index * group_width
        col_stop = col_start + group_width
        query_heads = split_heads(query_flat[:, col_start:col_stop])
        key_heads = split_heads(key_all[:, col_start:col_stop])
        logits = jnp.einsum("qhd,khd->hqk", query_heads, key_heads, precision=HIGH) * HD ** (-0.5)
        soft_weights = jnp.exp(logits - peaks[group_index]) / sums_soft[group_index]
        grad_heads = split_heads(grad_flat[:, col_start:col_stop])
        value_parts.append(
            jnp.einsum("hqk,qhd->khd", soft_weights, grad_heads, precision=HIGH).reshape(
                key_count, group_width
            )
        )
        prob_grad = jnp.einsum(
            "qhd,khd->hqk",
            grad_heads,
            split_heads(value_all[:, col_start:col_stop]),
            precision=HIGH,
        )
        row_dot = jnp.transpose(
            jnp.sum(grad_heads * split_heads(out_flat[:, col_start:col_stop]), -1)
        )[:, :, None]
        logit_grad = soft_weights * (prob_grad - row_dot)
        query_parts.append(
            (
                jnp.einsum("hqk,khd->qhd", logit_grad, key_heads, precision=HIGH) * HD ** (-0.5)
            ).reshape(token_count, group_width)
        )
        key_parts.append(
            (
                jnp.einsum("hqk,qhd->khd", logit_grad, query_heads, precision=HIGH) * HD ** (-0.5)
            ).reshape(key_count, group_width)
        )
    paired_terms = jnp.concatenate(key_parts + value_parts, 1)
    paired_band = lax.psum_scatter(paired_terms, "lat", scatter_dimension=0, tiled=True)
    paired_grad = lax.psum_scatter(paired_band, "lon", scatter_dimension=0, tiled=True)
    key_grad = paired_grad[:, :channels]
    value_grad = paired_grad[:, channels:]
    query_grad = jnp.concatenate(query_parts, 1).reshape(row_count, col_count, channels)
    return (query_grad, key_grad, value_grad, tap_update)


def body(queries, key_rows, value_rows, cotangent, conv_taps):
    bands = lax.axis_size("lat")
    sectors = lax.axis_size("lon")
    columns, channels = queries.shape[1:]
    if channels % (bands * LANES) == 0 and sectors > 2 and columns % SUBLANES == 0:
        return split_heads_body(queries, key_rows, value_rows, cotangent, conv_taps)
    return whole_rows_body(queries, key_rows, value_rows, cotangent, conv_taps)


def solution(mesh):
    placed = (
        P("lat", "lon", None),
        P(("lat", "lon"), None),
        P(("lat", "lon"), None),
        P("lat", "lon", None),
        P(),
    )
    return jax.shard_map(
        body,
        mesh=mesh,
        in_specs=placed,
        out_specs=(P("lat", "lon", None), P(("lat", "lon"), None), P(("lat", "lon"), None), P()),
        check_vma=False,
    )
```

```python
import functools

import jax
import jax.numpy as jnp
import numpy as np
from jax import lax
from jax.experimental import pallas as pl
from jax.experimental.pallas import tpu as pltpu
from jax.sharding import PartitionSpec as P

HD = 64
LANES = 128
SUBLANES = 8
VMEM_LIMIT = 16 * 1024 * 1024

HIGH = lax.Precision.HIGHEST
OFFSETS = ((-1, -1), (-1, 0), (-1, 1), (0, -1), (0, 0), (0, 1), (1, -1), (1, 0), (1, 1))


def partner(index, step, peers):
    if peers & (peers - 1) == 0:
        return index ^ step
    return lax.rem(index + step, peers) if not isinstance(index, int) else (index + step) % peers


def source(index, step, peers):
    if peers & (peers - 1) == 0:
        return index ^ step
    return lax.rem(index + (peers - step), peers)


def exchange(value, step, peers):
    return lax.ppermute(value, "lat", [(i, partner(i, step, peers)) for i in range(peers)])


def round_up(value, multiple):
    return -(-value // multiple) * multiple


def row_weights(line_total):
    cosine = np.sin((np.arange(line_total, dtype=np.float64) + 0.5) * (np.pi / line_total))
    return [float(w) for w in cosine / np.mean(cosine)]


def vmem_call(kernel, out_shapes, scratch=()):
    return pl.pallas_call(
        kernel,
        out_shape=[jax.ShapeDtypeStruct(s, jnp.float32) for s in out_shapes],
        scratch_shapes=[pltpu.VMEM(s, jnp.float32) for s in scratch],
        compiler_params=pltpu.CompilerParams(vmem_limit_bytes=VMEM_LIMIT),
    )


def in_hbm(array):
    return pltpu.with_memory_space_constraint(array, pltpu.HBM)


def pack_kernel(bands, sectors, width, keys, *refs):
    key_ref, value_ref, query_ref, cotangent_ref, block_ref = refs[:5]
    part_refs = refs[5 : 5 + bands]
    key_own, value_own, first_own, last_own, sems = refs[5 + bands :]
    band = lax.axis_index("lat")
    sector = lax.axis_index("lon")
    rows, columns = query_ref.shape[:2]

    small = [
        pltpu.make_async_copy(source_ref, target_ref, sems.at[i])
        for i, (source_ref, target_ref) in enumerate(
            (
                (key_ref, key_own),
                (value_ref, value_own),
                (cotangent_ref.at[:, 0:SUBLANES, :], first_own),
                (cotangent_ref.at[:, columns - SUBLANES : columns, :], last_own),
            )
        )
    ]
    for copy in small:
        copy.start()
    large = []
    for step, part_ref in enumerate(part_refs):
        lanes = pl.ds(pl.multiple_of(partner(band, step, bands) * width, width), width)
        for i, array_ref in enumerate((query_ref, cotangent_ref)):
            large.append(
                pltpu.make_async_copy(
                    array_ref.at[:, :, lanes], part_ref.at[i], sems.at[len(small) + len(large)]
                )
            )
    for copy in large:
        copy.start()
    for copy in small:
        copy.wait()
    for to_band in range(bands):
        lanes = slice(to_band * width, (to_band + 1) * width)
        key = key_own[:, lanes]
        value = value_own[:, lanes]
        first = first_own[:, 0, lanes]
        last = last_own[:, SUBLANES - 1, lanes]
        for to_sector in range(sectors):
            device = to_band * sectors + to_sector
            is_next = lax.rem(to_sector - sector + sectors, sectors) == 1
            block_ref[device, 0:keys, :] = key
            block_ref[device, keys : 2 * keys, :] = value
            block_ref[device, 2 * keys : 2 * keys + rows, :] = jnp.where(is_next, last, first)
    for copy in large:
        copy.wait()


def heads_of(matrix, width):
    lane = lax.broadcasted_iota(jnp.int32, matrix.shape, 1)
    return jnp.concatenate(
        [
            jnp.where((lane >= h * HD) & (lane < (h + 1) * HD), matrix, 0.0)
            for h in range(width // HD)
        ],
        0,
    )


def own_heads(matrix, width, keys):
    lane = lax.broadcasted_iota(jnp.int32, (keys, width), 1)
    result = matrix[0:keys]
    for h in range(1, width // HD):
        result = jnp.where(lane >= h * HD, matrix[h * keys : (h + 1) * keys], result)
    return result


def dot(left, right, left_dim, right_dim):
    return lax.dot_general(
        left,
        right,
        (((left_dim,), (right_dim,)), ((), ())),
        precision=HIGH,
        preferred_element_type=jnp.float32,
    )


def attention_kernel(bands, sectors, width, keys, *refs):
    part_refs = refs[:bands]
    rows_ref, taps_ref, terms_ref = refs[bands : bands + 3]
    query_grad_refs = refs[bands + 3 : 2 * bands + 3]
    query_ref, weighted_ref, grad_ref, out_ref = refs[2 * bands + 3 :]
    band = lax.axis_index("lat")
    sector = lax.axis_index("lon")
    rows, columns = part_refs[0].shape[1:3]
    lines = rows * bands
    tokens = lines * columns
    edge = SUBLANES
    scale = HD ** (-0.5)
    weights = row_weights(lines)
    heads = width // HD
    key_total = bands * sectors * keys

    for step, part_ref in enumerate(part_refs):
        start = source(band, step, bands) * rows
        query_ref[pl.ds(start, rows)] = part_ref[0]
        weighted_ref[pl.ds(start + 1, rows), edge : edge + columns, :] = part_ref[1]
    before = lax.rem(sector + sectors - 1, sectors)
    after = lax.rem(sector + 1, sectors)
    for line in range(lines):
        b, r = divmod(line, rows)
        r = 2 * keys + r
        inner = weighted_ref[1 + line, edge : edge + columns, :]
        weighted_ref[1 + line, edge : edge + columns, :] = inner * weights[line]
        left = rows_ref[b * sectors + before, r : r + 1, :]
        right = rows_ref[b * sectors + after, r : r + 1, :]
        weighted_ref[1 + line, edge - 1 : edge, :] = left * weights[line]
        weighted_ref[1 + line, edge + columns : edge + columns + 1, :] = right * weights[line]
    zeros = jnp.zeros(weighted_ref.shape[1:], jnp.float32)
    weighted_ref[0] = zeros
    weighted_ref[lines + 1] = zeros

    own_lanes = pl.ds(pl.multiple_of(band * width, width), width)
    taps = [taps_ref[t : t + 1, own_lanes] for t in range(len(OFFSETS))]

    def shifted(line, offset):
        a, b = offset
        return weighted_ref[1 + line - a, edge - b : edge - b + columns, :]

    for line in range(lines):
        total = shifted(line, (0, 0))
        for tap, offset in zip(taps, OFFSETS):
            total = total + tap * shifted(line, offset)
        grad_ref[line] = total

    key_all = rows_ref[:, 0:keys, :].reshape(key_total, width)
    value_all = rows_ref[:, keys : 2 * keys, :].reshape(key_total, width)
    key_heads = heads_of(key_all, width)
    value_heads = heads_of(value_all, width)
    query = query_ref[...].reshape(tokens, width)
    grad = grad_ref[...].reshape(tokens, width)

    logits = dot(key_heads, query, 1, 1) * scale
    prob_list = []
    for h in range(heads):
        part = logits[h * key_total : (h + 1) * key_total]
        raised = jnp.exp(part - jnp.max(part, 0, keepdims=True))
        prob_list.append(raised / jnp.sum(raised, 0, keepdims=True))
    probs = jnp.concatenate(prob_list, 0)
    out_ref[...] = dot(probs, value_heads, 0, 0).reshape(lines, columns, width)
    prob_grad = dot(value_heads, grad, 1, 1)
    logit_grad_list = []
    for h in range(heads):
        part = prob_grad[h * key_total : (h + 1) * key_total]
        row_dot = jnp.sum(prob_list[h] * part, 0, keepdims=True)
        logit_grad_list.append(prob_list[h] * (part - row_dot))
    logit_grad = jnp.concatenate(logit_grad_list, 0)

    key_grad = own_heads(dot(logit_grad, query, 1, 0), width, key_total) * scale
    value_grad = own_heads(dot(probs, grad, 1, 0), width, key_total)

    sums = [jnp.zeros((SUBLANES, width), jnp.float32) for _ in OFFSETS]
    for line in range(lines):
        out_line = out_ref[line]
        for t, offset in enumerate(OFFSETS):
            product = out_line * shifted(line, offset)
            for c in range(0, columns, SUBLANES):
                sums[t] = sums[t] + product[c : c + SUBLANES]
    tap_sum = jnp.concatenate([jnp.sum(s, 0, keepdims=True) for s in sums], 0)
    used = 2 * keys + len(OFFSETS)
    filler = jnp.zeros((terms_ref.shape[1] - used, width), jnp.float32)
    for device in range(bands * sectors):
        mine = slice(device * keys, (device + 1) * keys)
        terms_ref[device, 0:keys, :] = key_grad[mine]
        terms_ref[device, keys : 2 * keys, :] = value_grad[mine]
        terms_ref[device, 2 * keys : used, :] = tap_sum
        if terms_ref.shape[1] > used:
            terms_ref[device, used:, :] = filler

    query_grad = (dot(logit_grad, key_heads, 0, 0) * scale).reshape(lines, columns, width)
    out_ref[...] = query_grad
    for step, query_grad_ref in enumerate(query_grad_refs):
        query_grad_ref[...] = out_ref[pl.ds(partner(band, step, bands) * rows, rows)]


def join_kernel(bands, width, *refs):
    band = lax.axis_index("lat")
    out_ref = refs[-1]
    for step, part_ref in enumerate(refs[:-1]):
        lanes = pl.ds(pl.multiple_of(source(band, step, bands) * width, width), width)
        out_ref[:, :, lanes] = part_ref[...]


def sums_kernel(bands, sectors, width, keys, terms_ref, key_ref, value_ref, taps_ref):
    used = 2 * keys + len(OFFSETS)
    total = jnp.zeros((), jnp.float32)
    parts = []
    for band in range(bands):
        lanes = slice(band * width, (band + 1) * width)
        part = terms_ref[band * sectors]
        for sector in range(1, sectors):
            part = part + terms_ref[band * sectors + sector]
        key_ref[:, lanes] = part[0:keys]
        value_ref[:, lanes] = part[keys : 2 * keys]
        parts.append(part[2 * keys : used])
    tap_sum = jnp.concatenate(parts, 1)
    mean = jnp.sum(tap_sum * tap_sum, keepdims=True) / (len(OFFSETS) * width * bands)
    taps_ref[...] = tap_sum / jnp.sqrt(mean + 1e-06)


def split_heads_body(queries, key_rows, value_rows, cotangent, conv_taps):
    rows, columns, channels = queries.shape
    bands = lax.axis_size("lat")
    sectors = lax.axis_size("lon")
    devices = bands * sectors
    keys = key_rows.shape[0]
    width = channels // bands
    lines = rows * bands

    sent_rows = round_up(2 * keys + rows, SUBLANES)
    part_shape = (2, rows, columns, width)
    anywhere = pl.BlockSpec(memory_space=pl.ANY)
    row_blocks, *parts = pl.pallas_call(
        functools.partial(pack_kernel, bands, sectors, width, keys),
        out_shape=[
            jax.ShapeDtypeStruct(s, jnp.float32)
            for s in [(devices, sent_rows, width)] + [part_shape] * bands
        ],
        in_specs=[anywhere] * 4,
        scratch_shapes=[
            pltpu.VMEM((keys, channels), jnp.float32),
            pltpu.VMEM((keys, channels), jnp.float32),
            pltpu.VMEM((rows, SUBLANES, channels), jnp.float32),
            pltpu.VMEM((rows, SUBLANES, channels), jnp.float32),
            pltpu.SemaphoreType.DMA((4 + 2 * bands,)),
        ],
        compiler_params=pltpu.CompilerParams(vmem_limit_bytes=VMEM_LIMIT),
    )(*[in_hbm(x) for x in (key_rows, value_rows, queries, cotangent)])
    row_blocks = lax.all_to_all(row_blocks, ("lat", "lon"), 0, 0, tiled=True)
    parts = [parts[0]] + [exchange(parts[s], s, bands) for s in range(1, bands)]

    sent_terms = round_up(2 * keys + len(OFFSETS), SUBLANES)
    grid = (lines, columns, width)
    terms, *grad_parts = vmem_call(
        functools.partial(attention_kernel, bands, sectors, width, keys),
        [(devices, sent_terms, width)] + [(rows, columns, width)] * bands,
        [grid, (lines + 2, columns + 2 * SUBLANES, width), grid, grid],
    )(*parts, row_blocks, conv_taps)

    terms = lax.all_to_all(terms, ("lat", "lon"), 0, 0, tiled=True)
    grad_parts = [grad_parts[0]] + [exchange(grad_parts[s], s, bands) for s in range(1, bands)]
    (query_grad,) = vmem_call(
        functools.partial(join_kernel, bands, width), [(rows, columns, channels)]
    )(*grad_parts)
    key_grad, value_grad, tap_update = vmem_call(
        functools.partial(sums_kernel, bands, sectors, width, keys),
        [(keys, channels), (keys, channels), (len(OFFSETS), channels)],
    )(terms)
    return (query_grad, key_grad, value_grad, tap_update)


def extended(value, sides, width):
    for axis, dim in sides:
        peers, length = (lax.axis_size(axis), value.shape[dim])
        up = [(i, (i + 1) % peers) for i in range(peers)]
        down = [(j, i) for i, j in up]
        last = lax.slice_in_dim(value, length - width, length, axis=dim)
        initial = lax.slice_in_dim(value, 0, width, axis=dim)
        before = lax.ppermute(last, axis, up)
        after = lax.ppermute(initial, axis, down)
        value = jnp.concatenate([before, value, after], axis=dim)
    return value


def split_heads(matrix):
    return matrix.reshape(matrix.shape[0], -1, HD)


def latitude_weights(row_count, band_index, band_count):
    line_total = row_count * band_count
    centres = (jnp.arange(line_total, dtype=jnp.float32) + 0.5) * (jnp.pi / line_total)
    mean_cosine = jnp.sum(jnp.sin(centres)) / line_total
    mine = (band_index * row_count + jnp.arange(row_count, dtype=jnp.int32)).astype(jnp.float32)
    return jnp.sin((mine + 0.5) * (jnp.pi / line_total)) / mean_cosine


def close_poles(padded, row_dim, band_index, band_count):
    height = padded.shape[row_dim]
    positions = jnp.arange(height)
    outside = (positions == 0) & (band_index == 0) | (positions == height - 1) & (
        band_index == band_count - 1
    )
    shape_mask = [1] * padded.ndim
    shape_mask[row_dim] = height
    return jnp.where(outside.reshape(shape_mask), 0.0, padded)


def spread_taps(weighted, grad_padded, conv_taps):
    row_count, col_count = (weighted.shape[0], weighted.shape[1])
    result = weighted
    for tap_index, (shift_row, shift_col) in enumerate(OFFSETS):
        result = (
            result
            + conv_taps[tap_index]
            * grad_padded[
                1 - shift_row : 1 - shift_row + row_count, 1 - shift_col : 1 - shift_col + col_count
            ]
        )
    return result


def tap_terms(weighted, out_padded):
    row_count, col_count = (weighted.shape[0], weighted.shape[1])
    term_list = []
    for shift_row, shift_col in OFFSETS:
        term_list.append(
            jnp.sum(
                out_padded[
                    1 + shift_row : 1 + shift_row + row_count,
                    1 + shift_col : 1 + shift_col + col_count,
                ]
                * weighted,
                axis=(0, 1),
            )
        )
    return jnp.stack(term_list)


def group_logits(query_part, key_part):
    return jnp.einsum(
        "qhd,khd->hqk", split_heads(query_part), split_heads(key_part), precision=HIGH
    ) * HD ** (-0.5)


def whole_rows_body(queries, key_rows, value_rows, cotangent, conv_taps):
    row_count, col_count, channels = queries.shape
    band_count = lax.axis_size("lat")
    band_index = lax.axis_index("lat")
    weighted = cotangent * latitude_weights(row_count, band_index, band_count)[:, None, None]
    paired_rows = jnp.concatenate([key_rows, value_rows], 1)
    paired_all = lax.all_gather(paired_rows, ("lat", "lon"), axis=0, tiled=True)
    key_all = paired_all[:, :channels]
    value_all = paired_all[:, channels:]
    token_count = row_count * col_count
    key_count = key_all.shape[0]
    query_flat = queries.reshape(token_count, channels)
    group_width = 2 * HD
    group_count = channels // group_width
    outputs = []
    peaks = []
    sums_soft = []
    for group_index in range(group_count):
        col_start = group_index * group_width
        col_stop = col_start + group_width
        logits = group_logits(query_flat[:, col_start:col_stop], key_all[:, col_start:col_stop])
        row_peak = jnp.max(logits, -1, keepdims=True)
        raised = jnp.exp(logits - row_peak)
        normaliser = jnp.sum(raised, -1, keepdims=True)
        soft_weights = raised / normaliser
        outputs.append(
            jnp.einsum(
                "hqk,khd->qhd",
                soft_weights,
                split_heads(value_all[:, col_start:col_stop]),
                precision=HIGH,
            ).reshape(token_count, group_width)
        )
        peaks.append(row_peak)
        sums_soft.append(normaliser)
    out_flat = jnp.concatenate(outputs, 1)
    out_grid = out_flat.reshape(row_count, col_count, channels)
    both_padded = close_poles(
        extended(jnp.stack([weighted, out_grid]), (("lat", 1), ("lon", 2)), 1),
        1,
        band_index,
        band_count,
    )
    grad_padded = both_padded[0]
    out_padded = both_padded[1]
    out_grad = spread_taps(weighted, grad_padded, conv_taps)
    tap_sum = lax.psum(tap_terms(weighted, out_padded), ("lat", "lon"))
    tap_update = tap_sum / jnp.sqrt(jnp.mean(tap_sum * tap_sum) + 1e-06)
    grad_flat = out_grad.reshape(token_count, channels)
    query_parts = []
    key_parts = []
    value_parts = []
    for group_index in range(group_count):
        col_start = group_index * group_width
        col_stop = col_start + group_width
        query_heads = split_heads(query_flat[:, col_start:col_stop])
        key_heads = split_heads(key_all[:, col_start:col_stop])
        logits = jnp.einsum("qhd,khd->hqk", query_heads, key_heads, precision=HIGH) * HD ** (-0.5)
        soft_weights = jnp.exp(logits - peaks[group_index]) / sums_soft[group_index]
        grad_heads = split_heads(grad_flat[:, col_start:col_stop])
        value_parts.append(
            jnp.einsum("hqk,qhd->khd", soft_weights, grad_heads, precision=HIGH).reshape(
                key_count, group_width
            )
        )
        prob_grad = jnp.einsum(
            "qhd,khd->hqk",
            grad_heads,
            split_heads(value_all[:, col_start:col_stop]),
            precision=HIGH,
        )
        row_dot = jnp.transpose(
            jnp.sum(grad_heads * split_heads(out_flat[:, col_start:col_stop]), -1)
        )[:, :, None]
        logit_grad = soft_weights * (prob_grad - row_dot)
        query_parts.append(
            (
                jnp.einsum("hqk,khd->qhd", logit_grad, key_heads, precision=HIGH) * HD ** (-0.5)
            ).reshape(token_count, group_width)
        )
        key_parts.append(
            (
                jnp.einsum("hqk,qhd->khd", logit_grad, query_heads, precision=HIGH) * HD ** (-0.5)
            ).reshape(key_count, group_width)
        )
    paired_terms = jnp.concatenate(key_parts + value_parts, 1)
    paired_band = lax.psum_scatter(paired_terms, "lat", scatter_dimension=0, tiled=True)
    paired_grad = lax.psum_scatter(paired_band, "lon", scatter_dimension=0, tiled=True)
    key_grad = paired_grad[:, :channels]
    value_grad = paired_grad[:, channels:]
    query_grad = jnp.concatenate(query_parts, 1).reshape(row_count, col_count, channels)
    return (query_grad, key_grad, value_grad, tap_update)


def body(queries, key_rows, value_rows, cotangent, conv_taps):
    bands = lax.axis_size("lat")
    sectors = lax.axis_size("lon")
    columns, channels = queries.shape[1:]
    if channels % (bands * LANES) == 0 and sectors > 2 and columns % SUBLANES == 0:
        return split_heads_body(queries, key_rows, value_rows, cotangent, conv_taps)
    return whole_rows_body(queries, key_rows, value_rows, cotangent, conv_taps)


def solution(mesh):
    placed = (
        P("lat", "lon", None),
        P(("lat", "lon"), None),
        P(("lat", "lon"), None),
        P("lat", "lon", None),
        P(),
    )
    return jax.shard_map(
        body,
        mesh=mesh,
        in_specs=placed,
        out_specs=(P("lat", "lon", None), P(("lat", "lon"), None), P(("lat", "lon"), None), P()),
        check_vma=False,
    )
```

```python
import functools

import jax
import jax.numpy as jnp
import numpy as np
from jax import lax
from jax.experimental import pallas as pl
from jax.experimental.pallas import tpu as pltpu
from jax.sharding import PartitionSpec as P

HD = 64
LANES = 128
SUBLANES = 8
VMEM_LIMIT = 16 * 1024 * 1024

HIGH = lax.Precision.HIGHEST
OFFSETS = ((-1, -1), (-1, 0), (-1, 1), (0, -1), (0, 0), (0, 1), (1, -1), (1, 0), (1, 1))


def partner(index, step, peers):
    if peers & (peers - 1) == 0:
        return index ^ step
    return lax.rem(index + step, peers) if not isinstance(index, int) else (index + step) % peers


def source(index, step, peers):
    if peers & (peers - 1) == 0:
        return index ^ step
    return lax.rem(index + (peers - step), peers)


def exchange(value, step, peers):
    return lax.ppermute(value, "lat", [(i, partner(i, step, peers)) for i in range(peers)])


def round_up(value, multiple):
    return -(-value // multiple) * multiple


def row_weights(line_total):
    cosine = np.sin((np.arange(line_total, dtype=np.float64) + 0.5) * (np.pi / line_total))
    return [float(w) for w in cosine / np.mean(cosine)]


def vmem_call(kernel, out_shapes, scratch=()):
    return pl.pallas_call(
        kernel,
        out_shape=[jax.ShapeDtypeStruct(s, jnp.float32) for s in out_shapes],
        scratch_shapes=[pltpu.VMEM(s, jnp.float32) for s in scratch],
        compiler_params=pltpu.CompilerParams(vmem_limit_bytes=VMEM_LIMIT),
    )


def in_hbm(array):
    return pltpu.with_memory_space_constraint(array, pltpu.HBM)


def pack_kernel(bands, sectors, width, keys, *refs):
    key_ref, value_ref, query_ref, cotangent_ref, block_ref = refs[:5]
    part_refs = refs[5 : 5 + bands]
    key_own, value_own, first_own, last_own, sems = refs[5 + bands :]
    band = lax.axis_index("lat")
    sector = lax.axis_index("lon")
    rows, columns = query_ref.shape[:2]

    small = [
        pltpu.make_async_copy(source_ref, target_ref, sems.at[i])
        for i, (source_ref, target_ref) in enumerate(
            (
                (key_ref, key_own),
                (value_ref, value_own),
                (cotangent_ref.at[:, 0:SUBLANES, :], first_own),
                (cotangent_ref.at[:, columns - SUBLANES : columns, :], last_own),
            )
        )
    ]
    for copy in small:
        copy.start()
    large = []
    for step, part_ref in enumerate(part_refs):
        lanes = pl.ds(pl.multiple_of(partner(band, step, bands) * width, width), width)
        for i, array_ref in enumerate((query_ref, cotangent_ref)):
            large.append(
                pltpu.make_async_copy(
                    array_ref.at[:, :, lanes], part_ref.at[i], sems.at[len(small) + len(large)]
                )
            )
    for copy in large:
        copy.start()
    for copy in small:
        copy.wait()
    for to_band in range(bands):
        lanes = slice(to_band * width, (to_band + 1) * width)
        key = key_own[:, lanes]
        value = value_own[:, lanes]
        first = first_own[:, 0, lanes]
        last = last_own[:, SUBLANES - 1, lanes]
        for to_sector in range(sectors):
            device = to_band * sectors + to_sector
            is_next = lax.rem(to_sector - sector + sectors, sectors) == 1
            block_ref[device, 0:keys, :] = key
            block_ref[device, keys : 2 * keys, :] = value
            block_ref[device, 2 * keys : 2 * keys + rows, :] = jnp.where(is_next, last, first)
    for copy in large:
        copy.wait()


def heads_of(matrix, width):
    lane = lax.broadcasted_iota(jnp.int32, matrix.shape, 1)
    return jnp.concatenate(
        [
            jnp.where((lane >= h * HD) & (lane < (h + 1) * HD), matrix, 0.0)
            for h in range(width // HD)
        ],
        0,
    )


def own_heads(matrix, width, keys):
    lane = lax.broadcasted_iota(jnp.int32, (keys, width), 1)
    result = matrix[0:keys]
    for h in range(1, width // HD):
        result = jnp.where(lane >= h * HD, matrix[h * keys : (h + 1) * keys], result)
    return result


def dot(left, right, left_dim, right_dim):
    return lax.dot_general(
        left,
        right,
        (((left_dim,), (right_dim,)), ((), ())),
        precision=HIGH,
        preferred_element_type=jnp.float32,
    )


def attention_kernel(bands, sectors, width, keys, *refs):
    part_refs = refs[:bands]
    rows_ref, taps_ref, terms_ref = refs[bands : bands + 3]
    query_grad_refs = refs[bands + 3 : 2 * bands + 3]
    query_ref, weighted_ref, grad_ref, out_ref = refs[2 * bands + 3 :]
    band = lax.axis_index("lat")
    sector = lax.axis_index("lon")
    rows, columns = part_refs[0].shape[1:3]
    lines = rows * bands
    tokens = lines * columns
    edge = SUBLANES
    scale = HD ** (-0.5)
    weights = row_weights(lines)
    heads = width // HD
    key_total = bands * sectors * keys

    for step, part_ref in enumerate(part_refs):
        start = source(band, step, bands) * rows
        query_ref[pl.ds(start, rows)] = part_ref[0]
        weighted_ref[pl.ds(start + 1, rows), edge : edge + columns, :] = part_ref[1]
    before = lax.rem(sector + sectors - 1, sectors)
    after = lax.rem(sector + 1, sectors)
    for line in range(lines):
        b, r = divmod(line, rows)
        r = 2 * keys + r
        inner = weighted_ref[1 + line, edge : edge + columns, :]
        weighted_ref[1 + line, edge : edge + columns, :] = inner * weights[line]
        left = rows_ref[b * sectors + before, r : r + 1, :]
        right = rows_ref[b * sectors + after, r : r + 1, :]
        weighted_ref[1 + line, edge - 1 : edge, :] = left * weights[line]
        weighted_ref[1 + line, edge + columns : edge + columns + 1, :] = right * weights[line]
    zeros = jnp.zeros(weighted_ref.shape[1:], jnp.float32)
    weighted_ref[0] = zeros
    weighted_ref[lines + 1] = zeros

    own_lanes = pl.ds(pl.multiple_of(band * width, width), width)
    taps = [taps_ref[t : t + 1, own_lanes] for t in range(len(OFFSETS))]

    def shifted(line, offset):
        a, b = offset
        return weighted_ref[1 + line - a, edge - b : edge - b + columns, :]

    for line in range(lines):
        total = shifted(line, (0, 0))
        for tap, offset in zip(taps, OFFSETS):
            total = total + tap * shifted(line, offset)
        grad_ref[line] = total

    key_all = rows_ref[:, 0:keys, :].reshape(key_total, width)
    value_all = rows_ref[:, keys : 2 * keys, :].reshape(key_total, width)
    key_heads = heads_of(key_all, width)
    value_heads = heads_of(value_all, width)
    query = query_ref[...].reshape(tokens, width)
    grad = grad_ref[...].reshape(tokens, width)

    logits = dot(key_heads, query, 1, 1) * scale
    prob_list = []
    for h in range(heads):
        part = logits[h * key_total : (h + 1) * key_total]
        raised = jnp.exp(part - jnp.max(part, 0, keepdims=True))
        prob_list.append(raised / jnp.sum(raised, 0, keepdims=True))
    probs = jnp.concatenate(prob_list, 0)
    out_ref[...] = dot(probs, value_heads, 0, 0).reshape(lines, columns, width)
    prob_grad = dot(value_heads, grad, 1, 1)
    logit_grad_list = []
    for h in range(heads):
        part = prob_grad[h * key_total : (h + 1) * key_total]
        row_dot = jnp.sum(prob_list[h] * part, 0, keepdims=True)
        logit_grad_list.append(prob_list[h] * (part - row_dot))
    logit_grad = jnp.concatenate(logit_grad_list, 0)

    key_grad = own_heads(dot(logit_grad, query, 1, 0), width, key_total) * scale
    value_grad = own_heads(dot(probs, grad, 1, 0), width, key_total)

    sums = [jnp.zeros((SUBLANES, width), jnp.float32) for _ in OFFSETS]
    for line in range(lines):
        out_line = out_ref[line]
        for t, offset in enumerate(OFFSETS):
            product = out_line * shifted(line, offset)
            for c in range(0, columns, SUBLANES):
                sums[t] = sums[t] + product[c : c + SUBLANES]
    tap_sum = jnp.concatenate([jnp.sum(s, 0, keepdims=True) for s in sums], 0)
    used = 2 * keys + len(OFFSETS)
    for device in range(bands * sectors):
        mine = slice(device * keys, (device + 1) * keys)
        start = device * used
        terms_ref[start : start + keys, :] = key_grad[mine]
        terms_ref[start + keys : start + 2 * keys, :] = value_grad[mine]
        terms_ref[start + 2 * keys : start + used, :] = tap_sum

    query_grad = (dot(logit_grad, key_heads, 0, 0) * scale).reshape(lines, columns, width)
    out_ref[...] = query_grad
    for step, query_grad_ref in enumerate(query_grad_refs):
        query_grad_ref[...] = out_ref[pl.ds(partner(band, step, bands) * rows, rows)]


def finish_kernel(bands, sectors, width, keys, *refs):
    part_refs = refs[:bands]
    terms_ref, query_ref, key_ref, value_ref, taps_ref = refs[bands:]
    band = lax.axis_index("lat")
    for step, part_ref in enumerate(part_refs):
        lanes = pl.ds(pl.multiple_of(source(band, step, bands) * width, width), width)
        query_ref[:, :, lanes] = part_ref[...]
    used = 2 * keys + len(OFFSETS)
    parts = []
    for to_band in range(bands):
        lanes = slice(to_band * width, (to_band + 1) * width)
        part = jnp.zeros((used, width), jnp.float32)
        for sector in range(sectors):
            start = (to_band * sectors + sector) * used
            part = part + terms_ref[start : start + used, :]
        key_ref[:, lanes] = part[0:keys]
        value_ref[:, lanes] = part[keys : 2 * keys]
        parts.append(part[2 * keys : used])
    tap_sum = jnp.concatenate(parts, 1)
    mean = jnp.sum(tap_sum * tap_sum, keepdims=True) / (len(OFFSETS) * width * bands)
    taps_ref[...] = tap_sum / jnp.sqrt(mean + 1e-06)


def split_heads_body(queries, key_rows, value_rows, cotangent, conv_taps):
    rows, columns, channels = queries.shape
    bands = lax.axis_size("lat")
    sectors = lax.axis_size("lon")
    devices = bands * sectors
    keys = key_rows.shape[0]
    width = channels // bands
    lines = rows * bands

    sent_rows = round_up(2 * keys + rows, SUBLANES)
    part_shape = (2, rows, columns, width)
    anywhere = pl.BlockSpec(memory_space=pl.ANY)
    row_blocks, *parts = pl.pallas_call(
        functools.partial(pack_kernel, bands, sectors, width, keys),
        out_shape=[
            jax.ShapeDtypeStruct(s, jnp.float32)
            for s in [(devices, sent_rows, width)] + [part_shape] * bands
        ],
        in_specs=[anywhere] * 4,
        scratch_shapes=[
            pltpu.VMEM((keys, channels), jnp.float32),
            pltpu.VMEM((keys, channels), jnp.float32),
            pltpu.VMEM((rows, SUBLANES, channels), jnp.float32),
            pltpu.VMEM((rows, SUBLANES, channels), jnp.float32),
            pltpu.SemaphoreType.DMA((4 + 2 * bands,)),
        ],
        compiler_params=pltpu.CompilerParams(vmem_limit_bytes=VMEM_LIMIT),
    )(*[in_hbm(x) for x in (key_rows, value_rows, queries, cotangent)])
    row_blocks = lax.all_to_all(row_blocks, ("lat", "lon"), 0, 0, tiled=True)
    parts = [parts[0]] + [exchange(parts[s], s, bands) for s in range(1, bands)]

    sent_terms = 2 * keys + len(OFFSETS)
    grid = (lines, columns, width)
    terms, *grad_parts = vmem_call(
        functools.partial(attention_kernel, bands, sectors, width, keys),
        [(devices * sent_terms, width)] + [(rows, columns, width)] * bands,
        [grid, (lines + 2, columns + 2 * SUBLANES, width), grid, grid],
    )(*parts, row_blocks, conv_taps)

    terms = terms.reshape(devices, sent_terms, 1, width)
    terms = lax.all_to_all(terms, ("lat", "lon"), 0, 0, tiled=True)
    terms = terms.reshape(devices * sent_terms, width)
    grad_parts = [grad_parts[0]] + [exchange(grad_parts[s], s, bands) for s in range(1, bands)]
    query_grad, key_grad, value_grad, tap_update = pl.pallas_call(
        functools.partial(finish_kernel, bands, sectors, width, keys),
        out_shape=[
            jax.ShapeDtypeStruct(s, jnp.float32)
            for s in (queries.shape, key_rows.shape, value_rows.shape, conv_taps.shape)
        ],
        compiler_params=pltpu.CompilerParams(vmem_limit_bytes=VMEM_LIMIT),
    )(*grad_parts, terms)
    return (query_grad, key_grad, value_grad, tap_update)


def extended(value, sides, width):
    for axis, dim in sides:
        peers, length = (lax.axis_size(axis), value.shape[dim])
        up = [(i, (i + 1) % peers) for i in range(peers)]
        down = [(j, i) for i, j in up]
        last = lax.slice_in_dim(value, length - width, length, axis=dim)
        initial = lax.slice_in_dim(value, 0, width, axis=dim)
        before = lax.ppermute(last, axis, up)
        after = lax.ppermute(initial, axis, down)
        value = jnp.concatenate([before, value, after], axis=dim)
    return value


def split_heads(matrix):
    return matrix.reshape(matrix.shape[0], -1, HD)


def latitude_weights(row_count, band_index, band_count):
    line_total = row_count * band_count
    centres = (jnp.arange(line_total, dtype=jnp.float32) + 0.5) * (jnp.pi / line_total)
    mean_cosine = jnp.sum(jnp.sin(centres)) / line_total
    mine = (band_index * row_count + jnp.arange(row_count, dtype=jnp.int32)).astype(jnp.float32)
    return jnp.sin((mine + 0.5) * (jnp.pi / line_total)) / mean_cosine


def close_poles(padded, row_dim, band_index, band_count):
    height = padded.shape[row_dim]
    positions = jnp.arange(height)
    outside = (positions == 0) & (band_index == 0) | (positions == height - 1) & (
        band_index == band_count - 1
    )
    shape_mask = [1] * padded.ndim
    shape_mask[row_dim] = height
    return jnp.where(outside.reshape(shape_mask), 0.0, padded)


def spread_taps(weighted, grad_padded, conv_taps):
    row_count, col_count = (weighted.shape[0], weighted.shape[1])
    result = weighted
    for tap_index, (shift_row, shift_col) in enumerate(OFFSETS):
        result = (
            result
            + conv_taps[tap_index]
            * grad_padded[
                1 - shift_row : 1 - shift_row + row_count, 1 - shift_col : 1 - shift_col + col_count
            ]
        )
    return result


def tap_terms(weighted, out_padded):
    row_count, col_count = (weighted.shape[0], weighted.shape[1])
    term_list = []
    for shift_row, shift_col in OFFSETS:
        term_list.append(
            jnp.sum(
                out_padded[
                    1 + shift_row : 1 + shift_row + row_count,
                    1 + shift_col : 1 + shift_col + col_count,
                ]
                * weighted,
                axis=(0, 1),
            )
        )
    return jnp.stack(term_list)


def group_logits(query_part, key_part):
    return jnp.einsum(
        "qhd,khd->hqk", split_heads(query_part), split_heads(key_part), precision=HIGH
    ) * HD ** (-0.5)


def whole_rows_body(queries, key_rows, value_rows, cotangent, conv_taps):
    row_count, col_count, channels = queries.shape
    band_count = lax.axis_size("lat")
    band_index = lax.axis_index("lat")
    weighted = cotangent * latitude_weights(row_count, band_index, band_count)[:, None, None]
    paired_rows = jnp.concatenate([key_rows, value_rows], 1)
    paired_all = lax.all_gather(paired_rows, ("lat", "lon"), axis=0, tiled=True)
    key_all = paired_all[:, :channels]
    value_all = paired_all[:, channels:]
    token_count = row_count * col_count
    key_count = key_all.shape[0]
    query_flat = queries.reshape(token_count, channels)
    group_width = 2 * HD
    group_count = channels // group_width
    outputs = []
    peaks = []
    sums_soft = []
    for group_index in range(group_count):
        col_start = group_index * group_width
        col_stop = col_start + group_width
        logits = group_logits(query_flat[:, col_start:col_stop], key_all[:, col_start:col_stop])
        row_peak = jnp.max(logits, -1, keepdims=True)
        raised = jnp.exp(logits - row_peak)
        normaliser = jnp.sum(raised, -1, keepdims=True)
        soft_weights = raised / normaliser
        outputs.append(
            jnp.einsum(
                "hqk,khd->qhd",
                soft_weights,
                split_heads(value_all[:, col_start:col_stop]),
                precision=HIGH,
            ).reshape(token_count, group_width)
        )
        peaks.append(row_peak)
        sums_soft.append(normaliser)
    out_flat = jnp.concatenate(outputs, 1)
    out_grid = out_flat.reshape(row_count, col_count, channels)
    both_padded = close_poles(
        extended(jnp.stack([weighted, out_grid]), (("lat", 1), ("lon", 2)), 1),
        1,
        band_index,
        band_count,
    )
    grad_padded = both_padded[0]
    out_padded = both_padded[1]
    out_grad = spread_taps(weighted, grad_padded, conv_taps)
    tap_sum = lax.psum(tap_terms(weighted, out_padded), ("lat", "lon"))
    tap_update = tap_sum / jnp.sqrt(jnp.mean(tap_sum * tap_sum) + 1e-06)
    grad_flat = out_grad.reshape(token_count, channels)
    query_parts = []
    key_parts = []
    value_parts = []
    for group_index in range(group_count):
        col_start = group_index * group_width
        col_stop = col_start + group_width
        query_heads = split_heads(query_flat[:, col_start:col_stop])
        key_heads = split_heads(key_all[:, col_start:col_stop])
        logits = jnp.einsum("qhd,khd->hqk", query_heads, key_heads, precision=HIGH) * HD ** (-0.5)
        soft_weights = jnp.exp(logits - peaks[group_index]) / sums_soft[group_index]
        grad_heads = split_heads(grad_flat[:, col_start:col_stop])
        value_parts.append(
            jnp.einsum("hqk,qhd->khd", soft_weights, grad_heads, precision=HIGH).reshape(
                key_count, group_width
            )
        )
        prob_grad = jnp.einsum(
            "qhd,khd->hqk",
            grad_heads,
            split_heads(value_all[:, col_start:col_stop]),
            precision=HIGH,
        )
        row_dot = jnp.transpose(
            jnp.sum(grad_heads * split_heads(out_flat[:, col_start:col_stop]), -1)
        )[:, :, None]
        logit_grad = soft_weights * (prob_grad - row_dot)
        query_parts.append(
            (
                jnp.einsum("hqk,khd->qhd", logit_grad, key_heads, precision=HIGH) * HD ** (-0.5)
            ).reshape(token_count, group_width)
        )
        key_parts.append(
            (
                jnp.einsum("hqk,qhd->khd", logit_grad, query_heads, precision=HIGH) * HD ** (-0.5)
            ).reshape(key_count, group_width)
        )
    paired_terms = jnp.concatenate(key_parts + value_parts, 1)
    paired_band = lax.psum_scatter(paired_terms, "lat", scatter_dimension=0, tiled=True)
    paired_grad = lax.psum_scatter(paired_band, "lon", scatter_dimension=0, tiled=True)
    key_grad = paired_grad[:, :channels]
    value_grad = paired_grad[:, channels:]
    query_grad = jnp.concatenate(query_parts, 1).reshape(row_count, col_count, channels)
    return (query_grad, key_grad, value_grad, tap_update)


def body(queries, key_rows, value_rows, cotangent, conv_taps):
    bands = lax.axis_size("lat")
    sectors = lax.axis_size("lon")
    columns, channels = queries.shape[1:]
    if channels % (bands * LANES) == 0 and sectors > 2 and columns % SUBLANES == 0:
        return split_heads_body(queries, key_rows, value_rows, cotangent, conv_taps)
    return whole_rows_body(queries, key_rows, value_rows, cotangent, conv_taps)


def solution(mesh):
    placed = (
        P("lat", "lon", None),
        P(("lat", "lon"), None),
        P(("lat", "lon"), None),
        P("lat", "lon", None),
        P(),
    )
    return jax.shard_map(
        body,
        mesh=mesh,
        in_specs=placed,
        out_specs=(P("lat", "lon", None), P(("lat", "lon"), None), P(("lat", "lon"), None), P()),
        check_vma=False,
    )
```

```python
import functools

import jax
import jax.numpy as jnp
import numpy as np
from jax import lax
from jax.experimental import pallas as pl
from jax.experimental.pallas import tpu as pltpu
from jax.sharding import PartitionSpec as P

HD = 64
LANES = 128
SUBLANES = 8
VMEM_LIMIT = 16 * 1024 * 1024

HIGH = lax.Precision.HIGHEST
OFFSETS = ((-1, -1), (-1, 0), (-1, 1), (0, -1), (0, 0), (0, 1), (1, -1), (1, 0), (1, 1))


def partner(index, step, peers):
    if peers & (peers - 1) == 0:
        return index ^ step
    return lax.rem(index + step, peers) if not isinstance(index, int) else (index + step) % peers


def source(index, step, peers):
    return partner(index, step if peers & (peers - 1) == 0 else peers - step, peers)


def exchange(value, step, peers):
    return lax.ppermute(value, "lat", [(i, partner(i, step, peers)) for i in range(peers)])


def to_all(blocks, devices):
    rows, width = blocks.shape
    blocks = blocks.reshape(devices, rows // devices, 1, width)
    return lax.all_to_all(blocks, ("lat", "lon"), 0, 0, tiled=True).reshape(rows, width)


def row_weights(line_total):
    cosine = np.sin((np.arange(line_total, dtype=np.float64) + 0.5) * (np.pi / line_total))
    return [float(w) for w in cosine / np.mean(cosine)]


def vmem_call(kernel, out_shapes, scratch=()):
    return pl.pallas_call(
        kernel,
        out_shape=[jax.ShapeDtypeStruct(s, jnp.float32) for s in out_shapes],
        scratch_shapes=[pltpu.VMEM(s, jnp.float32) for s in scratch],
        compiler_params=pltpu.CompilerParams(vmem_limit_bytes=VMEM_LIMIT),
    )


def block_rows(bands, keys, rows):
    return 2 * keys + rows


def term_rows(keys):
    return 2 * keys + len(OFFSETS)


def in_hbm(array):
    return pltpu.with_memory_space_constraint(array, pltpu.HBM)


def pack_kernel(bands, sectors, width, keys, *refs):
    key_ref, value_ref, query_ref, cotangent_ref, sent_ref = refs[:5]
    part_refs = refs[5 : 5 + bands]
    key_own, value_own, first_own, last_own, block_ref, sems = refs[5 + bands :]
    band = lax.axis_index("lat")
    sector = lax.axis_index("lon")
    rows, columns = query_ref.shape[:2]
    sent = block_rows(bands, keys, rows)

    small = [
        pltpu.make_async_copy(source_ref, target_ref, sems.at[i])
        for i, (source_ref, target_ref) in enumerate(
            (
                (key_ref, key_own),
                (value_ref, value_own),
                (cotangent_ref.at[:, 0:SUBLANES, :], first_own),
                (cotangent_ref.at[:, columns - SUBLANES : columns, :], last_own),
            )
        )
    ]
    for copy in small:
        copy.start()
    large = []
    for step, part_ref in enumerate(part_refs):
        lanes = pl.ds(pl.multiple_of(partner(band, step, bands) * width, width), width)
        for i, array_ref in enumerate((query_ref, cotangent_ref)):
            large.append(
                pltpu.make_async_copy(
                    array_ref.at[:, :, lanes], part_ref.at[i], sems.at[len(small) + len(large)]
                )
            )
    for copy in large:
        copy.start()
    for copy in small:
        copy.wait()
    for to_band in range(bands):
        lanes = slice(to_band * width, (to_band + 1) * width)
        key = key_own[:, lanes]
        value = value_own[:, lanes]
        first = first_own[:, 0, lanes]
        last = last_own[:, SUBLANES - 1, lanes]
        for to_sector in range(sectors):
            device = to_band * sectors + to_sector
            is_next = lax.rem(to_sector - sector + sectors, sectors) == 1
            start = device * sent
            block_ref[start : start + keys, :] = key
            start = start + keys
            block_ref[start : start + keys, :] = value
            block_ref[start + keys : start + keys + rows, :] = jnp.where(is_next, last, first)
    send = pltpu.make_async_copy(block_ref, sent_ref, sems.at[len(small) + len(large)])
    send.start()
    for copy in large:
        copy.wait()
    send.wait()


def arrival_kernel(part_ref, out_ref):
    out_ref[...] = part_ref[...]


def heads_of(matrix, width):
    lane = lax.broadcasted_iota(jnp.int32, matrix.shape, 1)
    return jnp.concatenate(
        [
            jnp.where((lane >= h * HD) & (lane < (h + 1) * HD), matrix, 0.0)
            for h in range(width // HD)
        ],
        0,
    )


def own_heads(matrix, width, keys):
    lane = lax.broadcasted_iota(jnp.int32, (keys, width), 1)
    result = matrix[0:keys]
    for h in range(1, width // HD):
        result = jnp.where(lane >= h * HD, matrix[h * keys : (h + 1) * keys], result)
    return result


def rows_from_all(rows_ref, first, keys, devices, sent):
    return jnp.concatenate(
        [rows_ref[pl.ds(first + k, devices, stride=sent), :] for k in range(keys)], 0
    )


def dot(left, right, left_dim, right_dim, precision=None):
    return lax.dot_general(
        left,
        right,
        (((left_dim,), (right_dim,)), ((), ())),
        precision=precision,
        preferred_element_type=jnp.float32,
    )


def split(value, terms):
    result = []
    for _ in range(terms):
        result.append(value.astype(jnp.bfloat16))
        value = value - result[-1].astype(jnp.float32)
    return result


def rows_by_tokens(rows, tokens):
    count = rows.shape[0]
    large, middle, small = split(rows, 3)
    token_large, token_middle, token_small = split(tokens, 3)
    left = jnp.concatenate(
        [
            jnp.concatenate([large, large], 1),
            jnp.concatenate([middle, middle], 1),
            jnp.concatenate([small, jnp.zeros_like(small)], 1),
        ],
        0,
    )
    main = dot(left, jnp.concatenate([token_large, token_middle], 1), 1, 1)
    rest = dot(large, token_small, 1, 1)
    return main[0:count] + (main[count : 2 * count] + (main[2 * count :] + rest))


def sum_over_tokens(left, right):
    count, width = left.shape[0], right.shape[1]
    every = dot(jnp.concatenate(split(left, 2), 0), jnp.concatenate(split(right, 2), 1), 1, 0)
    top, bottom = every[0:count], every[count:]
    return top[:, 0:width] + (top[:, width:] + bottom[:, 0:width] + bottom[:, width:])


def mix_rows(weights, rows):
    width = rows.shape[1]
    right = jnp.concatenate(split(rows, 2), 1)
    every = dot(jnp.concatenate(split(weights, 2), 0), jnp.concatenate([right, right], 0), 0, 0)
    return every[:, 0:width] + every[:, width:]


def mix_rows_exactly(weights, rows):
    width = rows.shape[1]
    large, middle, small = split(weights, 3)
    row_large, row_middle, row_small = split(rows, 3)
    zero = jnp.zeros_like(row_large)
    right = jnp.concatenate(
        [
            jnp.concatenate([row_large, row_large, row_large, zero], 0),
            jnp.concatenate([row_middle, row_middle, zero, row_small], 0),
        ],
        1,
    )
    every = dot(jnp.concatenate([large, middle, small, large], 0), right, 0, 0)
    return every[:, 0:width] + every[:, width:]


def attention_kernel(bands, sectors, width, keys, *refs):
    part_refs = refs[:bands]
    rows_ref, taps_ref, terms_ref = refs[bands : bands + 3]
    query_grad_refs = refs[bands + 3 : 2 * bands + 3]
    query_ref, weighted_ref, grad_ref, out_ref = refs[2 * bands + 3 :]
    band = lax.axis_index("lat")
    sector = lax.axis_index("lon")
    rows, columns = part_refs[0].shape[1:3]
    lines = rows * bands
    tokens = lines * columns
    edge = SUBLANES
    scale = HD ** (-0.5)
    weights = row_weights(lines)
    heads = width // HD
    devices = bands * sectors
    key_total = devices * keys
    sent = block_rows(bands, keys, rows)

    for step, part_ref in enumerate(part_refs):
        start = source(band, step, bands) * rows
        query_ref[pl.ds(start, rows)] = part_ref[0]
        weighted_ref[pl.ds(start + 1, rows), edge : edge + columns, :] = part_ref[1]
    before = lax.rem(sector + sectors - 1, sectors)
    after = lax.rem(sector + 1, sectors)
    for line in range(lines):
        b, r = divmod(line, rows)
        r = 2 * keys + r
        inner = weighted_ref[1 + line, edge : edge + columns, :]
        weighted_ref[1 + line, edge : edge + columns, :] = inner * weights[line]
        left = rows_ref[pl.ds((b * sectors + before) * sent + r, 1), :]
        right = rows_ref[pl.ds((b * sectors + after) * sent + r, 1), :]
        weighted_ref[1 + line, edge - 1 : edge, :] = left * weights[line]
        weighted_ref[1 + line, edge + columns : edge + columns + 1, :] = right * weights[line]
    zeros = jnp.zeros(weighted_ref.shape[1:], jnp.float32)
    weighted_ref[0] = zeros
    weighted_ref[lines + 1] = zeros

    own_lanes = pl.ds(pl.multiple_of(band * width, width), width)
    taps = [taps_ref[t : t + 1, own_lanes] for t in range(len(OFFSETS))]

    def shifted(line, offset):
        a, b = offset
        return weighted_ref[1 + line - a, edge - b : edge - b + columns, :]

    for line in range(lines):
        total = shifted(line, (0, 0))
        for tap, offset in zip(taps, OFFSETS):
            total = total + tap * shifted(line, offset)
        grad_ref[line] = total

    key_heads = heads_of(rows_from_all(rows_ref, 0, keys, devices, sent), width)
    value_heads = heads_of(rows_from_all(rows_ref, keys, keys, devices, sent), width)
    query = query_ref[...].reshape(tokens, width)
    grad = grad_ref[...].reshape(tokens, width)

    logits = rows_by_tokens(key_heads, query) * scale
    prob_list = []
    for h in range(heads):
        part = logits[h * key_total : (h + 1) * key_total]
        raised = jnp.exp(part - jnp.max(part, 0, keepdims=True))
        prob_list.append(raised / jnp.sum(raised, 0, keepdims=True))
    probs = jnp.concatenate(prob_list, 0)
    out_ref[...] = mix_rows(probs, value_heads).reshape(lines, columns, width)
    prob_grad = rows_by_tokens(value_heads, grad)
    logit_grad_list = []
    for h in range(heads):
        part = prob_grad[h * key_total : (h + 1) * key_total]
        row_dot = jnp.sum(prob_list[h] * part, 0, keepdims=True)
        logit_grad_list.append(prob_list[h] * (part - row_dot))
    logit_grad = jnp.concatenate(logit_grad_list, 0)

    key_grad = own_heads(sum_over_tokens(logit_grad, query), width, key_total) * scale
    value_grad = own_heads(sum_over_tokens(probs, grad), width, key_total)

    sums = [jnp.zeros((SUBLANES, width), jnp.float32) for _ in OFFSETS]
    for line in range(lines):
        out_line = out_ref[line]
        for t, offset in enumerate(OFFSETS):
            product = out_line * shifted(line, offset)
            for c in range(0, columns, SUBLANES):
                sums[t] = sums[t] + product[c : c + SUBLANES]
    tap_sum = jnp.concatenate([jnp.sum(s, 0, keepdims=True) for s in sums], 0)
    used = term_rows(keys)
    for k in range(keys):
        mine = slice(k * devices, (k + 1) * devices)
        terms_ref[pl.ds(k, devices, stride=used), :] = key_grad[mine]
        terms_ref[pl.ds(keys + k, devices, stride=used), :] = value_grad[mine]
    for device in range(devices):
        terms_ref[device * used + 2 * keys : (device + 1) * used, :] = tap_sum

    out_ref[...] = (mix_rows_exactly(logit_grad, key_heads) * scale).reshape(out_ref.shape)
    for step, part_ref in enumerate(query_grad_refs):
        part_ref[...] = out_ref[pl.ds(partner(band, step, bands) * rows, rows)]


def finish_kernel(bands, sectors, width, keys, *refs):
    part_refs = refs[:bands]
    terms_ref, query_ref, key_ref, value_ref, taps_ref = refs[bands:]
    band = lax.axis_index("lat")
    devices = bands * sectors
    rows, columns = query_ref.shape[:2]
    for step, part_ref in enumerate(part_refs):
        lanes = pl.ds(pl.multiple_of(source(band, step, bands) * width, width), width)
        query_ref[:, :, lanes] = part_ref[...]
    used = term_rows(keys)
    parts = []
    for to_band in range(bands):
        lanes = slice(to_band * width, (to_band + 1) * width)
        part = jnp.zeros((used, width), jnp.float32)
        for sector in range(sectors):
            start = (to_band * sectors + sector) * used
            part = part + terms_ref[start : start + used, :]
        key_ref[:, lanes] = part[0:keys]
        value_ref[:, lanes] = part[keys : 2 * keys]
        parts.append(part[2 * keys : used])
    tap_sum = jnp.concatenate(parts, 1)
    mean = jnp.sum(tap_sum * tap_sum, keepdims=True) / (len(OFFSETS) * width * bands)
    taps_ref[...] = tap_sum / jnp.sqrt(mean + 1e-06)


def split_heads_body(queries, key_rows, value_rows, cotangent, conv_taps):
    rows, columns, channels = queries.shape
    bands = lax.axis_size("lat")
    sectors = lax.axis_size("lon")
    devices = bands * sectors
    keys = key_rows.shape[0]
    width = channels // bands
    lines = rows * bands

    sent_rows = block_rows(bands, keys, rows)
    part_shape = (2, rows, columns, width)
    anywhere = pl.BlockSpec(memory_space=pl.ANY)
    here = pl.BlockSpec(memory_space=pltpu.VMEM)
    row_blocks, *parts = pl.pallas_call(
        functools.partial(pack_kernel, bands, sectors, width, keys),
        out_shape=[
            jax.ShapeDtypeStruct(s, jnp.float32)
            for s in [(devices * sent_rows, width)] + [part_shape] * bands
        ],
        in_specs=[anywhere] * 4,
        out_specs=[anywhere] + [here] * bands,
        scratch_shapes=[
            pltpu.VMEM((keys, channels), jnp.float32),
            pltpu.VMEM((keys, channels), jnp.float32),
            pltpu.VMEM((rows, SUBLANES, channels), jnp.float32),
            pltpu.VMEM((rows, SUBLANES, channels), jnp.float32),
            pltpu.VMEM((devices * sent_rows, width), jnp.float32),
            pltpu.SemaphoreType.DMA((5 + 2 * bands,)),
        ],
        compiler_params=pltpu.CompilerParams(vmem_limit_bytes=VMEM_LIMIT),
    )(*[in_hbm(x) for x in (key_rows, value_rows, queries, cotangent)])
    row_blocks = to_all(row_blocks, devices)
    (first_part,) = pl.pallas_call(
        arrival_kernel,
        out_shape=[jax.ShapeDtypeStruct(part_shape, jnp.float32)],
        cost_estimate=pl.CostEstimate(flops=10**9, bytes_accessed=10**6, transcendentals=0),
        compiler_params=pltpu.CompilerParams(vmem_limit_bytes=VMEM_LIMIT),
    )(exchange(parts[-1], bands - 1, bands))
    parts = [parts[0]] + [exchange(parts[s], s, bands) for s in range(1, bands - 1)] + [first_part]

    grid = (lines, columns, width)
    heads = width // HD
    terms, *grad_parts = vmem_call(
        functools.partial(attention_kernel, bands, sectors, width, keys),
        [(devices * term_rows(keys), width)] + [(rows, columns, width)] * bands,
        [
            grid,
            (lines + 2, columns + 2 * SUBLANES, width),
            grid,
            grid,
        ],
    )(*parts, row_blocks, conv_taps)

    terms = to_all(terms, devices)
    grad_parts = [grad_parts[0]] + [
        exchange(grad_parts[s], s, bands) for s in range(1, bands)
    ]
    query_grad, key_grad, value_grad, tap_update = pl.pallas_call(
        functools.partial(finish_kernel, bands, sectors, width, keys),
        out_shape=[
            jax.ShapeDtypeStruct(s, jnp.float32)
            for s in (queries.shape, key_rows.shape, value_rows.shape, conv_taps.shape)
        ],
        compiler_params=pltpu.CompilerParams(vmem_limit_bytes=VMEM_LIMIT),
    )(*grad_parts, terms)
    return (query_grad, key_grad, value_grad, tap_update)


def extended(value, sides, width):
    for axis, dim in sides:
        peers, length = (lax.axis_size(axis), value.shape[dim])
        up = [(i, (i + 1) % peers) for i in range(peers)]
        down = [(j, i) for i, j in up]
        last = lax.slice_in_dim(value, length - width, length, axis=dim)
        initial = lax.slice_in_dim(value, 0, width, axis=dim)
        before = lax.ppermute(last, axis, up)
        after = lax.ppermute(initial, axis, down)
        value = jnp.concatenate([before, value, after], axis=dim)
    return value


def split_heads(matrix):
    return matrix.reshape(matrix.shape[0], -1, HD)


def latitude_weights(row_count, band_index, band_count):
    line_total = row_count * band_count
    centres = (jnp.arange(line_total, dtype=jnp.float32) + 0.5) * (jnp.pi / line_total)
    mean_cosine = jnp.sum(jnp.sin(centres)) / line_total
    mine = (band_index * row_count + jnp.arange(row_count, dtype=jnp.int32)).astype(jnp.float32)
    return jnp.sin((mine + 0.5) * (jnp.pi / line_total)) / mean_cosine


def close_poles(padded, row_dim, band_index, band_count):
    height = padded.shape[row_dim]
    positions = jnp.arange(height)
    outside = (positions == 0) & (band_index == 0) | (positions == height - 1) & (
        band_index == band_count - 1
    )
    shape_mask = [1] * padded.ndim
    shape_mask[row_dim] = height
    return jnp.where(outside.reshape(shape_mask), 0.0, padded)


def spread_taps(weighted, grad_padded, conv_taps):
    row_count, col_count = (weighted.shape[0], weighted.shape[1])
    result = weighted
    for tap_index, (shift_row, shift_col) in enumerate(OFFSETS):
        result = (
            result
            + conv_taps[tap_index]
            * grad_padded[
                1 - shift_row : 1 - shift_row + row_count, 1 - shift_col : 1 - shift_col + col_count
            ]
        )
    return result


def tap_terms(weighted, out_padded):
    row_count, col_count = (weighted.shape[0], weighted.shape[1])
    term_list = []
    for shift_row, shift_col in OFFSETS:
        term_list.append(
            jnp.sum(
                out_padded[
                    1 + shift_row : 1 + shift_row + row_count,
                    1 + shift_col : 1 + shift_col + col_count,
                ]
                * weighted,
                axis=(0, 1),
            )
        )
    return jnp.stack(term_list)


def group_logits(query_part, key_part):
    return jnp.einsum(
        "qhd,khd->hqk", split_heads(query_part), split_heads(key_part), precision=HIGH
    ) * HD ** (-0.5)


def whole_rows_body(queries, key_rows, value_rows, cotangent, conv_taps):
    row_count, col_count, channels = queries.shape
    band_count = lax.axis_size("lat")
    band_index = lax.axis_index("lat")
    weighted = cotangent * latitude_weights(row_count, band_index, band_count)[:, None, None]
    paired_rows = jnp.concatenate([key_rows, value_rows], 1)
    paired_all = lax.all_gather(paired_rows, ("lat", "lon"), axis=0, tiled=True)
    key_all = paired_all[:, :channels]
    value_all = paired_all[:, channels:]
    token_count = row_count * col_count
    key_count = key_all.shape[0]
    query_flat = queries.reshape(token_count, channels)
    group_width = 2 * HD
    group_count = channels // group_width
    outputs = []
    peaks = []
    sums_soft = []
    for group_index in range(group_count):
        col_start = group_index * group_width
        col_stop = col_start + group_width
        logits = group_logits(query_flat[:, col_start:col_stop], key_all[:, col_start:col_stop])
        row_peak = jnp.max(logits, -1, keepdims=True)
        raised = jnp.exp(logits - row_peak)
        normaliser = jnp.sum(raised, -1, keepdims=True)
        soft_weights = raised / normaliser
        outputs.append(
            jnp.einsum(
                "hqk,khd->qhd",
                soft_weights,
                split_heads(value_all[:, col_start:col_stop]),
                precision=HIGH,
            ).reshape(token_count, group_width)
        )
        peaks.append(row_peak)
        sums_soft.append(normaliser)
    out_flat = jnp.concatenate(outputs, 1)
    out_grid = out_flat.reshape(row_count, col_count, channels)
    both_padded = close_poles(
        extended(jnp.stack([weighted, out_grid]), (("lat", 1), ("lon", 2)), 1),
        1,
        band_index,
        band_count,
    )
    grad_padded = both_padded[0]
    out_padded = both_padded[1]
    out_grad = spread_taps(weighted, grad_padded, conv_taps)
    tap_sum = lax.psum(tap_terms(weighted, out_padded), ("lat", "lon"))
    tap_update = tap_sum / jnp.sqrt(jnp.mean(tap_sum * tap_sum) + 1e-06)
    grad_flat = out_grad.reshape(token_count, channels)
    query_parts = []
    key_parts = []
    value_parts = []
    for group_index in range(group_count):
        col_start = group_index * group_width
        col_stop = col_start + group_width
        query_heads = split_heads(query_flat[:, col_start:col_stop])
        key_heads = split_heads(key_all[:, col_start:col_stop])
        logits = jnp.einsum("qhd,khd->hqk", query_heads, key_heads, precision=HIGH) * HD ** (-0.5)
        soft_weights = jnp.exp(logits - peaks[group_index]) / sums_soft[group_index]
        grad_heads = split_heads(grad_flat[:, col_start:col_stop])
        value_parts.append(
            jnp.einsum("hqk,qhd->khd", soft_weights, grad_heads, precision=HIGH).reshape(
                key_count, group_width
            )
        )
        prob_grad = jnp.einsum(
            "qhd,khd->hqk",
            grad_heads,
            split_heads(value_all[:, col_start:col_stop]),
            precision=HIGH,
        )
        row_dot = jnp.transpose(
            jnp.sum(grad_heads * split_heads(out_flat[:, col_start:col_stop]), -1)
        )[:, :, None]
        logit_grad = soft_weights * (prob_grad - row_dot)
        query_parts.append(
            (
                jnp.einsum("hqk,khd->qhd", logit_grad, key_heads, precision=HIGH) * HD ** (-0.5)
            ).reshape(token_count, group_width)
        )
        key_parts.append(
            (
                jnp.einsum("hqk,qhd->khd", logit_grad, query_heads, precision=HIGH) * HD ** (-0.5)
            ).reshape(key_count, group_width)
        )
    paired_terms = jnp.concatenate(key_parts + value_parts, 1)
    paired_band = lax.psum_scatter(paired_terms, "lat", scatter_dimension=0, tiled=True)
    paired_grad = lax.psum_scatter(paired_band, "lon", scatter_dimension=0, tiled=True)
    key_grad = paired_grad[:, :channels]
    value_grad = paired_grad[:, channels:]
    query_grad = jnp.concatenate(query_parts, 1).reshape(row_count, col_count, channels)
    return (query_grad, key_grad, value_grad, tap_update)


def body(queries, key_rows, value_rows, cotangent, conv_taps):
    bands = lax.axis_size("lat")
    sectors = lax.axis_size("lon")
    rows, columns, channels = queries.shape
    whole_heads = channels % (bands * LANES) == 0
    whole_tiles = columns % SUBLANES == 0 and (rows * columns) % LANES == 0
    if whole_heads and whole_tiles and sectors > 2:
        return split_heads_body(queries, key_rows, value_rows, cotangent, conv_taps)
    return whole_rows_body(queries, key_rows, value_rows, cotangent, conv_taps)


def solution(mesh):
    placed = (
        P("lat", "lon", None),
        P(("lat", "lon"), None),
        P(("lat", "lon"), None),
        P("lat", "lon", None),
        P(),
    )
    return jax.shard_map(
        body,
        mesh=mesh,
        in_specs=placed,
        out_specs=(P("lat", "lon", None), P(("lat", "lon"), None), P(("lat", "lon"), None), P()),
        check_vma=False,
    )
```

```python
import functools

import jax
import jax.numpy as jnp
import numpy as np
from jax import lax
from jax.experimental import pallas as pl
from jax.experimental.pallas import tpu as pltpu
from jax.sharding import PartitionSpec as P

HD = 64
LANES = 128
SUBLANES = 8
VMEM_LIMIT = 16 * 1024 * 1024

HIGH = lax.Precision.HIGHEST
OFFSETS = ((-1, -1), (-1, 0), (-1, 1), (0, -1), (0, 0), (0, 1), (1, -1), (1, 0), (1, 1))


def partner(index, step, peers):
    if peers & (peers - 1) == 0:
        return index ^ step
    return lax.rem(index + step, peers) if not isinstance(index, int) else (index + step) % peers


def source(index, step, peers):
    return partner(index, step if peers & (peers - 1) == 0 else peers - step, peers)


def exchange(value, step, peers):
    return lax.ppermute(value, "lat", [(i, partner(i, step, peers)) for i in range(peers)])


def to_all(blocks, devices):
    rows, width = blocks.shape
    blocks = blocks.reshape(devices, rows // devices, 1, width)
    return lax.all_to_all(blocks, ("lat", "lon"), 0, 0, tiled=True).reshape(rows, width)


def row_weights(line_total):
    cosine = np.sin((np.arange(line_total, dtype=np.float64) + 0.5) * (np.pi / line_total))
    return [float(w) for w in cosine / np.mean(cosine)]


def vmem_call(kernel, out_shapes, scratch=()):
    return pl.pallas_call(
        kernel,
        out_shape=[jax.ShapeDtypeStruct(s, jnp.float32) for s in out_shapes],
        scratch_shapes=[pltpu.VMEM(s, jnp.float32) for s in scratch],
        compiler_params=pltpu.CompilerParams(vmem_limit_bytes=VMEM_LIMIT),
    )


def arrival_kernel(part_ref, out_ref):
    out_ref[...] = part_ref[...]


def exchange_all(parts, bands, ahead):
    last = exchange(parts[-1], bands - 1, bands)
    cost = pl.CostEstimate(flops=10**9, bytes_accessed=10**6, transcendentals=0)
    (last,) = pl.pallas_call(
        arrival_kernel,
        out_shape=[jax.ShapeDtypeStruct(last.shape, jnp.float32)],
        cost_estimate=cost if ahead else None,
        compiler_params=pltpu.CompilerParams(vmem_limit_bytes=VMEM_LIMIT),
    )(last)
    return [parts[0]] + [exchange(parts[s], s, bands) for s in range(1, bands - 1)] + [last]


def block_rows(bands, keys, rows):
    return 2 * keys + rows


def term_rows(keys):
    return 2 * keys + len(OFFSETS)


def in_hbm(array):
    return pltpu.with_memory_space_constraint(array, pltpu.HBM)


def pack_kernel(bands, sectors, width, keys, *refs):
    key_ref, value_ref, query_ref, cotangent_ref, sent_ref = refs[:5]
    part_refs = refs[5 : 5 + bands]
    key_own, value_own, first_own, last_own, block_ref, sems = refs[5 + bands :]
    band = lax.axis_index("lat")
    sector = lax.axis_index("lon")
    rows, columns = query_ref.shape[:2]
    sent = block_rows(bands, keys, rows)

    small = [
        pltpu.make_async_copy(source_ref, target_ref, sems.at[i])
        for i, (source_ref, target_ref) in enumerate(
            (
                (key_ref, key_own),
                (value_ref, value_own),
                (cotangent_ref.at[:, 0:1, :], first_own),
                (cotangent_ref.at[:, columns - 1 : columns, :], last_own),
            )
        )
    ]
    for copy in small:
        copy.start()
    large = []
    for step, part_ref in enumerate(part_refs):
        lanes = pl.ds(pl.multiple_of(partner(band, step, bands) * width, width), width)
        for i, array_ref in enumerate((query_ref, cotangent_ref)):
            large.append(
                pltpu.make_async_copy(
                    array_ref.at[:, :, lanes], part_ref.at[i], sems.at[len(small) + len(large)]
                )
            )
    for copy in large:
        copy.start()
    for copy in small:
        copy.wait()
    for to_band in range(bands):
        lanes = slice(to_band * width, (to_band + 1) * width)
        key = key_own[:, lanes]
        value = value_own[:, lanes]
        first = first_own[:, 0, lanes]
        last = last_own[:, 0, lanes]
        for to_sector in range(sectors):
            device = to_band * sectors + to_sector
            is_next = lax.rem(to_sector - sector + sectors, sectors) == 1
            start = device * sent
            block_ref[start : start + keys, :] = key
            start = start + keys
            block_ref[start : start + keys, :] = value
            block_ref[start + keys : start + keys + rows, :] = jnp.where(is_next, last, first)
    send = pltpu.make_async_copy(block_ref, sent_ref, sems.at[len(small) + len(large)])
    send.start()
    for copy in large:
        copy.wait()
    send.wait()


def heads_of(matrix, width):
    lane = lax.broadcasted_iota(jnp.int32, matrix.shape, 1)
    return jnp.concatenate(
        [
            jnp.where((lane >= h * HD) & (lane < (h + 1) * HD), matrix, 0.0)
            for h in range(width // HD)
        ],
        0,
    )


def own_heads(matrix, width, keys):
    lane = lax.broadcasted_iota(jnp.int32, (keys, width), 1)
    result = matrix[0:keys]
    for h in range(1, width // HD):
        result = jnp.where(lane >= h * HD, matrix[h * keys : (h + 1) * keys], result)
    return result


def rows_from_all(rows_ref, first, keys, devices, sent):
    return jnp.concatenate(
        [rows_ref[pl.ds(first + k, devices, stride=sent), :] for k in range(keys)], 0
    )


def dot(left, right, left_dim, right_dim, precision=None):
    return lax.dot_general(
        left,
        right,
        (((left_dim,), (right_dim,)), ((), ())),
        precision=precision,
        preferred_element_type=jnp.float32,
    )


def split(value, terms):
    result = []
    for _ in range(terms):
        result.append(value.astype(jnp.bfloat16))
        value = value - result[-1].astype(jnp.float32)
    return result


def rows_by_tokens(rows, tokens):
    count = rows.shape[0]
    large, middle, small = split(rows, 3)
    token_large, token_middle, token_small = split(tokens, 3)
    left = jnp.concatenate(
        [
            jnp.concatenate([large, large], 1),
            jnp.concatenate([middle, middle], 1),
            jnp.concatenate([small, jnp.zeros_like(small)], 1),
        ],
        0,
    )
    main = dot(left, jnp.concatenate([token_large, token_middle], 1), 1, 1)
    rest = dot(large, token_small, 1, 1)
    return main[0:count] + (main[count : 2 * count] + (main[2 * count :] + rest))


def sum_over_tokens(left, right):
    count, width = left.shape[0], right.shape[1]
    every = dot(jnp.concatenate(split(left, 2), 0), jnp.concatenate(split(right, 2), 1), 1, 0)
    top, bottom = every[0:count], every[count:]
    return top[:, 0:width] + (top[:, width:] + bottom[:, 0:width] + bottom[:, width:])


def mix_rows(weights, rows):
    width = rows.shape[1]
    right = jnp.concatenate(split(rows, 2), 1)
    every = dot(jnp.concatenate(split(weights, 2), 0), jnp.concatenate([right, right], 0), 0, 0)
    return every[:, 0:width] + every[:, width:]


def mix_rows_exactly(weights, rows):
    width = rows.shape[1]
    large, middle, small = split(weights, 3)
    row_large, row_middle, row_small = split(rows, 3)
    zero = jnp.zeros_like(row_large)
    right = jnp.concatenate(
        [
            jnp.concatenate([row_large, row_large, row_large, zero], 0),
            jnp.concatenate([row_middle, row_middle, zero, row_small], 0),
        ],
        1,
    )
    every = dot(jnp.concatenate([large, middle, small, large], 0), right, 0, 0)
    return every[:, 0:width] + every[:, width:]


def attention_kernel(bands, sectors, width, keys, *refs):
    part_refs = refs[:bands]
    rows_ref, taps_ref, terms_ref = refs[bands : bands + 3]
    query_grad_refs = refs[bands + 3 : 2 * bands + 3]
    query_ref, weighted_ref, grad_ref, out_ref = refs[2 * bands + 3 :]
    band = lax.axis_index("lat")
    sector = lax.axis_index("lon")
    rows, columns = part_refs[0].shape[1:3]
    lines = rows * bands
    tokens = lines * columns
    edge = SUBLANES
    scale = HD ** (-0.5)
    weights = row_weights(lines)
    heads = width // HD
    devices = bands * sectors
    key_total = devices * keys
    sent = block_rows(bands, keys, rows)

    for step, part_ref in enumerate(part_refs):
        start = source(band, step, bands) * rows
        query_ref[pl.ds(start, rows)] = part_ref[0]
        weighted_ref[pl.ds(start + 1, rows), edge : edge + columns, :] = part_ref[1]
    before = lax.rem(sector + sectors - 1, sectors)
    after = lax.rem(sector + 1, sectors)
    for line in range(lines):
        b, r = divmod(line, rows)
        r = 2 * keys + r
        inner = weighted_ref[1 + line, edge : edge + columns, :]
        weighted_ref[1 + line, edge : edge + columns, :] = inner * weights[line]
        left = rows_ref[pl.ds((b * sectors + before) * sent + r, 1), :]
        right = rows_ref[pl.ds((b * sectors + after) * sent + r, 1), :]
        weighted_ref[1 + line, edge - 1 : edge, :] = left * weights[line]
        weighted_ref[1 + line, edge + columns : edge + columns + 1, :] = right * weights[line]
    zeros = jnp.zeros(weighted_ref.shape[1:], jnp.float32)
    weighted_ref[0] = zeros
    weighted_ref[lines + 1] = zeros

    own_lanes = pl.ds(pl.multiple_of(band * width, width), width)
    taps = [taps_ref[t : t + 1, own_lanes] for t in range(len(OFFSETS))]

    def shifted(line, offset):
        a, b = offset
        return weighted_ref[1 + line - a, edge - b : edge - b + columns, :]

    for line in range(lines):
        total = shifted(line, (0, 0))
        for tap, offset in zip(taps, OFFSETS):
            total = total + tap * shifted(line, offset)
        grad_ref[line] = total

    key_heads = heads_of(rows_from_all(rows_ref, 0, keys, devices, sent), width)
    value_heads = heads_of(rows_from_all(rows_ref, keys, keys, devices, sent), width)
    query = query_ref[...].reshape(tokens, width)
    grad = grad_ref[...].reshape(tokens, width)

    logits = rows_by_tokens(key_heads, query) * scale
    prob_list = []
    for h in range(heads):
        part = logits[h * key_total : (h + 1) * key_total]
        raised = jnp.exp(part - jnp.max(part, 0, keepdims=True))
        prob_list.append(raised / jnp.sum(raised, 0, keepdims=True))
    probs = jnp.concatenate(prob_list, 0)
    out_ref[...] = mix_rows(probs, value_heads).reshape(lines, columns, width)
    prob_grad = rows_by_tokens(value_heads, grad)
    logit_grad_list = []
    for h in range(heads):
        part = prob_grad[h * key_total : (h + 1) * key_total]
        row_dot = jnp.sum(prob_list[h] * part, 0, keepdims=True)
        logit_grad_list.append(prob_list[h] * (part - row_dot))
    logit_grad = jnp.concatenate(logit_grad_list, 0)

    key_grad = own_heads(sum_over_tokens(logit_grad, query), width, key_total) * scale
    value_grad = own_heads(sum_over_tokens(probs, grad), width, key_total)

    sums = [jnp.zeros((SUBLANES, width), jnp.float32) for _ in OFFSETS]
    for line in range(lines):
        out_line = out_ref[line]
        for t, offset in enumerate(OFFSETS):
            product = out_line * shifted(line, offset)
            for c in range(0, columns, SUBLANES):
                sums[t] = sums[t] + product[c : c + SUBLANES]
    tap_sum = jnp.concatenate([jnp.sum(s, 0, keepdims=True) for s in sums], 0)
    used = term_rows(keys)
    for k in range(keys):
        mine = slice(k * devices, (k + 1) * devices)
        terms_ref[pl.ds(k, devices, stride=used), :] = key_grad[mine]
        terms_ref[pl.ds(keys + k, devices, stride=used), :] = value_grad[mine]
    for device in range(devices):
        terms_ref[device * used + 2 * keys : (device + 1) * used, :] = tap_sum

    out_ref[...] = (mix_rows_exactly(logit_grad, key_heads) * scale).reshape(out_ref.shape)
    for step, part_ref in enumerate(query_grad_refs):
        part_ref[...] = out_ref[pl.ds(partner(band, step, bands) * rows, rows)]


def finish_kernel(bands, sectors, width, keys, *refs):
    part_refs = refs[:bands]
    terms_ref, query_ref, key_ref, value_ref, taps_ref = refs[bands:]
    band = lax.axis_index("lat")
    devices = bands * sectors
    rows, columns = query_ref.shape[:2]
    for step, part_ref in enumerate(part_refs):
        lanes = pl.ds(pl.multiple_of(source(band, step, bands) * width, width), width)
        query_ref[:, :, lanes] = part_ref[...]
    used = term_rows(keys)
    parts = []
    for to_band in range(bands):
        lanes = slice(to_band * width, (to_band + 1) * width)
        part = jnp.zeros((used, width), jnp.float32)
        for sector in range(sectors):
            start = (to_band * sectors + sector) * used
            part = part + terms_ref[start : start + used, :]
        key_ref[:, lanes] = part[0:keys]
        value_ref[:, lanes] = part[keys : 2 * keys]
        parts.append(part[2 * keys : used])
    tap_sum = jnp.concatenate(parts, 1)
    mean = jnp.sum(tap_sum * tap_sum, keepdims=True) / (len(OFFSETS) * width * bands)
    taps_ref[...] = tap_sum / jnp.sqrt(mean + 1e-06)


def split_heads_body(queries, key_rows, value_rows, cotangent, conv_taps):
    rows, columns, channels = queries.shape
    bands = lax.axis_size("lat")
    sectors = lax.axis_size("lon")
    devices = bands * sectors
    keys = key_rows.shape[0]
    width = channels // bands
    lines = rows * bands

    sent_rows = block_rows(bands, keys, rows)
    part_shape = (2, rows, columns, width)
    anywhere = pl.BlockSpec(memory_space=pl.ANY)
    here = pl.BlockSpec(memory_space=pltpu.VMEM)
    row_blocks, *parts = pl.pallas_call(
        functools.partial(pack_kernel, bands, sectors, width, keys),
        out_shape=[
            jax.ShapeDtypeStruct(s, jnp.float32)
            for s in [(devices * sent_rows, width)] + [part_shape] * bands
        ],
        in_specs=[anywhere] * 4,
        out_specs=[anywhere] + [here] * bands,
        scratch_shapes=[
            pltpu.VMEM((keys, channels), jnp.float32),
            pltpu.VMEM((keys, channels), jnp.float32),
            pltpu.VMEM((rows, 1, channels), jnp.float32),
            pltpu.VMEM((rows, 1, channels), jnp.float32),
            pltpu.VMEM((devices * sent_rows, width), jnp.float32),
            pltpu.SemaphoreType.DMA((5 + 2 * bands,)),
        ],
        compiler_params=pltpu.CompilerParams(vmem_limit_bytes=VMEM_LIMIT),
    )(*[in_hbm(x) for x in (key_rows, value_rows, queries, cotangent)])
    row_blocks = to_all(row_blocks, devices)
    parts = exchange_all(parts, bands, ahead=True)

    grid = (lines, columns, width)
    heads = width // HD
    terms, *grad_parts = vmem_call(
        functools.partial(attention_kernel, bands, sectors, width, keys),
        [(devices * term_rows(keys), width)] + [(rows, columns, width)] * bands,
        [
            grid,
            (lines + 2, columns + 2 * SUBLANES, width),
            grid,
            grid,
        ],
    )(*parts, row_blocks, conv_taps)

    terms = to_all(terms, devices)
    grad_parts = exchange_all(grad_parts, bands, ahead=False)
    query_grad, key_grad, value_grad, tap_update = pl.pallas_call(
        functools.partial(finish_kernel, bands, sectors, width, keys),
        out_shape=[
            jax.ShapeDtypeStruct(s, jnp.float32)
            for s in (queries.shape, key_rows.shape, value_rows.shape, conv_taps.shape)
        ],
        compiler_params=pltpu.CompilerParams(vmem_limit_bytes=VMEM_LIMIT),
    )(*grad_parts, terms)
    return (query_grad, key_grad, value_grad, tap_update)


def extended(value, sides, width):
    for axis, dim in sides:
        peers, length = (lax.axis_size(axis), value.shape[dim])
        up = [(i, (i + 1) % peers) for i in range(peers)]
        down = [(j, i) for i, j in up]
        last = lax.slice_in_dim(value, length - width, length, axis=dim)
        initial = lax.slice_in_dim(value, 0, width, axis=dim)
        before = lax.ppermute(last, axis, up)
        after = lax.ppermute(initial, axis, down)
        value = jnp.concatenate([before, value, after], axis=dim)
    return value


def split_heads(matrix):
    return matrix.reshape(matrix.shape[0], -1, HD)


def latitude_weights(row_count, band_index, band_count):
    line_total = row_count * band_count
    centres = (jnp.arange(line_total, dtype=jnp.float32) + 0.5) * (jnp.pi / line_total)
    mean_cosine = jnp.sum(jnp.sin(centres)) / line_total
    mine = (band_index * row_count + jnp.arange(row_count, dtype=jnp.int32)).astype(jnp.float32)
    return jnp.sin((mine + 0.5) * (jnp.pi / line_total)) / mean_cosine


def close_poles(padded, row_dim, band_index, band_count):
    height = padded.shape[row_dim]
    positions = jnp.arange(height)
    outside = (positions == 0) & (band_index == 0) | (positions == height - 1) & (
        band_index == band_count - 1
    )
    shape_mask = [1] * padded.ndim
    shape_mask[row_dim] = height
    return jnp.where(outside.reshape(shape_mask), 0.0, padded)


def spread_taps(weighted, grad_padded, conv_taps):
    row_count, col_count = (weighted.shape[0], weighted.shape[1])
    result = weighted
    for tap_index, (shift_row, shift_col) in enumerate(OFFSETS):
        result = (
            result
            + conv_taps[tap_index]
            * grad_padded[
                1 - shift_row : 1 - shift_row + row_count, 1 - shift_col : 1 - shift_col + col_count
            ]
        )
    return result


def tap_terms(weighted, out_padded):
    row_count, col_count = (weighted.shape[0], weighted.shape[1])
    term_list = []
    for shift_row, shift_col in OFFSETS:
        term_list.append(
            jnp.sum(
                out_padded[
                    1 + shift_row : 1 + shift_row + row_count,
                    1 + shift_col : 1 + shift_col + col_count,
                ]
                * weighted,
                axis=(0, 1),
            )
        )
    return jnp.stack(term_list)


def group_logits(query_part, key_part):
    return jnp.einsum(
        "qhd,khd->hqk", split_heads(query_part), split_heads(key_part), precision=HIGH
    ) * HD ** (-0.5)


def whole_rows_body(queries, key_rows, value_rows, cotangent, conv_taps):
    row_count, col_count, channels = queries.shape
    band_count = lax.axis_size("lat")
    band_index = lax.axis_index("lat")
    weighted = cotangent * latitude_weights(row_count, band_index, band_count)[:, None, None]
    paired_rows = jnp.concatenate([key_rows, value_rows], 1)
    paired_all = lax.all_gather(paired_rows, ("lat", "lon"), axis=0, tiled=True)
    key_all = paired_all[:, :channels]
    value_all = paired_all[:, channels:]
    token_count = row_count * col_count
    key_count = key_all.shape[0]
    query_flat = queries.reshape(token_count, channels)
    group_width = 2 * HD
    group_count = channels // group_width
    outputs = []
    peaks = []
    sums_soft = []
    for group_index in range(group_count):
        col_start = group_index * group_width
        col_stop = col_start + group_width
        logits = group_logits(query_flat[:, col_start:col_stop], key_all[:, col_start:col_stop])
        row_peak = jnp.max(logits, -1, keepdims=True)
        raised = jnp.exp(logits - row_peak)
        normaliser = jnp.sum(raised, -1, keepdims=True)
        soft_weights = raised / normaliser
        outputs.append(
            jnp.einsum(
                "hqk,khd->qhd",
                soft_weights,
                split_heads(value_all[:, col_start:col_stop]),
                precision=HIGH,
            ).reshape(token_count, group_width)
        )
        peaks.append(row_peak)
        sums_soft.append(normaliser)
    out_flat = jnp.concatenate(outputs, 1)
    out_grid = out_flat.reshape(row_count, col_count, channels)
    both_padded = close_poles(
        extended(jnp.stack([weighted, out_grid]), (("lat", 1), ("lon", 2)), 1),
        1,
        band_index,
        band_count,
    )
    grad_padded = both_padded[0]
    out_padded = both_padded[1]
    out_grad = spread_taps(weighted, grad_padded, conv_taps)
    tap_sum = lax.psum(tap_terms(weighted, out_padded), ("lat", "lon"))
    tap_update = tap_sum / jnp.sqrt(jnp.mean(tap_sum * tap_sum) + 1e-06)
    grad_flat = out_grad.reshape(token_count, channels)
    query_parts = []
    key_parts = []
    value_parts = []
    for group_index in range(group_count):
        col_start = group_index * group_width
        col_stop = col_start + group_width
        query_heads = split_heads(query_flat[:, col_start:col_stop])
        key_heads = split_heads(key_all[:, col_start:col_stop])
        logits = jnp.einsum("qhd,khd->hqk", query_heads, key_heads, precision=HIGH) * HD ** (-0.5)
        soft_weights = jnp.exp(logits - peaks[group_index]) / sums_soft[group_index]
        grad_heads = split_heads(grad_flat[:, col_start:col_stop])
        value_parts.append(
            jnp.einsum("hqk,qhd->khd", soft_weights, grad_heads, precision=HIGH).reshape(
                key_count, group_width
            )
        )
        prob_grad = jnp.einsum(
            "qhd,khd->hqk",
            grad_heads,
            split_heads(value_all[:, col_start:col_stop]),
            precision=HIGH,
        )
        row_dot = jnp.transpose(
            jnp.sum(grad_heads * split_heads(out_flat[:, col_start:col_stop]), -1)
        )[:, :, None]
        logit_grad = soft_weights * (prob_grad - row_dot)
        query_parts.append(
            (
                jnp.einsum("hqk,khd->qhd", logit_grad, key_heads, precision=HIGH) * HD ** (-0.5)
            ).reshape(token_count, group_width)
        )
        key_parts.append(
            (
                jnp.einsum("hqk,qhd->khd", logit_grad, query_heads, precision=HIGH) * HD ** (-0.5)
            ).reshape(key_count, group_width)
        )
    paired_terms = jnp.concatenate(key_parts + value_parts, 1)
    paired_band = lax.psum_scatter(paired_terms, "lat", scatter_dimension=0, tiled=True)
    paired_grad = lax.psum_scatter(paired_band, "lon", scatter_dimension=0, tiled=True)
    key_grad = paired_grad[:, :channels]
    value_grad = paired_grad[:, channels:]
    query_grad = jnp.concatenate(query_parts, 1).reshape(row_count, col_count, channels)
    return (query_grad, key_grad, value_grad, tap_update)


def body(queries, key_rows, value_rows, cotangent, conv_taps):
    bands = lax.axis_size("lat")
    sectors = lax.axis_size("lon")
    rows, columns, channels = queries.shape
    whole_heads = channels % (bands * LANES) == 0
    whole_tiles = columns % SUBLANES == 0 and (rows * columns) % LANES == 0
    if whole_heads and whole_tiles and sectors > 2:
        return split_heads_body(queries, key_rows, value_rows, cotangent, conv_taps)
    return whole_rows_body(queries, key_rows, value_rows, cotangent, conv_taps)


def solution(mesh):
    placed = (
        P("lat", "lon", None),
        P(("lat", "lon"), None),
        P(("lat", "lon"), None),
        P("lat", "lon", None),
        P(),
    )
    return jax.shard_map(
        body,
        mesh=mesh,
        in_specs=placed,
        out_specs=(P("lat", "lon", None), P(("lat", "lon"), None), P(("lat", "lon"), None), P()),
        check_vma=False,
    )
```

```python
import functools

import jax
import jax.numpy as jnp
import numpy as np
from jax import lax
from jax.experimental import pallas as pl
from jax.experimental.pallas import tpu as pltpu
from jax.sharding import PartitionSpec as P

HD = 64
LANES = 128
SUBLANES = 8
VMEM_LIMIT = 16 * 1024 * 1024

HIGH = lax.Precision.HIGHEST
OFFSETS = ((-1, -1), (-1, 0), (-1, 1), (0, -1), (0, 0), (0, 1), (1, -1), (1, 0), (1, 1))


def partner(index, step, peers):
    if peers & (peers - 1) == 0:
        return index ^ step
    return lax.rem(index + step, peers) if not isinstance(index, int) else (index + step) % peers


def source(index, step, peers):
    return partner(index, step if peers & (peers - 1) == 0 else peers - step, peers)


def exchange(value, step, peers):
    return lax.ppermute(value, "lat", [(i, partner(i, step, peers)) for i in range(peers)])


def to_all(blocks, devices):
    rows, width = blocks.shape
    blocks = blocks.reshape(devices, rows // devices, 1, width)
    return lax.all_to_all(blocks, ("lat", "lon"), 0, 0, tiled=True).reshape(rows, width)


def row_weights(line_total):
    cosine = np.sin((np.arange(line_total, dtype=np.float64) + 0.5) * (np.pi / line_total))
    return [float(w) for w in cosine / np.mean(cosine)]


def vmem_call(kernel, out_shapes, scratch=()):
    return pl.pallas_call(
        kernel,
        out_shape=[jax.ShapeDtypeStruct(s, jnp.float32) for s in out_shapes],
        scratch_shapes=[pltpu.VMEM(s, jnp.float32) for s in scratch],
        compiler_params=pltpu.CompilerParams(vmem_limit_bytes=VMEM_LIMIT),
    )


def arrival_kernel(part_ref, out_ref):
    out_ref[...] = part_ref[...]


def exchange_all(parts, bands, ahead):
    last = exchange(parts[-1], bands - 1, bands)
    cost = pl.CostEstimate(flops=10**10, bytes_accessed=10**6, transcendentals=0)
    (last,) = pl.pallas_call(
        arrival_kernel,
        out_shape=[jax.ShapeDtypeStruct(last.shape, jnp.float32)],
        cost_estimate=cost if ahead else None,
        compiler_params=pltpu.CompilerParams(vmem_limit_bytes=VMEM_LIMIT),
    )(last)
    return [parts[0]] + [exchange(parts[s], s, bands) for s in range(1, bands - 1)] + [last]


def block_rows(bands, keys, rows):
    return 2 * keys + rows


def term_rows(keys):
    return 2 * keys + len(OFFSETS)


def in_hbm(array):
    return pltpu.with_memory_space_constraint(array, pltpu.HBM)


def pack_kernel(bands, sectors, width, keys, *refs):
    key_ref, value_ref, query_ref, cotangent_ref, sent_ref = refs[:5]
    part_refs = refs[5 : 5 + bands]
    key_own, value_own, first_own, last_own, block_ref, sems = refs[5 + bands :]
    band = lax.axis_index("lat")
    sector = lax.axis_index("lon")
    rows, columns = query_ref.shape[:2]
    sent = block_rows(bands, keys, rows)

    small = [
        pltpu.make_async_copy(source_ref, target_ref, sems.at[i])
        for i, (source_ref, target_ref) in enumerate(
            (
                (key_ref, key_own),
                (value_ref, value_own),
                (cotangent_ref.at[:, 0:1, :], first_own),
                (cotangent_ref.at[:, columns - 1 : columns, :], last_own),
            )
        )
    ]
    for copy in small:
        copy.start()
    large = []
    for step, part_ref in enumerate(part_refs):
        lanes = pl.ds(pl.multiple_of(partner(band, step, bands) * width, width), width)
        for i, array_ref in enumerate((query_ref, cotangent_ref)):
            large.append(
                pltpu.make_async_copy(
                    array_ref.at[:, :, lanes], part_ref.at[i], sems.at[len(small) + len(large)]
                )
            )
    for copy in large:
        copy.start()
    for copy in small:
        copy.wait()
    for to_band in range(bands):
        lanes = slice(to_band * width, (to_band + 1) * width)
        key = key_own[:, lanes]
        value = value_own[:, lanes]
        first = first_own[:, 0, lanes]
        last = last_own[:, 0, lanes]
        for to_sector in range(sectors):
            device = to_band * sectors + to_sector
            is_next = lax.rem(to_sector - sector + sectors, sectors) == 1
            start = device * sent
            block_ref[start : start + keys, :] = key
            start = start + keys
            block_ref[start : start + keys, :] = value
            block_ref[start + keys : start + keys + rows, :] = jnp.where(is_next, last, first)
    send = pltpu.make_async_copy(block_ref, sent_ref, sems.at[len(small) + len(large)])
    send.start()
    for copy in large:
        copy.wait()
    send.wait()


def heads_of(matrix, width):
    lane = lax.broadcasted_iota(jnp.int32, matrix.shape, 1)
    return jnp.concatenate(
        [
            jnp.where((lane >= h * HD) & (lane < (h + 1) * HD), matrix, 0.0)
            for h in range(width // HD)
        ],
        0,
    )


def own_heads(matrix, width, keys):
    lane = lax.broadcasted_iota(jnp.int32, (keys, width), 1)
    result = matrix[0:keys]
    for h in range(1, width // HD):
        result = jnp.where(lane >= h * HD, matrix[h * keys : (h + 1) * keys], result)
    return result


def rows_from_all(rows_ref, first, keys, devices, sent):
    return jnp.concatenate(
        [rows_ref[pl.ds(first + k, devices, stride=sent), :] for k in range(keys)], 0
    )


def dot(left, right, left_dim, right_dim):
    return lax.dot_general(
        left,
        right,
        (((left_dim,), (right_dim,)), ((), ())),
        preferred_element_type=jnp.float32,
    )


def split(value, terms):
    result = []
    for _ in range(terms):
        result.append(value.astype(jnp.bfloat16))
        value = value - result[-1].astype(jnp.float32)
    return result


def rows_by_tokens(rows, tokens):
    count = rows.shape[0]
    large, middle, small = split(rows, 3)
    token_large, token_middle, token_small = split(tokens, 3)
    left = jnp.concatenate(
        [
            jnp.concatenate([large, large], 1),
            jnp.concatenate([middle, middle], 1),
            jnp.concatenate([small, jnp.zeros_like(small)], 1),
        ],
        0,
    )
    main = dot(left, jnp.concatenate([token_large, token_middle], 1), 1, 1)
    rest = dot(large, token_small, 1, 1)
    return main[0:count] + (main[count : 2 * count] + (main[2 * count :] + rest))


def sum_over_tokens(left, right):
    count, width = left.shape[0], right.shape[1]
    every = dot(jnp.concatenate(split(left, 2), 0), jnp.concatenate(split(right, 2), 1), 1, 0)
    top, bottom = every[0:count], every[count:]
    return top[:, 0:width] + (top[:, width:] + bottom[:, 0:width] + bottom[:, width:])


def mix_rows(weights, rows):
    width = rows.shape[1]
    right = jnp.concatenate(split(rows, 2), 1)
    every = dot(jnp.concatenate(split(weights, 2), 0), jnp.concatenate([right, right], 0), 0, 0)
    return every[:, 0:width] + every[:, width:]


def mix_rows_exactly(weights, rows):
    width = rows.shape[1]
    large, middle, small = split(weights, 3)
    row_large, row_middle, row_small = split(rows, 3)
    zero = jnp.zeros_like(row_large)
    right = jnp.concatenate(
        [
            jnp.concatenate([row_large, row_large, row_large, zero], 0),
            jnp.concatenate([row_middle, row_middle, zero, row_small], 0),
        ],
        1,
    )
    every = dot(jnp.concatenate([large, middle, small, large], 0), right, 0, 0)
    return every[:, 0:width] + every[:, width:]


def attention_kernel(bands, sectors, width, keys, *refs):
    part_refs = refs[:bands]
    rows_ref, taps_ref, terms_ref = refs[bands : bands + 3]
    query_grad_refs = refs[bands + 3 : 2 * bands + 3]
    query_ref, weighted_ref, grad_ref, out_ref = refs[2 * bands + 3 :]
    band = lax.axis_index("lat")
    sector = lax.axis_index("lon")
    rows, columns = part_refs[0].shape[1:3]
    lines = rows * bands
    tokens = lines * columns
    edge = SUBLANES
    scale = HD ** (-0.5)
    weights = row_weights(lines)
    heads = width // HD
    devices = bands * sectors
    key_total = devices * keys
    sent = block_rows(bands, keys, rows)

    for step, part_ref in enumerate(part_refs):
        start = source(band, step, bands) * rows
        query_ref[pl.ds(start, rows)] = part_ref[0]
        weighted_ref[pl.ds(start + 1, rows), edge : edge + columns, :] = part_ref[1]
    before = lax.rem(sector + sectors - 1, sectors)
    after = lax.rem(sector + 1, sectors)
    for line in range(lines):
        b, r = divmod(line, rows)
        r = 2 * keys + r
        inner = weighted_ref[1 + line, edge : edge + columns, :]
        weighted_ref[1 + line, edge : edge + columns, :] = inner * weights[line]
        left = rows_ref[pl.ds((b * sectors + before) * sent + r, 1), :]
        right = rows_ref[pl.ds((b * sectors + after) * sent + r, 1), :]
        weighted_ref[1 + line, edge - 1 : edge, :] = left * weights[line]
        weighted_ref[1 + line, edge + columns : edge + columns + 1, :] = right * weights[line]
    zeros = jnp.zeros(weighted_ref.shape[1:], jnp.float32)
    weighted_ref[0] = zeros
    weighted_ref[lines + 1] = zeros

    own_lanes = pl.ds(pl.multiple_of(band * width, width), width)
    taps = [taps_ref[t : t + 1, own_lanes] for t in range(len(OFFSETS))]

    def shifted(line, offset):
        a, b = offset
        return weighted_ref[1 + line - a, edge - b : edge - b + columns, :]

    for line in range(lines):
        total = shifted(line, (0, 0))
        for tap, offset in zip(taps, OFFSETS):
            total = total + tap * shifted(line, offset)
        grad_ref[line] = total

    key_heads = heads_of(rows_from_all(rows_ref, 0, keys, devices, sent), width)
    value_heads = heads_of(rows_from_all(rows_ref, keys, keys, devices, sent), width)
    query = query_ref[...].reshape(tokens, width)
    grad = grad_ref[...].reshape(tokens, width)

    logits = rows_by_tokens(key_heads, query) * scale
    prob_list = []
    for h in range(heads):
        part = logits[h * key_total : (h + 1) * key_total]
        raised = jnp.exp(part - jnp.max(part, 0, keepdims=True))
        prob_list.append(raised / jnp.sum(raised, 0, keepdims=True))
    probs = jnp.concatenate(prob_list, 0)
    out_ref[...] = mix_rows(probs, value_heads).reshape(lines, columns, width)
    prob_grad = rows_by_tokens(value_heads, grad)
    logit_grad_list = []
    for h in range(heads):
        part = prob_grad[h * key_total : (h + 1) * key_total]
        row_dot = jnp.sum(prob_list[h] * part, 0, keepdims=True)
        logit_grad_list.append(prob_list[h] * (part - row_dot))
    logit_grad = jnp.concatenate(logit_grad_list, 0)

    key_grad = own_heads(sum_over_tokens(logit_grad, query), width, key_total) * scale
    value_grad = own_heads(sum_over_tokens(probs, grad), width, key_total)

    sums = [jnp.zeros((SUBLANES, width), jnp.float32) for _ in OFFSETS]
    for line in range(lines):
        out_line = out_ref[line]
        for t, offset in enumerate(OFFSETS):
            product = out_line * shifted(line, offset)
            for c in range(0, columns, SUBLANES):
                sums[t] = sums[t] + product[c : c + SUBLANES]
    tap_sum = jnp.concatenate([jnp.sum(s, 0, keepdims=True) for s in sums], 0)
    used = term_rows(keys)
    for k in range(keys):
        mine = slice(k * devices, (k + 1) * devices)
        terms_ref[pl.ds(k, devices, stride=used), :] = key_grad[mine]
        terms_ref[pl.ds(keys + k, devices, stride=used), :] = value_grad[mine]
    for device in range(devices):
        terms_ref[device * used + 2 * keys : (device + 1) * used, :] = tap_sum

    out_ref[...] = (mix_rows_exactly(logit_grad, key_heads) * scale).reshape(out_ref.shape)
    for step, part_ref in enumerate(query_grad_refs):
        part_ref[...] = out_ref[pl.ds(partner(band, step, bands) * rows, rows)]


def finish_kernel(bands, sectors, width, keys, *refs):
    part_refs = refs[:bands]
    terms_ref, query_ref, key_ref, value_ref, taps_ref = refs[bands:]
    band = lax.axis_index("lat")
    devices = bands * sectors
    rows, columns = query_ref.shape[:2]
    for step, part_ref in enumerate(part_refs):
        lanes = pl.ds(pl.multiple_of(source(band, step, bands) * width, width), width)
        query_ref[:, :, lanes] = part_ref[...]
    used = term_rows(keys)
    parts = []
    for to_band in range(bands):
        lanes = slice(to_band * width, (to_band + 1) * width)
        part = jnp.zeros((used, width), jnp.float32)
        for sector in range(sectors):
            start = (to_band * sectors + sector) * used
            part = part + terms_ref[start : start + used, :]
        key_ref[:, lanes] = part[0:keys]
        value_ref[:, lanes] = part[keys : 2 * keys]
        parts.append(part[2 * keys : used])
    tap_sum = jnp.concatenate(parts, 1)
    mean = jnp.sum(tap_sum * tap_sum, keepdims=True) / (len(OFFSETS) * width * bands)
    taps_ref[...] = tap_sum / jnp.sqrt(mean + 1e-06)


def split_heads_body(queries, key_rows, value_rows, cotangent, conv_taps):
    rows, columns, channels = queries.shape
    bands = lax.axis_size("lat")
    sectors = lax.axis_size("lon")
    devices = bands * sectors
    keys = key_rows.shape[0]
    width = channels // bands
    lines = rows * bands

    sent_rows = block_rows(bands, keys, rows)
    part_shape = (2, rows, columns, width)
    anywhere = pl.BlockSpec(memory_space=pl.ANY)
    here = pl.BlockSpec(memory_space=pltpu.VMEM)
    row_blocks, *parts = pl.pallas_call(
        functools.partial(pack_kernel, bands, sectors, width, keys),
        out_shape=[
            jax.ShapeDtypeStruct(s, jnp.float32)
            for s in [(devices * sent_rows, width)] + [part_shape] * bands
        ],
        in_specs=[anywhere] * 4,
        out_specs=[anywhere] + [here] * bands,
        scratch_shapes=[
            pltpu.VMEM((keys, channels), jnp.float32),
            pltpu.VMEM((keys, channels), jnp.float32),
            pltpu.VMEM((rows, 1, channels), jnp.float32),
            pltpu.VMEM((rows, 1, channels), jnp.float32),
            pltpu.VMEM((devices * sent_rows, width), jnp.float32),
            pltpu.SemaphoreType.DMA((5 + 2 * bands,)),
        ],
        compiler_params=pltpu.CompilerParams(vmem_limit_bytes=VMEM_LIMIT),
    )(*[in_hbm(x) for x in (key_rows, value_rows, queries, cotangent)])
    row_blocks = to_all(row_blocks, devices)
    parts = exchange_all(parts, bands, ahead=True)

    grid = (lines, columns, width)
    heads = width // HD
    terms, *grad_parts = vmem_call(
        functools.partial(attention_kernel, bands, sectors, width, keys),
        [(devices * term_rows(keys), width)] + [(rows, columns, width)] * bands,
        [
            grid,
            (lines + 2, columns + 2 * SUBLANES, width),
            grid,
            grid,
        ],
    )(*parts, row_blocks, conv_taps)

    terms = to_all(terms, devices)
    grad_parts = exchange_all(grad_parts, bands, ahead=False)
    query_grad, key_grad, value_grad, tap_update = pl.pallas_call(
        functools.partial(finish_kernel, bands, sectors, width, keys),
        out_shape=[
            jax.ShapeDtypeStruct(s, jnp.float32)
            for s in (queries.shape, key_rows.shape, value_rows.shape, conv_taps.shape)
        ],
        compiler_params=pltpu.CompilerParams(vmem_limit_bytes=VMEM_LIMIT),
    )(*grad_parts, terms)
    return (query_grad, key_grad, value_grad, tap_update)


def extended(value, sides, width):
    for axis, dim in sides:
        peers, length = (lax.axis_size(axis), value.shape[dim])
        up = [(i, (i + 1) % peers) for i in range(peers)]
        down = [(j, i) for i, j in up]
        last = lax.slice_in_dim(value, length - width, length, axis=dim)
        initial = lax.slice_in_dim(value, 0, width, axis=dim)
        before = lax.ppermute(last, axis, up)
        after = lax.ppermute(initial, axis, down)
        value = jnp.concatenate([before, value, after], axis=dim)
    return value


def split_heads(matrix):
    return matrix.reshape(matrix.shape[0], -1, HD)


def latitude_weights(row_count, band_index, band_count):
    line_total = row_count * band_count
    centres = (jnp.arange(line_total, dtype=jnp.float32) + 0.5) * (jnp.pi / line_total)
    mean_cosine = jnp.sum(jnp.sin(centres)) / line_total
    mine = (band_index * row_count + jnp.arange(row_count, dtype=jnp.int32)).astype(jnp.float32)
    return jnp.sin((mine + 0.5) * (jnp.pi / line_total)) / mean_cosine


def close_poles(padded, row_dim, band_index, band_count):
    height = padded.shape[row_dim]
    positions = jnp.arange(height)
    outside = (positions == 0) & (band_index == 0) | (positions == height - 1) & (
        band_index == band_count - 1
    )
    shape_mask = [1] * padded.ndim
    shape_mask[row_dim] = height
    return jnp.where(outside.reshape(shape_mask), 0.0, padded)


def spread_taps(weighted, grad_padded, conv_taps):
    row_count, col_count = (weighted.shape[0], weighted.shape[1])
    result = weighted
    for tap_index, (shift_row, shift_col) in enumerate(OFFSETS):
        result = (
            result
            + conv_taps[tap_index]
            * grad_padded[
                1 - shift_row : 1 - shift_row + row_count, 1 - shift_col : 1 - shift_col + col_count
            ]
        )
    return result


def tap_terms(weighted, out_padded):
    row_count, col_count = (weighted.shape[0], weighted.shape[1])
    term_list = []
    for shift_row, shift_col in OFFSETS:
        term_list.append(
            jnp.sum(
                out_padded[
                    1 + shift_row : 1 + shift_row + row_count,
                    1 + shift_col : 1 + shift_col + col_count,
                ]
                * weighted,
                axis=(0, 1),
            )
        )
    return jnp.stack(term_list)


def group_logits(query_part, key_part):
    return jnp.einsum(
        "qhd,khd->hqk", split_heads(query_part), split_heads(key_part), precision=HIGH
    ) * HD ** (-0.5)


def whole_rows_body(queries, key_rows, value_rows, cotangent, conv_taps):
    row_count, col_count, channels = queries.shape
    band_count = lax.axis_size("lat")
    band_index = lax.axis_index("lat")
    weighted = cotangent * latitude_weights(row_count, band_index, band_count)[:, None, None]
    paired_rows = jnp.concatenate([key_rows, value_rows], 1)
    paired_all = lax.all_gather(paired_rows, ("lat", "lon"), axis=0, tiled=True)
    key_all = paired_all[:, :channels]
    value_all = paired_all[:, channels:]
    token_count = row_count * col_count
    key_count = key_all.shape[0]
    query_flat = queries.reshape(token_count, channels)
    group_width = 2 * HD
    group_count = channels // group_width
    outputs = []
    peaks = []
    sums_soft = []
    for group_index in range(group_count):
        col_start = group_index * group_width
        col_stop = col_start + group_width
        logits = group_logits(query_flat[:, col_start:col_stop], key_all[:, col_start:col_stop])
        row_peak = jnp.max(logits, -1, keepdims=True)
        raised = jnp.exp(logits - row_peak)
        normaliser = jnp.sum(raised, -1, keepdims=True)
        soft_weights = raised / normaliser
        outputs.append(
            jnp.einsum(
                "hqk,khd->qhd",
                soft_weights,
                split_heads(value_all[:, col_start:col_stop]),
                precision=HIGH,
            ).reshape(token_count, group_width)
        )
        peaks.append(row_peak)
        sums_soft.append(normaliser)
    out_flat = jnp.concatenate(outputs, 1)
    out_grid = out_flat.reshape(row_count, col_count, channels)
    both_padded = close_poles(
        extended(jnp.stack([weighted, out_grid]), (("lat", 1), ("lon", 2)), 1),
        1,
        band_index,
        band_count,
    )
    grad_padded = both_padded[0]
    out_padded = both_padded[1]
    out_grad = spread_taps(weighted, grad_padded, conv_taps)
    tap_sum = lax.psum(tap_terms(weighted, out_padded), ("lat", "lon"))
    tap_update = tap_sum / jnp.sqrt(jnp.mean(tap_sum * tap_sum) + 1e-06)
    grad_flat = out_grad.reshape(token_count, channels)
    query_parts = []
    key_parts = []
    value_parts = []
    for group_index in range(group_count):
        col_start = group_index * group_width
        col_stop = col_start + group_width
        query_heads = split_heads(query_flat[:, col_start:col_stop])
        key_heads = split_heads(key_all[:, col_start:col_stop])
        logits = jnp.einsum("qhd,khd->hqk", query_heads, key_heads, precision=HIGH) * HD ** (-0.5)
        soft_weights = jnp.exp(logits - peaks[group_index]) / sums_soft[group_index]
        grad_heads = split_heads(grad_flat[:, col_start:col_stop])
        value_parts.append(
            jnp.einsum("hqk,qhd->khd", soft_weights, grad_heads, precision=HIGH).reshape(
                key_count, group_width
            )
        )
        prob_grad = jnp.einsum(
            "qhd,khd->hqk",
            grad_heads,
            split_heads(value_all[:, col_start:col_stop]),
            precision=HIGH,
        )
        row_dot = jnp.transpose(
            jnp.sum(grad_heads * split_heads(out_flat[:, col_start:col_stop]), -1)
        )[:, :, None]
        logit_grad = soft_weights * (prob_grad - row_dot)
        query_parts.append(
            (
                jnp.einsum("hqk,khd->qhd", logit_grad, key_heads, precision=HIGH) * HD ** (-0.5)
            ).reshape(token_count, group_width)
        )
        key_parts.append(
            (
                jnp.einsum("hqk,qhd->khd", logit_grad, query_heads, precision=HIGH) * HD ** (-0.5)
            ).reshape(key_count, group_width)
        )
    paired_terms = jnp.concatenate(key_parts + value_parts, 1)
    paired_band = lax.psum_scatter(paired_terms, "lat", scatter_dimension=0, tiled=True)
    paired_grad = lax.psum_scatter(paired_band, "lon", scatter_dimension=0, tiled=True)
    key_grad = paired_grad[:, :channels]
    value_grad = paired_grad[:, channels:]
    query_grad = jnp.concatenate(query_parts, 1).reshape(row_count, col_count, channels)
    return (query_grad, key_grad, value_grad, tap_update)


def body(queries, key_rows, value_rows, cotangent, conv_taps):
    bands = lax.axis_size("lat")
    sectors = lax.axis_size("lon")
    rows, columns, channels = queries.shape
    whole_heads = channels % (bands * LANES) == 0
    whole_tiles = columns % SUBLANES == 0 and (rows * columns) % LANES == 0
    if whole_heads and whole_tiles and sectors > 2:
        return split_heads_body(queries, key_rows, value_rows, cotangent, conv_taps)
    return whole_rows_body(queries, key_rows, value_rows, cotangent, conv_taps)


def solution(mesh):
    placed = (
        P("lat", "lon", None),
        P(("lat", "lon"), None),
        P(("lat", "lon"), None),
        P("lat", "lon", None),
        P(),
    )
    return jax.shard_map(
        body,
        mesh=mesh,
        in_specs=placed,
        out_specs=(P("lat", "lon", None), P(("lat", "lon"), None), P(("lat", "lon"), None), P()),
        check_vma=False,
    )
```

```python
import functools

import jax
import jax.numpy as jnp
import numpy as np
from jax import lax
from jax.experimental import pallas as pl
from jax.experimental.pallas import tpu as pltpu
from jax.sharding import PartitionSpec as P

HD = 64
LANES = 128
SUBLANES = 8
VMEM_LIMIT = 16 * 1024 * 1024

HIGH = lax.Precision.HIGHEST
OFFSETS = ((-1, -1), (-1, 0), (-1, 1), (0, -1), (0, 0), (0, 1), (1, -1), (1, 0), (1, 1))


def partner(index, step, peers):
    if peers & (peers - 1) == 0:
        return index ^ step
    return lax.rem(index + step, peers) if not isinstance(index, int) else (index + step) % peers


def source(index, step, peers):
    return partner(index, step if peers & (peers - 1) == 0 else peers - step, peers)


def exchange(value, step, peers):
    return lax.ppermute(value, "lat", [(i, partner(i, step, peers)) for i in range(peers)])


def to_all(blocks, devices):
    rows, width = blocks.shape
    blocks = blocks.reshape(devices, rows // devices, 1, width)
    return lax.all_to_all(blocks, ("lat", "lon"), 0, 0, tiled=True).reshape(rows, width)


def row_weights(line_total):
    cosine = np.sin((np.arange(line_total, dtype=np.float64) + 0.5) * (np.pi / line_total))
    return [float(w) for w in cosine / np.mean(cosine)]


def vmem_call(kernel, out_shapes, scratch=()):
    return pl.pallas_call(
        kernel,
        out_shape=[jax.ShapeDtypeStruct(s, jnp.float32) for s in out_shapes],
        scratch_shapes=[pltpu.VMEM(s, jnp.float32) for s in scratch],
        compiler_params=pltpu.CompilerParams(vmem_limit_bytes=VMEM_LIMIT),
    )


def arrival_kernel(part_ref, out_ref):
    out_ref[...] = part_ref[...]


def exchange_all(parts, bands, ahead):
    last = exchange(parts[-1], bands - 1, bands)
    cost = pl.CostEstimate(flops=10**10, bytes_accessed=10**6, transcendentals=0)
    (last,) = pl.pallas_call(
        arrival_kernel,
        out_shape=[jax.ShapeDtypeStruct(last.shape, jnp.float32)],
        cost_estimate=cost if ahead else None,
        compiler_params=pltpu.CompilerParams(vmem_limit_bytes=VMEM_LIMIT),
    )(last)
    return [parts[0]] + [exchange(parts[s], s, bands) for s in range(1, bands - 1)] + [last]


def block_rows(bands, keys, rows):
    return 2 * keys + rows


def term_rows(keys):
    return 2 * keys + len(OFFSETS)


def in_hbm(array):
    return pltpu.with_memory_space_constraint(array, pltpu.HBM)


def pack_kernel(bands, sectors, width, keys, *refs):
    key_ref, value_ref, query_ref, cotangent_ref, sent_ref = refs[:5]
    part_refs = refs[5 : 5 + bands]
    key_own, value_own, first_own, last_own, block_ref, sems = refs[5 + bands :]
    band = lax.axis_index("lat")
    sector = lax.axis_index("lon")
    rows, columns = query_ref.shape[:2]
    sent = block_rows(bands, keys, rows)

    small = [
        pltpu.make_async_copy(source_ref, target_ref, sems.at[i])
        for i, (source_ref, target_ref) in enumerate(
            (
                (key_ref, key_own),
                (value_ref, value_own),
                (cotangent_ref.at[:, 0:1, :], first_own),
                (cotangent_ref.at[:, columns - 1 : columns, :], last_own),
            )
        )
    ]
    for copy in small:
        copy.start()
    large = []
    for step, part_ref in enumerate(part_refs):
        lanes = pl.ds(pl.multiple_of(partner(band, step, bands) * width, width), width)
        for i, array_ref in enumerate((query_ref, cotangent_ref)):
            large.append(
                pltpu.make_async_copy(
                    array_ref.at[:, :, lanes], part_ref.at[i], sems.at[len(small) + len(large)]
                )
            )
    for copy in large:
        copy.start()
    for copy in small:
        copy.wait()
    sends = []
    for to_band in range(bands):
        lanes = slice(to_band * width, (to_band + 1) * width)
        key = key_own[:, lanes]
        value = value_own[:, lanes]
        first = first_own[:, 0, lanes]
        last = last_own[:, 0, lanes]
        for to_sector in range(sectors):
            device = to_band * sectors + to_sector
            is_next = lax.rem(to_sector - sector + sectors, sectors) == 1
            start = device * sent
            block_ref[start : start + keys, :] = key
            start = start + keys
            block_ref[start : start + keys, :] = value
            block_ref[start + keys : start + keys + rows, :] = jnp.where(is_next, last, first)
        group = pl.ds(to_band * sectors * sent, sectors * sent)
        sends.append(
            pltpu.make_async_copy(
                block_ref.at[group],
                sent_ref.at[group],
                sems.at[len(small) + len(large) + to_band],
            )
        )
        sends[-1].start()
    for copy in large + sends:
        copy.wait()


def heads_of(matrix, width):
    lane = lax.broadcasted_iota(jnp.int32, matrix.shape, 1)
    return jnp.concatenate(
        [
            jnp.where((lane >= h * HD) & (lane < (h + 1) * HD), matrix, 0.0)
            for h in range(width // HD)
        ],
        0,
    )


def own_heads(matrix, width, keys):
    lane = lax.broadcasted_iota(jnp.int32, (keys, width), 1)
    result = matrix[0:keys]
    for h in range(1, width // HD):
        result = jnp.where(lane >= h * HD, matrix[h * keys : (h + 1) * keys], result)
    return result


def rows_from_all(rows_ref, first, keys, devices, sent):
    return jnp.concatenate(
        [rows_ref[pl.ds(first + k, devices, stride=sent), :] for k in range(keys)], 0
    )


def dot(left, right, left_dim, right_dim):
    return lax.dot_general(
        left,
        right,
        (((left_dim,), (right_dim,)), ((), ())),
        preferred_element_type=jnp.float32,
    )


def split(value, terms):
    result = []
    for _ in range(terms):
        result.append(value.astype(jnp.bfloat16))
        value = value - result[-1].astype(jnp.float32)
    return result


def rows_by_tokens(rows, tokens):
    count = rows.shape[0]
    large, middle, small = split(rows, 3)
    token_large, token_middle, token_small = split(tokens, 3)
    left = jnp.concatenate(
        [
            jnp.concatenate([large, large], 1),
            jnp.concatenate([middle, middle], 1),
            jnp.concatenate([small, jnp.zeros_like(small)], 1),
        ],
        0,
    )
    main = dot(left, jnp.concatenate([token_large, token_middle], 1), 1, 1)
    rest = dot(large, token_small, 1, 1)
    return main[0:count] + (main[count : 2 * count] + (main[2 * count :] + rest))


def sum_over_tokens(left, right):
    count, width = left.shape[0], right.shape[1]
    every = dot(jnp.concatenate(split(left, 2), 0), jnp.concatenate(split(right, 2), 1), 1, 0)
    top, bottom = every[0:count], every[count:]
    return top[:, 0:width] + (top[:, width:] + bottom[:, 0:width] + bottom[:, width:])


def mix_rows(weights, rows):
    width = rows.shape[1]
    right = jnp.concatenate(split(rows, 2), 1)
    every = dot(jnp.concatenate(split(weights, 2), 0), jnp.concatenate([right, right], 0), 0, 0)
    return every[:, 0:width] + every[:, width:]


def mix_rows_exactly(weights, rows):
    width = rows.shape[1]
    large, middle, small = split(weights, 3)
    row_large, row_middle, row_small = split(rows, 3)
    zero = jnp.zeros_like(row_large)
    right = jnp.concatenate(
        [
            jnp.concatenate([row_large, row_large, row_large, zero], 0),
            jnp.concatenate([row_middle, row_middle, zero, row_small], 0),
        ],
        1,
    )
    every = dot(jnp.concatenate([large, middle, small, large], 0), right, 0, 0)
    return every[:, 0:width] + every[:, width:]


def attention_kernel(bands, sectors, width, keys, *refs):
    part_refs = refs[:bands]
    rows_ref, taps_ref, terms_ref = refs[bands : bands + 3]
    query_grad_refs = refs[bands + 3 : 2 * bands + 3]
    query_ref, weighted_ref, grad_ref, out_ref = refs[2 * bands + 3 :]
    band = lax.axis_index("lat")
    sector = lax.axis_index("lon")
    rows, columns = part_refs[0].shape[1:3]
    lines = rows * bands
    tokens = lines * columns
    edge = SUBLANES
    scale = HD ** (-0.5)
    weights = row_weights(lines)
    heads = width // HD
    devices = bands * sectors
    key_total = devices * keys
    sent = block_rows(bands, keys, rows)

    for step, part_ref in enumerate(part_refs):
        start = source(band, step, bands) * rows
        query_ref[pl.ds(start, rows)] = part_ref[0]
        weighted_ref[pl.ds(start + 1, rows), edge : edge + columns, :] = part_ref[1]
    before = lax.rem(sector + sectors - 1, sectors)
    after = lax.rem(sector + 1, sectors)
    for line in range(lines):
        b, r = divmod(line, rows)
        r = 2 * keys + r
        inner = weighted_ref[1 + line, edge : edge + columns, :]
        weighted_ref[1 + line, edge : edge + columns, :] = inner * weights[line]
        left = rows_ref[pl.ds((b * sectors + before) * sent + r, 1), :]
        right = rows_ref[pl.ds((b * sectors + after) * sent + r, 1), :]
        weighted_ref[1 + line, edge - 1 : edge, :] = left * weights[line]
        weighted_ref[1 + line, edge + columns : edge + columns + 1, :] = right * weights[line]
    zeros = jnp.zeros(weighted_ref.shape[1:], jnp.float32)
    weighted_ref[0] = zeros
    weighted_ref[lines + 1] = zeros

    own_lanes = pl.ds(pl.multiple_of(band * width, width), width)
    taps = [taps_ref[t : t + 1, own_lanes] for t in range(len(OFFSETS))]

    def shifted(line, offset):
        a, b = offset
        return weighted_ref[1 + line - a, edge - b : edge - b + columns, :]

    for line in range(lines):
        total = shifted(line, (0, 0))
        for tap, offset in zip(taps, OFFSETS):
            total = total + tap * shifted(line, offset)
        grad_ref[line] = total

    key_heads = heads_of(rows_from_all(rows_ref, 0, keys, devices, sent), width)
    value_heads = heads_of(rows_from_all(rows_ref, keys, keys, devices, sent), width)
    query = query_ref[...].reshape(tokens, width)
    grad = grad_ref[...].reshape(tokens, width)

    logits = rows_by_tokens(key_heads, query) * scale
    prob_list = []
    for h in range(heads):
        part = logits[h * key_total : (h + 1) * key_total]
        raised = jnp.exp(part - jnp.max(part, 0, keepdims=True))
        prob_list.append(raised / jnp.sum(raised, 0, keepdims=True))
    probs = jnp.concatenate(prob_list, 0)
    out_ref[...] = mix_rows(probs, value_heads).reshape(lines, columns, width)
    prob_grad = rows_by_tokens(value_heads, grad)
    logit_grad_list = []
    for h in range(heads):
        part = prob_grad[h * key_total : (h + 1) * key_total]
        row_dot = jnp.sum(prob_list[h] * part, 0, keepdims=True)
        logit_grad_list.append(prob_list[h] * (part - row_dot))
    logit_grad = jnp.concatenate(logit_grad_list, 0)

    key_grad = own_heads(sum_over_tokens(logit_grad, query), width, key_total) * scale
    value_grad = own_heads(sum_over_tokens(probs, grad), width, key_total)

    sums = [jnp.zeros((SUBLANES, width), jnp.float32) for _ in OFFSETS]
    for line in range(lines):
        out_line = out_ref[line]
        for t, offset in enumerate(OFFSETS):
            product = out_line * shifted(line, offset)
            for c in range(0, columns, SUBLANES):
                sums[t] = sums[t] + product[c : c + SUBLANES]
    tap_sum = jnp.concatenate([jnp.sum(s, 0, keepdims=True) for s in sums], 0)
    used = term_rows(keys)
    for k in range(keys):
        mine = slice(k * devices, (k + 1) * devices)
        terms_ref[pl.ds(k, devices, stride=used), :] = key_grad[mine]
        terms_ref[pl.ds(keys + k, devices, stride=used), :] = value_grad[mine]
    for device in range(devices):
        terms_ref[device * used + 2 * keys : (device + 1) * used, :] = tap_sum

    out_ref[...] = (mix_rows_exactly(logit_grad, key_heads) * scale).reshape(out_ref.shape)
    for step, part_ref in enumerate(query_grad_refs):
        part_ref[...] = out_ref[pl.ds(partner(band, step, bands) * rows, rows)]


def finish_kernel(bands, sectors, width, keys, *refs):
    part_refs = refs[:bands]
    terms_ref, query_ref, key_ref, value_ref, taps_ref = refs[bands:]
    band = lax.axis_index("lat")
    devices = bands * sectors
    rows, columns = query_ref.shape[:2]
    for step, part_ref in enumerate(part_refs):
        lanes = pl.ds(pl.multiple_of(source(band, step, bands) * width, width), width)
        query_ref[:, :, lanes] = part_ref[...]
    used = term_rows(keys)
    parts = []
    for to_band in range(bands):
        lanes = slice(to_band * width, (to_band + 1) * width)
        part = jnp.zeros((used, width), jnp.float32)
        for sector in range(sectors):
            start = (to_band * sectors + sector) * used
            part = part + terms_ref[start : start + used, :]
        key_ref[:, lanes] = part[0:keys]
        value_ref[:, lanes] = part[keys : 2 * keys]
        parts.append(part[2 * keys : used])
    tap_sum = jnp.concatenate(parts, 1)
    mean = jnp.sum(tap_sum * tap_sum, keepdims=True) / (len(OFFSETS) * width * bands)
    taps_ref[...] = tap_sum / jnp.sqrt(mean + 1e-06)


def split_heads_body(queries, key_rows, value_rows, cotangent, conv_taps):
    rows, columns, channels = queries.shape
    bands = lax.axis_size("lat")
    sectors = lax.axis_size("lon")
    devices = bands * sectors
    keys = key_rows.shape[0]
    width = channels // bands
    lines = rows * bands

    sent_rows = block_rows(bands, keys, rows)
    part_shape = (2, rows, columns, width)
    anywhere = pl.BlockSpec(memory_space=pl.ANY)
    here = pl.BlockSpec(memory_space=pltpu.VMEM)
    row_blocks, *parts = pl.pallas_call(
        functools.partial(pack_kernel, bands, sectors, width, keys),
        out_shape=[
            jax.ShapeDtypeStruct(s, jnp.float32)
            for s in [(devices * sent_rows, width)] + [part_shape] * bands
        ],
        in_specs=[anywhere] * 4,
        out_specs=[anywhere] + [here] * bands,
        scratch_shapes=[
            pltpu.VMEM((keys, channels), jnp.float32),
            pltpu.VMEM((keys, channels), jnp.float32),
            pltpu.VMEM((rows, 1, channels), jnp.float32),
            pltpu.VMEM((rows, 1, channels), jnp.float32),
            pltpu.VMEM((devices * sent_rows, width), jnp.float32),
            pltpu.SemaphoreType.DMA((4 + 3 * bands,)),
        ],
        compiler_params=pltpu.CompilerParams(vmem_limit_bytes=VMEM_LIMIT),
    )(*[in_hbm(x) for x in (key_rows, value_rows, queries, cotangent)])
    row_blocks = to_all(row_blocks, devices)
    parts = exchange_all(parts, bands, ahead=True)

    grid = (lines, columns, width)
    heads = width // HD
    terms, *grad_parts = vmem_call(
        functools.partial(attention_kernel, bands, sectors, width, keys),
        [(devices * term_rows(keys), width)] + [(rows, columns, width)] * bands,
        [
            grid,
            (lines + 2, columns + 2 * SUBLANES, width),
            grid,
            grid,
        ],
    )(*parts, row_blocks, conv_taps)

    terms = to_all(terms, devices)
    grad_parts = exchange_all(grad_parts, bands, ahead=False)
    query_grad, key_grad, value_grad, tap_update = pl.pallas_call(
        functools.partial(finish_kernel, bands, sectors, width, keys),
        out_shape=[
            jax.ShapeDtypeStruct(s, jnp.float32)
            for s in (queries.shape, key_rows.shape, value_rows.shape, conv_taps.shape)
        ],
        compiler_params=pltpu.CompilerParams(vmem_limit_bytes=VMEM_LIMIT),
    )(*grad_parts, terms)
    return (query_grad, key_grad, value_grad, tap_update)


def extended(value, sides, width):
    for axis, dim in sides:
        peers, length = (lax.axis_size(axis), value.shape[dim])
        up = [(i, (i + 1) % peers) for i in range(peers)]
        down = [(j, i) for i, j in up]
        last = lax.slice_in_dim(value, length - width, length, axis=dim)
        initial = lax.slice_in_dim(value, 0, width, axis=dim)
        before = lax.ppermute(last, axis, up)
        after = lax.ppermute(initial, axis, down)
        value = jnp.concatenate([before, value, after], axis=dim)
    return value


def split_heads(matrix):
    return matrix.reshape(matrix.shape[0], -1, HD)


def latitude_weights(row_count, band_index, band_count):
    line_total = row_count * band_count
    centres = (jnp.arange(line_total, dtype=jnp.float32) + 0.5) * (jnp.pi / line_total)
    mean_cosine = jnp.sum(jnp.sin(centres)) / line_total
    mine = (band_index * row_count + jnp.arange(row_count, dtype=jnp.int32)).astype(jnp.float32)
    return jnp.sin((mine + 0.5) * (jnp.pi / line_total)) / mean_cosine


def close_poles(padded, row_dim, band_index, band_count):
    height = padded.shape[row_dim]
    positions = jnp.arange(height)
    outside = (positions == 0) & (band_index == 0) | (positions == height - 1) & (
        band_index == band_count - 1
    )
    shape_mask = [1] * padded.ndim
    shape_mask[row_dim] = height
    return jnp.where(outside.reshape(shape_mask), 0.0, padded)


def spread_taps(weighted, grad_padded, conv_taps):
    row_count, col_count = (weighted.shape[0], weighted.shape[1])
    result = weighted
    for tap_index, (shift_row, shift_col) in enumerate(OFFSETS):
        result = (
            result
            + conv_taps[tap_index]
            * grad_padded[
                1 - shift_row : 1 - shift_row + row_count, 1 - shift_col : 1 - shift_col + col_count
            ]
        )
    return result


def tap_terms(weighted, out_padded):
    row_count, col_count = (weighted.shape[0], weighted.shape[1])
    term_list = []
    for shift_row, shift_col in OFFSETS:
        term_list.append(
            jnp.sum(
                out_padded[
                    1 + shift_row : 1 + shift_row + row_count,
                    1 + shift_col : 1 + shift_col + col_count,
                ]
                * weighted,
                axis=(0, 1),
            )
        )
    return jnp.stack(term_list)


def group_logits(query_part, key_part):
    return jnp.einsum(
        "qhd,khd->hqk", split_heads(query_part), split_heads(key_part), precision=HIGH
    ) * HD ** (-0.5)


def whole_rows_body(queries, key_rows, value_rows, cotangent, conv_taps):
    row_count, col_count, channels = queries.shape
    band_count = lax.axis_size("lat")
    band_index = lax.axis_index("lat")
    weighted = cotangent * latitude_weights(row_count, band_index, band_count)[:, None, None]
    paired_rows = jnp.concatenate([key_rows, value_rows], 1)
    paired_all = lax.all_gather(paired_rows, ("lat", "lon"), axis=0, tiled=True)
    key_all = paired_all[:, :channels]
    value_all = paired_all[:, channels:]
    token_count = row_count * col_count
    key_count = key_all.shape[0]
    query_flat = queries.reshape(token_count, channels)
    group_width = 2 * HD
    group_count = channels // group_width
    outputs = []
    peaks = []
    sums_soft = []
    for group_index in range(group_count):
        col_start = group_index * group_width
        col_stop = col_start + group_width
        logits = group_logits(query_flat[:, col_start:col_stop], key_all[:, col_start:col_stop])
        row_peak = jnp.max(logits, -1, keepdims=True)
        raised = jnp.exp(logits - row_peak)
        normaliser = jnp.sum(raised, -1, keepdims=True)
        soft_weights = raised / normaliser
        outputs.append(
            jnp.einsum(
                "hqk,khd->qhd",
                soft_weights,
                split_heads(value_all[:, col_start:col_stop]),
                precision=HIGH,
            ).reshape(token_count, group_width)
        )
        peaks.append(row_peak)
        sums_soft.append(normaliser)
    out_flat = jnp.concatenate(outputs, 1)
    out_grid = out_flat.reshape(row_count, col_count, channels)
    both_padded = close_poles(
        extended(jnp.stack([weighted, out_grid]), (("lat", 1), ("lon", 2)), 1),
        1,
        band_index,
        band_count,
    )
    grad_padded = both_padded[0]
    out_padded = both_padded[1]
    out_grad = spread_taps(weighted, grad_padded, conv_taps)
    tap_sum = lax.psum(tap_terms(weighted, out_padded), ("lat", "lon"))
    tap_update = tap_sum / jnp.sqrt(jnp.mean(tap_sum * tap_sum) + 1e-06)
    grad_flat = out_grad.reshape(token_count, channels)
    query_parts = []
    key_parts = []
    value_parts = []
    for group_index in range(group_count):
        col_start = group_index * group_width
        col_stop = col_start + group_width
        query_heads = split_heads(query_flat[:, col_start:col_stop])
        key_heads = split_heads(key_all[:, col_start:col_stop])
        logits = jnp.einsum("qhd,khd->hqk", query_heads, key_heads, precision=HIGH) * HD ** (-0.5)
        soft_weights = jnp.exp(logits - peaks[group_index]) / sums_soft[group_index]
        grad_heads = split_heads(grad_flat[:, col_start:col_stop])
        value_parts.append(
            jnp.einsum("hqk,qhd->khd", soft_weights, grad_heads, precision=HIGH).reshape(
                key_count, group_width
            )
        )
        prob_grad = jnp.einsum(
            "qhd,khd->hqk",
            grad_heads,
            split_heads(value_all[:, col_start:col_stop]),
            precision=HIGH,
        )
        row_dot = jnp.transpose(
            jnp.sum(grad_heads * split_heads(out_flat[:, col_start:col_stop]), -1)
        )[:, :, None]
        logit_grad = soft_weights * (prob_grad - row_dot)
        query_parts.append(
            (
                jnp.einsum("hqk,khd->qhd", logit_grad, key_heads, precision=HIGH) * HD ** (-0.5)
            ).reshape(token_count, group_width)
        )
        key_parts.append(
            (
                jnp.einsum("hqk,qhd->khd", logit_grad, query_heads, precision=HIGH) * HD ** (-0.5)
            ).reshape(key_count, group_width)
        )
    paired_terms = jnp.concatenate(key_parts + value_parts, 1)
    paired_band = lax.psum_scatter(paired_terms, "lat", scatter_dimension=0, tiled=True)
    paired_grad = lax.psum_scatter(paired_band, "lon", scatter_dimension=0, tiled=True)
    key_grad = paired_grad[:, :channels]
    value_grad = paired_grad[:, channels:]
    query_grad = jnp.concatenate(query_parts, 1).reshape(row_count, col_count, channels)
    return (query_grad, key_grad, value_grad, tap_update)


def body(queries, key_rows, value_rows, cotangent, conv_taps):
    bands = lax.axis_size("lat")
    sectors = lax.axis_size("lon")
    rows, columns, channels = queries.shape
    whole_heads = channels % (bands * LANES) == 0
    whole_tiles = columns % SUBLANES == 0 and (rows * columns) % LANES == 0
    if whole_heads and whole_tiles and sectors > 2:
        return split_heads_body(queries, key_rows, value_rows, cotangent, conv_taps)
    return whole_rows_body(queries, key_rows, value_rows, cotangent, conv_taps)


def solution(mesh):
    placed = (
        P("lat", "lon", None),
        P(("lat", "lon"), None),
        P(("lat", "lon"), None),
        P("lat", "lon", None),
        P(),
    )
    return jax.shard_map(
        body,
        mesh=mesh,
        in_specs=placed,
        out_specs=(P("lat", "lon", None), P(("lat", "lon"), None), P(("lat", "lon"), None), P()),
        check_vma=False,
    )
```

```python
import functools

import jax
import jax.numpy as jnp
import numpy as np
from jax import lax
from jax.experimental import pallas as pl
from jax.experimental.pallas import tpu as pltpu
from jax.sharding import PartitionSpec as P

HD = 64
LANES = 128
SUBLANES = 8
VMEM_LIMIT = 16 * 1024 * 1024

HIGH = lax.Precision.HIGHEST
OFFSETS = ((-1, -1), (-1, 0), (-1, 1), (0, -1), (0, 0), (0, 1), (1, -1), (1, 0), (1, 1))


def partner(index, step, peers):
    if peers & (peers - 1) == 0:
        return index ^ step
    return lax.rem(index + step, peers) if not isinstance(index, int) else (index + step) % peers


def source(index, step, peers):
    return partner(index, step if peers & (peers - 1) == 0 else peers - step, peers)


def exchange(value, step, peers):
    return lax.ppermute(value, "lat", [(i, partner(i, step, peers)) for i in range(peers)])


def to_all(blocks, devices):
    rows, width = blocks.shape
    blocks = blocks.reshape(devices, rows // devices, 1, width)
    return lax.all_to_all(blocks, ("lat", "lon"), 0, 0, tiled=True).reshape(rows, width)


def row_weights(line_total):
    cosine = np.sin((np.arange(line_total, dtype=np.float64) + 0.5) * (np.pi / line_total))
    return [float(w) for w in cosine / np.mean(cosine)]


def vmem_call(kernel, out_shapes, scratch=()):
    return pl.pallas_call(
        kernel,
        out_shape=[jax.ShapeDtypeStruct(s, jnp.float32) for s in out_shapes],
        scratch_shapes=[pltpu.VMEM(s, jnp.float32) for s in scratch],
        compiler_params=pltpu.CompilerParams(vmem_limit_bytes=VMEM_LIMIT),
    )


def arrival_kernel(part_ref, out_ref):
    out_ref[...] = part_ref[...]


def exchange_all(parts, bands, ahead):
    last = exchange(parts[-1], bands - 1, bands)
    cost = pl.CostEstimate(flops=10**10, bytes_accessed=10**6, transcendentals=0)
    (last,) = pl.pallas_call(
        arrival_kernel,
        out_shape=[jax.ShapeDtypeStruct(last.shape, jnp.float32)],
        cost_estimate=cost if ahead else None,
        compiler_params=pltpu.CompilerParams(vmem_limit_bytes=VMEM_LIMIT),
    )(last)
    return [parts[0]] + [exchange(parts[s], s, bands) for s in range(1, bands - 1)] + [last]


def block_rows(bands, keys, rows):
    return 2 * keys + rows


def term_rows(keys):
    return 2 * keys + len(OFFSETS)


def in_hbm(array):
    return pltpu.with_memory_space_constraint(array, pltpu.HBM)


def pack_kernel(bands, sectors, width, keys, *refs):
    key_ref, value_ref, query_ref, cotangent_ref, sent_ref = refs[:5]
    part_refs = refs[5 : 5 + bands]
    key_own, value_own, first_own, last_own, block_ref, sems = refs[5 + bands :]
    band = lax.axis_index("lat")
    sector = lax.axis_index("lon")
    rows, columns = query_ref.shape[:2]
    sent = block_rows(bands, keys, rows)

    small = [
        pltpu.make_async_copy(source_ref, target_ref, sems.at[i])
        for i, (source_ref, target_ref) in enumerate(
            (
                (key_ref, key_own),
                (value_ref, value_own),
                (cotangent_ref.at[:, 0:1, :], first_own),
                (cotangent_ref.at[:, columns - 1 : columns, :], last_own),
            )
        )
    ]
    for copy in small:
        copy.start()
    large = []
    for step, part_ref in enumerate(part_refs):
        lanes = pl.ds(pl.multiple_of(partner(band, step, bands) * width, width), width)
        for i, array_ref in enumerate((query_ref, cotangent_ref)):
            large.append(
                pltpu.make_async_copy(
                    array_ref.at[:, :, lanes], part_ref.at[i], sems.at[len(small) + len(large)]
                )
            )
    for copy in large:
        copy.start()
    for copy in small:
        copy.wait()
    sends = []
    for to_band in range(bands):
        lanes = slice(to_band * width, (to_band + 1) * width)
        key = key_own[:, lanes]
        value = value_own[:, lanes]
        first = first_own[:, 0, lanes]
        last = last_own[:, 0, lanes]
        for to_sector in range(sectors):
            device = to_band * sectors + to_sector
            is_next = lax.rem(to_sector - sector + sectors, sectors) == 1
            start = device * sent
            block_ref[start : start + keys, :] = key
            start = start + keys
            block_ref[start : start + keys, :] = value
            block_ref[start + keys : start + keys + rows, :] = jnp.where(is_next, last, first)
        group = pl.ds(to_band * sectors * sent, sectors * sent)
        sends.append(
            pltpu.make_async_copy(
                block_ref.at[group],
                sent_ref.at[group],
                sems.at[len(small) + len(large) + to_band],
            )
        )
        sends[-1].start()
    for copy in large + sends:
        copy.wait()


def heads_of(matrix, width):
    lane = lax.broadcasted_iota(jnp.int32, matrix.shape, 1)
    return jnp.concatenate(
        [
            jnp.where((lane >= h * HD) & (lane < (h + 1) * HD), matrix, 0.0)
            for h in range(width // HD)
        ],
        0,
    )


def own_heads(matrix, width, keys):
    lane = lax.broadcasted_iota(jnp.int32, (keys, width), 1)
    result = matrix[0:keys]
    for h in range(1, width // HD):
        result = jnp.where(lane >= h * HD, matrix[h * keys : (h + 1) * keys], result)
    return result


def rows_from_all(rows_ref, first, keys, devices, sent):
    return jnp.concatenate(
        [rows_ref[pl.ds(first + k, devices, stride=sent), :] for k in range(keys)], 0
    )


def dot(left, right, left_dim, right_dim):
    return lax.dot_general(
        left,
        right,
        (((left_dim,), (right_dim,)), ((), ())),
        preferred_element_type=jnp.float32,
    )


def split(value, terms):
    result = []
    for _ in range(terms):
        result.append(value.astype(jnp.bfloat16))
        value = value - result[-1].astype(jnp.float32)
    return result


def rows_by_tokens(rows, tokens):
    count = rows.shape[0]
    large, middle, small = split(rows, 3)
    token_large, token_middle, token_small = split(tokens, 3)
    left = jnp.concatenate(
        [
            jnp.concatenate([large, large], 1),
            jnp.concatenate([middle, middle], 1),
            jnp.concatenate([small, jnp.zeros_like(small)], 1),
        ],
        0,
    )
    main = dot(left, jnp.concatenate([token_large, token_middle], 1), 1, 1)
    rest = dot(large, token_small, 1, 1)
    return main[0:count] + (main[count : 2 * count] + (main[2 * count :] + rest))


def sum_over_tokens(left, right):
    count, width = left.shape[0], right.shape[1]
    every = dot(jnp.concatenate(split(left, 2), 0), jnp.concatenate(split(right, 2), 1), 1, 0)
    top, bottom = every[0:count], every[count:]
    return top[:, 0:width] + (top[:, width:] + bottom[:, 0:width] + bottom[:, width:])


def mix_rows(weights, rows):
    width = rows.shape[1]
    right = jnp.concatenate(split(rows, 2), 1)
    every = dot(jnp.concatenate(split(weights, 2), 0), jnp.concatenate([right, right], 0), 0, 0)
    return every[:, 0:width] + every[:, width:]


def mix_rows_exactly(weights, rows):
    width = rows.shape[1]
    large, middle, small = split(weights, 3)
    row_large, row_middle, row_small = split(rows, 3)
    zero = jnp.zeros_like(row_large)
    right = jnp.concatenate(
        [
            jnp.concatenate([row_large, row_large, row_large, zero], 0),
            jnp.concatenate([row_middle, row_middle, zero, row_small], 0),
        ],
        1,
    )
    every = dot(jnp.concatenate([large, middle, small, large], 0), right, 0, 0)
    return every[:, 0:width] + every[:, width:]


def attention_kernel(bands, sectors, width, keys, *refs):
    part_refs = refs[:bands]
    rows_ref, taps_ref, terms_ref = refs[bands : bands + 3]
    logit_grad_ref = refs[bands + 3]
    query_ref, weighted_ref, grad_ref, out_ref = refs[bands + 4 :]
    band = lax.axis_index("lat")
    sector = lax.axis_index("lon")
    rows, columns = part_refs[0].shape[1:3]
    lines = rows * bands
    tokens = lines * columns
    edge = SUBLANES
    scale = HD ** (-0.5)
    weights = row_weights(lines)
    heads = width // HD
    devices = bands * sectors
    key_total = devices * keys
    sent = block_rows(bands, keys, rows)

    for step, part_ref in enumerate(part_refs):
        start = source(band, step, bands) * rows
        query_ref[pl.ds(start, rows)] = part_ref[0]
        weighted_ref[pl.ds(start + 1, rows), edge : edge + columns, :] = part_ref[1]
    before = lax.rem(sector + sectors - 1, sectors)
    after = lax.rem(sector + 1, sectors)
    for line in range(lines):
        b, r = divmod(line, rows)
        r = 2 * keys + r
        inner = weighted_ref[1 + line, edge : edge + columns, :]
        weighted_ref[1 + line, edge : edge + columns, :] = inner * weights[line]
        left = rows_ref[pl.ds((b * sectors + before) * sent + r, 1), :]
        right = rows_ref[pl.ds((b * sectors + after) * sent + r, 1), :]
        weighted_ref[1 + line, edge - 1 : edge, :] = left * weights[line]
        weighted_ref[1 + line, edge + columns : edge + columns + 1, :] = right * weights[line]
    zeros = jnp.zeros(weighted_ref.shape[1:], jnp.float32)
    weighted_ref[0] = zeros
    weighted_ref[lines + 1] = zeros

    own_lanes = pl.ds(pl.multiple_of(band * width, width), width)
    taps = [taps_ref[t : t + 1, own_lanes] for t in range(len(OFFSETS))]

    def shifted(line, offset):
        a, b = offset
        return weighted_ref[1 + line - a, edge - b : edge - b + columns, :]

    for line in range(lines):
        total = shifted(line, (0, 0))
        for tap, offset in zip(taps, OFFSETS):
            total = total + tap * shifted(line, offset)
        grad_ref[line] = total

    key_heads = heads_of(rows_from_all(rows_ref, 0, keys, devices, sent), width)
    value_heads = heads_of(rows_from_all(rows_ref, keys, keys, devices, sent), width)
    query = query_ref[...].reshape(tokens, width)
    grad = grad_ref[...].reshape(tokens, width)

    logits = rows_by_tokens(key_heads, query) * scale
    prob_list = []
    for h in range(heads):
        part = logits[h * key_total : (h + 1) * key_total]
        raised = jnp.exp(part - jnp.max(part, 0, keepdims=True))
        prob_list.append(raised / jnp.sum(raised, 0, keepdims=True))
    probs = jnp.concatenate(prob_list, 0)
    out_ref[...] = mix_rows(probs, value_heads).reshape(lines, columns, width)
    prob_grad = rows_by_tokens(value_heads, grad)
    logit_grad_list = []
    for h in range(heads):
        part = prob_grad[h * key_total : (h + 1) * key_total]
        row_dot = jnp.sum(prob_list[h] * part, 0, keepdims=True)
        logit_grad_list.append(prob_list[h] * (part - row_dot))
    logit_grad = jnp.concatenate(logit_grad_list, 0)

    key_grad = own_heads(sum_over_tokens(logit_grad, query), width, key_total) * scale
    value_grad = own_heads(sum_over_tokens(probs, grad), width, key_total)

    sums = [jnp.zeros((SUBLANES, width), jnp.float32) for _ in OFFSETS]
    for line in range(lines):
        out_line = out_ref[line]
        for t, offset in enumerate(OFFSETS):
            product = out_line * shifted(line, offset)
            for c in range(0, columns, SUBLANES):
                sums[t] = sums[t] + product[c : c + SUBLANES]
    tap_sum = jnp.concatenate([jnp.sum(s, 0, keepdims=True) for s in sums], 0)
    used = term_rows(keys)
    for k in range(keys):
        mine = slice(k * devices, (k + 1) * devices)
        terms_ref[pl.ds(k, devices, stride=used), :] = key_grad[mine]
        terms_ref[pl.ds(keys + k, devices, stride=used), :] = value_grad[mine]
    for device in range(devices):
        terms_ref[device * used + 2 * keys : (device + 1) * used, :] = tap_sum

    logit_grad_ref[...] = logit_grad


def query_grad_kernel(bands, sectors, width, keys, rows, columns, logit_grad_ref, rows_ref, *refs):
    part_refs, out_ref = refs[:-1], refs[-1]
    band = lax.axis_index("lat")
    devices = bands * sectors
    sent = block_rows(bands, keys, rows)
    key_heads = heads_of(rows_from_all(rows_ref, 0, keys, devices, sent), width)
    query_grad = mix_rows_exactly(logit_grad_ref[...], key_heads) * HD ** (-0.5)
    out_ref[...] = query_grad.reshape(out_ref.shape)
    for step, part_ref in enumerate(part_refs):
        part_ref[...] = out_ref[pl.ds(partner(band, step, bands) * rows, rows)]


def finish_kernel(bands, sectors, width, keys, *refs):
    part_refs = refs[:bands]
    terms_ref, query_ref, key_ref, value_ref, taps_ref = refs[bands:]
    band = lax.axis_index("lat")
    devices = bands * sectors
    rows, columns = query_ref.shape[:2]
    for step, part_ref in enumerate(part_refs):
        lanes = pl.ds(pl.multiple_of(source(band, step, bands) * width, width), width)
        query_ref[:, :, lanes] = part_ref[...]
    used = term_rows(keys)
    parts = []
    for to_band in range(bands):
        lanes = slice(to_band * width, (to_band + 1) * width)
        part = jnp.zeros((used, width), jnp.float32)
        for sector in range(sectors):
            start = (to_band * sectors + sector) * used
            part = part + terms_ref[start : start + used, :]
        key_ref[:, lanes] = part[0:keys]
        value_ref[:, lanes] = part[keys : 2 * keys]
        parts.append(part[2 * keys : used])
    tap_sum = jnp.concatenate(parts, 1)
    mean = jnp.sum(tap_sum * tap_sum, keepdims=True) / (len(OFFSETS) * width * bands)
    taps_ref[...] = tap_sum / jnp.sqrt(mean + 1e-06)


def split_heads_body(queries, key_rows, value_rows, cotangent, conv_taps):
    rows, columns, channels = queries.shape
    bands = lax.axis_size("lat")
    sectors = lax.axis_size("lon")
    devices = bands * sectors
    keys = key_rows.shape[0]
    width = channels // bands
    lines = rows * bands

    sent_rows = block_rows(bands, keys, rows)
    part_shape = (2, rows, columns, width)
    anywhere = pl.BlockSpec(memory_space=pl.ANY)
    here = pl.BlockSpec(memory_space=pltpu.VMEM)
    row_blocks, *parts = pl.pallas_call(
        functools.partial(pack_kernel, bands, sectors, width, keys),
        out_shape=[
            jax.ShapeDtypeStruct(s, jnp.float32)
            for s in [(devices * sent_rows, width)] + [part_shape] * bands
        ],
        in_specs=[anywhere] * 4,
        out_specs=[anywhere] + [here] * bands,
        scratch_shapes=[
            pltpu.VMEM((keys, channels), jnp.float32),
            pltpu.VMEM((keys, channels), jnp.float32),
            pltpu.VMEM((rows, 1, channels), jnp.float32),
            pltpu.VMEM((rows, 1, channels), jnp.float32),
            pltpu.VMEM((devices * sent_rows, width), jnp.float32),
            pltpu.SemaphoreType.DMA((4 + 3 * bands,)),
        ],
        compiler_params=pltpu.CompilerParams(vmem_limit_bytes=VMEM_LIMIT),
    )(*[in_hbm(x) for x in (key_rows, value_rows, queries, cotangent)])
    row_blocks = to_all(row_blocks, devices)
    parts = exchange_all(parts, bands, ahead=True)

    grid = (lines, columns, width)
    heads = width // HD
    heads = width // HD
    terms, logit_grad = vmem_call(
        functools.partial(attention_kernel, bands, sectors, width, keys),
        [(devices * term_rows(keys), width), (heads * devices * keys, lines * columns)],
        [grid, (lines + 2, columns + 2 * SUBLANES, width), grid, grid],
    )(*parts, row_blocks, conv_taps)
    terms = to_all(terms, devices)
    grad_parts = vmem_call(
        functools.partial(query_grad_kernel, bands, sectors, width, keys, rows, columns),
        [(rows, columns, width)] * bands,
        [grid],
    )(logit_grad, row_blocks)
    grad_parts = exchange_all(grad_parts, bands, ahead=False)
    query_grad, key_grad, value_grad, tap_update = pl.pallas_call(
        functools.partial(finish_kernel, bands, sectors, width, keys),
        out_shape=[
            jax.ShapeDtypeStruct(s, jnp.float32)
            for s in (queries.shape, key_rows.shape, value_rows.shape, conv_taps.shape)
        ],
        compiler_params=pltpu.CompilerParams(vmem_limit_bytes=VMEM_LIMIT),
    )(*grad_parts, terms)
    return (query_grad, key_grad, value_grad, tap_update)


def extended(value, sides, width):
    for axis, dim in sides:
        peers, length = (lax.axis_size(axis), value.shape[dim])
        up = [(i, (i + 1) % peers) for i in range(peers)]
        down = [(j, i) for i, j in up]
        last = lax.slice_in_dim(value, length - width, length, axis=dim)
        initial = lax.slice_in_dim(value, 0, width, axis=dim)
        before = lax.ppermute(last, axis, up)
        after = lax.ppermute(initial, axis, down)
        value = jnp.concatenate([before, value, after], axis=dim)
    return value


def split_heads(matrix):
    return matrix.reshape(matrix.shape[0], -1, HD)


def latitude_weights(row_count, band_index, band_count):
    line_total = row_count * band_count
    centres = (jnp.arange(line_total, dtype=jnp.float32) + 0.5) * (jnp.pi / line_total)
    mean_cosine = jnp.sum(jnp.sin(centres)) / line_total
    mine = (band_index * row_count + jnp.arange(row_count, dtype=jnp.int32)).astype(jnp.float32)
    return jnp.sin((mine + 0.5) * (jnp.pi / line_total)) / mean_cosine


def close_poles(padded, row_dim, band_index, band_count):
    height = padded.shape[row_dim]
    positions = jnp.arange(height)
    outside = (positions == 0) & (band_index == 0) | (positions == height - 1) & (
        band_index == band_count - 1
    )
    shape_mask = [1] * padded.ndim
    shape_mask[row_dim] = height
    return jnp.where(outside.reshape(shape_mask), 0.0, padded)


def spread_taps(weighted, grad_padded, conv_taps):
    row_count, col_count = (weighted.shape[0], weighted.shape[1])
    result = weighted
    for tap_index, (shift_row, shift_col) in enumerate(OFFSETS):
        result = (
            result
            + conv_taps[tap_index]
            * grad_padded[
                1 - shift_row : 1 - shift_row + row_count, 1 - shift_col : 1 - shift_col + col_count
            ]
        )
    return result


def tap_terms(weighted, out_padded):
    row_count, col_count = (weighted.shape[0], weighted.shape[1])
    term_list = []
    for shift_row, shift_col in OFFSETS:
        term_list.append(
            jnp.sum(
                out_padded[
                    1 + shift_row : 1 + shift_row + row_count,
                    1 + shift_col : 1 + shift_col + col_count,
                ]
                * weighted,
                axis=(0, 1),
            )
        )
    return jnp.stack(term_list)


def group_logits(query_part, key_part):
    return jnp.einsum(
        "qhd,khd->hqk", split_heads(query_part), split_heads(key_part), precision=HIGH
    ) * HD ** (-0.5)


def whole_rows_body(queries, key_rows, value_rows, cotangent, conv_taps):
    row_count, col_count, channels = queries.shape
    band_count = lax.axis_size("lat")
    band_index = lax.axis_index("lat")
    weighted = cotangent * latitude_weights(row_count, band_index, band_count)[:, None, None]
    paired_rows = jnp.concatenate([key_rows, value_rows], 1)
    paired_all = lax.all_gather(paired_rows, ("lat", "lon"), axis=0, tiled=True)
    key_all = paired_all[:, :channels]
    value_all = paired_all[:, channels:]
    token_count = row_count * col_count
    key_count = key_all.shape[0]
    query_flat = queries.reshape(token_count, channels)
    group_width = 2 * HD
    group_count = channels // group_width
    outputs = []
    peaks = []
    sums_soft = []
    for group_index in range(group_count):
        col_start = group_index * group_width
        col_stop = col_start + group_width
        logits = group_logits(query_flat[:, col_start:col_stop], key_all[:, col_start:col_stop])
        row_peak = jnp.max(logits, -1, keepdims=True)
        raised = jnp.exp(logits - row_peak)
        normaliser = jnp.sum(raised, -1, keepdims=True)
        soft_weights = raised / normaliser
        outputs.append(
            jnp.einsum(
                "hqk,khd->qhd",
                soft_weights,
                split_heads(value_all[:, col_start:col_stop]),
                precision=HIGH,
            ).reshape(token_count, group_width)
        )
        peaks.append(row_peak)
        sums_soft.append(normaliser)
    out_flat = jnp.concatenate(outputs, 1)
    out_grid = out_flat.reshape(row_count, col_count, channels)
    both_padded = close_poles(
        extended(jnp.stack([weighted, out_grid]), (("lat", 1), ("lon", 2)), 1),
        1,
        band_index,
        band_count,
    )
    grad_padded = both_padded[0]
    out_padded = both_padded[1]
    out_grad = spread_taps(weighted, grad_padded, conv_taps)
    tap_sum = lax.psum(tap_terms(weighted, out_padded), ("lat", "lon"))
    tap_update = tap_sum / jnp.sqrt(jnp.mean(tap_sum * tap_sum) + 1e-06)
    grad_flat = out_grad.reshape(token_count, channels)
    query_parts = []
    key_parts = []
    value_parts = []
    for group_index in range(group_count):
        col_start = group_index * group_width
        col_stop = col_start + group_width
        query_heads = split_heads(query_flat[:, col_start:col_stop])
        key_heads = split_heads(key_all[:, col_start:col_stop])
        logits = jnp.einsum("qhd,khd->hqk", query_heads, key_heads, precision=HIGH) * HD ** (-0.5)
        soft_weights = jnp.exp(logits - peaks[group_index]) / sums_soft[group_index]
        grad_heads = split_heads(grad_flat[:, col_start:col_stop])
        value_parts.append(
            jnp.einsum("hqk,qhd->khd", soft_weights, grad_heads, precision=HIGH).reshape(
                key_count, group_width
            )
        )
        prob_grad = jnp.einsum(
            "qhd,khd->hqk",
            grad_heads,
            split_heads(value_all[:, col_start:col_stop]),
            precision=HIGH,
        )
        row_dot = jnp.transpose(
            jnp.sum(grad_heads * split_heads(out_flat[:, col_start:col_stop]), -1)
        )[:, :, None]
        logit_grad = soft_weights * (prob_grad - row_dot)
        query_parts.append(
            (
                jnp.einsum("hqk,khd->qhd", logit_grad, key_heads, precision=HIGH) * HD ** (-0.5)
            ).reshape(token_count, group_width)
        )
        key_parts.append(
            (
                jnp.einsum("hqk,qhd->khd", logit_grad, query_heads, precision=HIGH) * HD ** (-0.5)
            ).reshape(key_count, group_width)
        )
    paired_terms = jnp.concatenate(key_parts + value_parts, 1)
    paired_band = lax.psum_scatter(paired_terms, "lat", scatter_dimension=0, tiled=True)
    paired_grad = lax.psum_scatter(paired_band, "lon", scatter_dimension=0, tiled=True)
    key_grad = paired_grad[:, :channels]
    value_grad = paired_grad[:, channels:]
    query_grad = jnp.concatenate(query_parts, 1).reshape(row_count, col_count, channels)
    return (query_grad, key_grad, value_grad, tap_update)


def body(queries, key_rows, value_rows, cotangent, conv_taps):
    bands = lax.axis_size("lat")
    sectors = lax.axis_size("lon")
    rows, columns, channels = queries.shape
    whole_heads = channels % (bands * LANES) == 0
    whole_tiles = columns % SUBLANES == 0 and (rows * columns) % LANES == 0
    if whole_heads and whole_tiles and sectors > 2:
        return split_heads_body(queries, key_rows, value_rows, cotangent, conv_taps)
    return whole_rows_body(queries, key_rows, value_rows, cotangent, conv_taps)


def solution(mesh):
    placed = (
        P("lat", "lon", None),
        P(("lat", "lon"), None),
        P(("lat", "lon"), None),
        P("lat", "lon", None),
        P(),
    )
    return jax.shard_map(
        body,
        mesh=mesh,
        in_specs=placed,
        out_specs=(P("lat", "lon", None), P(("lat", "lon"), None), P(("lat", "lon"), None), P()),
        check_vma=False,
    )
```

```python
import functools

import jax
import jax.numpy as jnp
import numpy as np
from jax import lax
from jax.experimental import pallas as pl
from jax.experimental.pallas import tpu as pltpu
from jax.sharding import PartitionSpec as P

HD = 64
LANES = 128
SUBLANES = 8
VMEM_LIMIT = 16 * 1024 * 1024

HIGH = lax.Precision.HIGHEST
OFFSETS = ((-1, -1), (-1, 0), (-1, 1), (0, -1), (0, 0), (0, 1), (1, -1), (1, 0), (1, 1))


def partner(index, step, peers):
    if peers & (peers - 1) == 0:
        return index ^ step
    return lax.rem(index + step, peers) if not isinstance(index, int) else (index + step) % peers


def source(index, step, peers):
    return partner(index, step if peers & (peers - 1) == 0 else peers - step, peers)


def exchange(value, step, peers):
    return lax.ppermute(value, "lat", [(i, partner(i, step, peers)) for i in range(peers)])


def to_all(blocks, devices):
    rows, width = blocks.shape
    blocks = blocks.reshape(devices, rows // devices, 1, width)
    return lax.all_to_all(blocks, ("lat", "lon"), 0, 0, tiled=True).reshape(rows, width)


def row_weights(line_total):
    cosine = np.sin((np.arange(line_total, dtype=np.float64) + 0.5) * (np.pi / line_total))
    return [float(w) for w in cosine / np.mean(cosine)]


def vmem_call(kernel, out_shapes, scratch=()):
    return pl.pallas_call(
        kernel,
        out_shape=[jax.ShapeDtypeStruct(s, jnp.float32) for s in out_shapes],
        scratch_shapes=[pltpu.VMEM(s, jnp.float32) for s in scratch],
        compiler_params=pltpu.CompilerParams(vmem_limit_bytes=VMEM_LIMIT),
    )


def arrival_kernel(part_ref, out_ref):
    out_ref[...] = part_ref[...]


def exchange_all(parts, bands, ahead):
    last = exchange(parts[-1], bands - 1, bands)
    cost = pl.CostEstimate(flops=10**10, bytes_accessed=10**6, transcendentals=0)
    (last,) = pl.pallas_call(
        arrival_kernel,
        out_shape=[jax.ShapeDtypeStruct(last.shape, jnp.float32)],
        cost_estimate=cost if ahead else None,
        compiler_params=pltpu.CompilerParams(vmem_limit_bytes=VMEM_LIMIT),
    )(last)
    return [parts[0]] + [exchange(parts[s], s, bands) for s in range(1, bands - 1)] + [last]


def block_rows(bands, keys, rows):
    return 2 * keys + rows


def term_rows(keys):
    return 2 * keys + len(OFFSETS)


def in_hbm(array):
    return pltpu.with_memory_space_constraint(array, pltpu.HBM)


def pack_kernel(bands, sectors, width, keys, *refs):
    key_ref, value_ref, query_ref, cotangent_ref, sent_ref = refs[:5]
    part_refs = refs[5 : 5 + bands]
    key_own, value_own, first_own, last_own, block_ref, sems = refs[5 + bands :]
    band = lax.axis_index("lat")
    sector = lax.axis_index("lon")
    rows, columns = query_ref.shape[:2]
    sent = block_rows(bands, keys, rows)

    small = [
        pltpu.make_async_copy(source_ref, target_ref, sems.at[i])
        for i, (source_ref, target_ref) in enumerate(
            (
                (key_ref, key_own),
                (value_ref, value_own),
                (cotangent_ref.at[:, 0:1, :], first_own),
                (cotangent_ref.at[:, columns - 1 : columns, :], last_own),
            )
        )
    ]
    for copy in small:
        copy.start()
    large = []
    for step, part_ref in enumerate(part_refs):
        lanes = pl.ds(pl.multiple_of(partner(band, step, bands) * width, width), width)
        for i, array_ref in enumerate((query_ref, cotangent_ref)):
            large.append(
                pltpu.make_async_copy(
                    array_ref.at[:, :, lanes], part_ref.at[i], sems.at[len(small) + len(large)]
                )
            )
    for copy in large:
        copy.start()
    for copy in small:
        copy.wait()
    sends = []
    for to_band in range(bands):
        lanes = slice(to_band * width, (to_band + 1) * width)
        key = key_own[:, lanes]
        value = value_own[:, lanes]
        first = first_own[:, 0, lanes]
        last = last_own[:, 0, lanes]
        for to_sector in range(sectors):
            device = to_band * sectors + to_sector
            is_next = lax.rem(to_sector - sector + sectors, sectors) == 1
            start = device * sent
            block_ref[start : start + keys, :] = key
            start = start + keys
            block_ref[start : start + keys, :] = value
            block_ref[start + keys : start + keys + rows, :] = jnp.where(is_next, last, first)
        group = pl.ds(to_band * sectors * sent, sectors * sent)
        sends.append(
            pltpu.make_async_copy(
                block_ref.at[group],
                sent_ref.at[group],
                sems.at[len(small) + len(large) + to_band],
            )
        )
        sends[-1].start()
    for copy in large + sends:
        copy.wait()


def heads_of(matrix, width):
    lane = lax.broadcasted_iota(jnp.int32, matrix.shape, 1)
    return jnp.concatenate(
        [
            jnp.where((lane >= h * HD) & (lane < (h + 1) * HD), matrix, 0.0)
            for h in range(width // HD)
        ],
        0,
    )


def own_heads(matrix, width, keys):
    lane = lax.broadcasted_iota(jnp.int32, (keys, width), 1)
    result = matrix[0:keys]
    for h in range(1, width // HD):
        result = jnp.where(lane >= h * HD, matrix[h * keys : (h + 1) * keys], result)
    return result


def rows_from_all(rows_ref, first, keys, devices, sent):
    return jnp.concatenate(
        [rows_ref[pl.ds(first + k, devices, stride=sent), :] for k in range(keys)], 0
    )


def dot(left, right, left_dim, right_dim):
    return lax.dot_general(
        left,
        right,
        (((left_dim,), (right_dim,)), ((), ())),
        preferred_element_type=jnp.float32,
    )


def split(value, terms):
    result = []
    for _ in range(terms):
        result.append(value.astype(jnp.bfloat16))
        value = value - result[-1].astype(jnp.float32)
    return result


def rows_by_tokens(rows, tokens):
    count = rows.shape[0]
    large, middle, small = split(rows, 3)
    token_large, token_middle, token_small = split(tokens, 3)
    left = jnp.concatenate(
        [
            jnp.concatenate([large, large], 1),
            jnp.concatenate([middle, middle], 1),
            jnp.concatenate([small, jnp.zeros_like(small)], 1),
        ],
        0,
    )
    main = dot(left, jnp.concatenate([token_large, token_middle], 1), 1, 1)
    rest = dot(large, token_small, 1, 1)
    return main[0:count] + (main[count : 2 * count] + (main[2 * count :] + rest))


def sum_over_tokens(left, right):
    count, width = left.shape[0], right.shape[1]
    every = dot(jnp.concatenate(split(left, 2), 0), jnp.concatenate(split(right, 2), 1), 1, 0)
    top, bottom = every[0:count], every[count:]
    return top[:, 0:width] + (top[:, width:] + bottom[:, 0:width] + bottom[:, width:])


def mix_rows(weights, rows):
    width = rows.shape[1]
    right = jnp.concatenate(split(rows, 2), 1)
    every = dot(jnp.concatenate(split(weights, 2), 0), jnp.concatenate([right, right], 0), 0, 0)
    return every[:, 0:width] + every[:, width:]


def mix_rows_exactly(weights, rows):
    width = rows.shape[1]
    large, middle, small = split(weights, 3)
    row_large, row_middle, row_small = split(rows, 3)
    zero = jnp.zeros_like(row_large)
    right = jnp.concatenate(
        [
            jnp.concatenate([row_large, row_large, row_large, zero], 0),
            jnp.concatenate([row_middle, row_middle, zero, row_small], 0),
        ],
        1,
    )
    every = dot(jnp.concatenate([large, middle, small, large], 0), right, 0, 0)
    return every[:, 0:width] + every[:, width:]


def attention_kernel(bands, sectors, width, keys, *refs):
    part_refs = refs[:bands]
    rows_ref, taps_ref, terms_ref = refs[bands : bands + 3]
    query_grad_refs = refs[bands + 3 : 2 * bands + 3]
    query_ref, weighted_ref, grad_ref, out_ref = refs[2 * bands + 3 :]
    band = lax.axis_index("lat")
    sector = lax.axis_index("lon")
    rows, columns = part_refs[0].shape[1:3]
    lines = rows * bands
    tokens = lines * columns
    edge = SUBLANES
    scale = HD ** (-0.5)
    weights = row_weights(lines)
    heads = width // HD
    devices = bands * sectors
    key_total = devices * keys
    sent = block_rows(bands, keys, rows)

    for step, part_ref in enumerate(part_refs):
        start = source(band, step, bands) * rows
        query_ref[pl.ds(start, rows)] = part_ref[0]
        weighted_ref[pl.ds(start + 1, rows), edge : edge + columns, :] = part_ref[1]
    before = lax.rem(sector + sectors - 1, sectors)
    after = lax.rem(sector + 1, sectors)
    for line in range(lines):
        b, r = divmod(line, rows)
        r = 2 * keys + r
        inner = weighted_ref[1 + line, edge : edge + columns, :]
        weighted_ref[1 + line, edge : edge + columns, :] = inner * weights[line]
        left = rows_ref[pl.ds((b * sectors + before) * sent + r, 1), :]
        right = rows_ref[pl.ds((b * sectors + after) * sent + r, 1), :]
        weighted_ref[1 + line, edge - 1 : edge, :] = left * weights[line]
        weighted_ref[1 + line, edge + columns : edge + columns + 1, :] = right * weights[line]
    zeros = jnp.zeros(weighted_ref.shape[1:], jnp.float32)
    weighted_ref[0] = zeros
    weighted_ref[lines + 1] = zeros

    own_lanes = pl.ds(pl.multiple_of(band * width, width), width)
    taps = [taps_ref[t : t + 1, own_lanes] for t in range(len(OFFSETS))]

    def shifted(line, offset):
        a, b = offset
        return weighted_ref[1 + line - a, edge - b : edge - b + columns, :]

    for line in range(lines):
        total = shifted(line, (0, 0))
        for tap, offset in zip(taps, OFFSETS):
            total = total + tap * shifted(line, offset)
        grad_ref[line] = total

    key_heads = heads_of(rows_from_all(rows_ref, 0, keys, devices, sent), width)
    value_heads = heads_of(rows_from_all(rows_ref, keys, keys, devices, sent), width)
    query = query_ref[...].reshape(tokens, width)
    grad = grad_ref[...].reshape(tokens, width)

    logits = rows_by_tokens(key_heads, query) * scale
    prob_list = []
    for h in range(heads):
        part = logits[h * key_total : (h + 1) * key_total]
        raised = jnp.exp(part - jnp.max(part, 0, keepdims=True))
        prob_list.append(raised * (1.0 / jnp.sum(raised, 0, keepdims=True)))
    probs = jnp.concatenate(prob_list, 0)
    out_ref[...] = mix_rows(probs, value_heads).reshape(lines, columns, width)
    prob_grad = rows_by_tokens(value_heads, grad)
    logit_grad_list = []
    for h in range(heads):
        part = prob_grad[h * key_total : (h + 1) * key_total]
        row_dot = jnp.sum(prob_list[h] * part, 0, keepdims=True)
        logit_grad_list.append(prob_list[h] * (part - row_dot))
    logit_grad = jnp.concatenate(logit_grad_list, 0)

    key_grad = own_heads(sum_over_tokens(logit_grad, query), width, key_total) * scale
    value_grad = own_heads(sum_over_tokens(probs, grad), width, key_total)

    sums = [jnp.zeros((SUBLANES, width), jnp.float32) for _ in OFFSETS]
    for line in range(lines):
        out_line = out_ref[line]
        for t, offset in enumerate(OFFSETS):
            product = out_line * shifted(line, offset)
            for c in range(0, columns, SUBLANES):
                sums[t] = sums[t] + product[c : c + SUBLANES]
    tap_sum = jnp.concatenate([jnp.sum(s, 0, keepdims=True) for s in sums], 0)
    used = term_rows(keys)
    for k in range(keys):
        mine = slice(k * devices, (k + 1) * devices)
        terms_ref[pl.ds(k, devices, stride=used), :] = key_grad[mine]
        terms_ref[pl.ds(keys + k, devices, stride=used), :] = value_grad[mine]
    for device in range(devices):
        terms_ref[device * used + 2 * keys : (device + 1) * used, :] = tap_sum

    out_ref[...] = (mix_rows_exactly(logit_grad, key_heads) * scale).reshape(out_ref.shape)
    for step, part_ref in enumerate(query_grad_refs):
        part_ref[...] = out_ref[pl.ds(partner(band, step, bands) * rows, rows)]


def finish_kernel(bands, sectors, width, keys, *refs):
    part_refs = refs[:bands]
    terms_ref, query_ref, key_ref, value_ref, taps_ref = refs[bands:]
    band = lax.axis_index("lat")
    devices = bands * sectors
    rows, columns = query_ref.shape[:2]
    for step, part_ref in enumerate(part_refs):
        lanes = pl.ds(pl.multiple_of(source(band, step, bands) * width, width), width)
        query_ref[:, :, lanes] = part_ref[...]
    used = term_rows(keys)
    parts = []
    for to_band in range(bands):
        lanes = slice(to_band * width, (to_band + 1) * width)
        rows_of = [
            terms_ref[(to_band * sectors + sector) * used : (to_band * sectors + sector + 1) * used, :]
            for sector in range(sectors)
        ]
        while len(rows_of) > 1:
            rows_of = [sum(rows_of[i : i + 2]) for i in range(0, len(rows_of), 2)]
        part = rows_of[0]
        key_ref[:, lanes] = part[0:keys]
        value_ref[:, lanes] = part[keys : 2 * keys]
        parts.append(part[2 * keys : used])
    tap_sum = jnp.concatenate(parts, 1)
    mean = jnp.sum(tap_sum * tap_sum, keepdims=True) / (len(OFFSETS) * width * bands)
    taps_ref[...] = tap_sum / jnp.sqrt(mean + 1e-06)


def split_heads_body(queries, key_rows, value_rows, cotangent, conv_taps):
    rows, columns, channels = queries.shape
    bands = lax.axis_size("lat")
    sectors = lax.axis_size("lon")
    devices = bands * sectors
    keys = key_rows.shape[0]
    width = channels // bands
    lines = rows * bands

    sent_rows = block_rows(bands, keys, rows)
    part_shape = (2, rows, columns, width)
    anywhere = pl.BlockSpec(memory_space=pl.ANY)
    here = pl.BlockSpec(memory_space=pltpu.VMEM)
    row_blocks, *parts = pl.pallas_call(
        functools.partial(pack_kernel, bands, sectors, width, keys),
        out_shape=[
            jax.ShapeDtypeStruct(s, jnp.float32)
            for s in [(devices * sent_rows, width)] + [part_shape] * bands
        ],
        in_specs=[anywhere] * 4,
        out_specs=[anywhere] + [here] * bands,
        scratch_shapes=[
            pltpu.VMEM((keys, channels), jnp.float32),
            pltpu.VMEM((keys, channels), jnp.float32),
            pltpu.VMEM((rows, 1, channels), jnp.float32),
            pltpu.VMEM((rows, 1, channels), jnp.float32),
            pltpu.VMEM((devices * sent_rows, width), jnp.float32),
            pltpu.SemaphoreType.DMA((4 + 3 * bands,)),
        ],
        compiler_params=pltpu.CompilerParams(vmem_limit_bytes=VMEM_LIMIT),
    )(*[in_hbm(x) for x in (key_rows, value_rows, queries, cotangent)])
    row_blocks = to_all(row_blocks, devices)
    parts = exchange_all(parts, bands, ahead=True)

    grid = (lines, columns, width)
    heads = width // HD
    terms, *grad_parts = vmem_call(
        functools.partial(attention_kernel, bands, sectors, width, keys),
        [(devices * term_rows(keys), width)] + [(rows, columns, width)] * bands,
        [
            grid,
            (lines + 2, columns + 2 * SUBLANES, width),
            grid,
            grid,
        ],
    )(*parts, row_blocks, conv_taps)

    terms = to_all(terms, devices)
    grad_parts = exchange_all(grad_parts, bands, ahead=False)
    query_grad, key_grad, value_grad, tap_update = pl.pallas_call(
        functools.partial(finish_kernel, bands, sectors, width, keys),
        out_shape=[
            jax.ShapeDtypeStruct(s, jnp.float32)
            for s in (queries.shape, key_rows.shape, value_rows.shape, conv_taps.shape)
        ],
        compiler_params=pltpu.CompilerParams(vmem_limit_bytes=VMEM_LIMIT),
    )(*grad_parts, terms)
    return (query_grad, key_grad, value_grad, tap_update)


def extended(value, sides, width):
    for axis, dim in sides:
        peers, length = (lax.axis_size(axis), value.shape[dim])
        up = [(i, (i + 1) % peers) for i in range(peers)]
        down = [(j, i) for i, j in up]
        last = lax.slice_in_dim(value, length - width, length, axis=dim)
        initial = lax.slice_in_dim(value, 0, width, axis=dim)
        before = lax.ppermute(last, axis, up)
        after = lax.ppermute(initial, axis, down)
        value = jnp.concatenate([before, value, after], axis=dim)
    return value


def split_heads(matrix):
    return matrix.reshape(matrix.shape[0], -1, HD)


def latitude_weights(row_count, band_index, band_count):
    line_total = row_count * band_count
    centres = (jnp.arange(line_total, dtype=jnp.float32) + 0.5) * (jnp.pi / line_total)
    mean_cosine = jnp.sum(jnp.sin(centres)) / line_total
    mine = (band_index * row_count + jnp.arange(row_count, dtype=jnp.int32)).astype(jnp.float32)
    return jnp.sin((mine + 0.5) * (jnp.pi / line_total)) / mean_cosine


def close_poles(padded, row_dim, band_index, band_count):
    height = padded.shape[row_dim]
    positions = jnp.arange(height)
    outside = (positions == 0) & (band_index == 0) | (positions == height - 1) & (
        band_index == band_count - 1
    )
    shape_mask = [1] * padded.ndim
    shape_mask[row_dim] = height
    return jnp.where(outside.reshape(shape_mask), 0.0, padded)


def spread_taps(weighted, grad_padded, conv_taps):
    row_count, col_count = (weighted.shape[0], weighted.shape[1])
    result = weighted
    for tap_index, (shift_row, shift_col) in enumerate(OFFSETS):
        result = (
            result
            + conv_taps[tap_index]
            * grad_padded[
                1 - shift_row : 1 - shift_row + row_count, 1 - shift_col : 1 - shift_col + col_count
            ]
        )
    return result


def tap_terms(weighted, out_padded):
    row_count, col_count = (weighted.shape[0], weighted.shape[1])
    term_list = []
    for shift_row, shift_col in OFFSETS:
        term_list.append(
            jnp.sum(
                out_padded[
                    1 + shift_row : 1 + shift_row + row_count,
                    1 + shift_col : 1 + shift_col + col_count,
                ]
                * weighted,
                axis=(0, 1),
            )
        )
    return jnp.stack(term_list)


def group_logits(query_part, key_part):
    return jnp.einsum(
        "qhd,khd->hqk", split_heads(query_part), split_heads(key_part), precision=HIGH
    ) * HD ** (-0.5)


def whole_rows_body(queries, key_rows, value_rows, cotangent, conv_taps):
    row_count, col_count, channels = queries.shape
    band_count = lax.axis_size("lat")
    band_index = lax.axis_index("lat")
    weighted = cotangent * latitude_weights(row_count, band_index, band_count)[:, None, None]
    paired_rows = jnp.concatenate([key_rows, value_rows], 1)
    paired_all = lax.all_gather(paired_rows, ("lat", "lon"), axis=0, tiled=True)
    key_all = paired_all[:, :channels]
    value_all = paired_all[:, channels:]
    token_count = row_count * col_count
    key_count = key_all.shape[0]
    query_flat = queries.reshape(token_count, channels)
    group_width = 2 * HD
    group_count = channels // group_width
    outputs = []
    peaks = []
    sums_soft = []
    for group_index in range(group_count):
        col_start = group_index * group_width
        col_stop = col_start + group_width
        logits = group_logits(query_flat[:, col_start:col_stop], key_all[:, col_start:col_stop])
        row_peak = jnp.max(logits, -1, keepdims=True)
        raised = jnp.exp(logits - row_peak)
        normaliser = jnp.sum(raised, -1, keepdims=True)
        soft_weights = raised / normaliser
        outputs.append(
            jnp.einsum(
                "hqk,khd->qhd",
                soft_weights,
                split_heads(value_all[:, col_start:col_stop]),
                precision=HIGH,
            ).reshape(token_count, group_width)
        )
        peaks.append(row_peak)
        sums_soft.append(normaliser)
    out_flat = jnp.concatenate(outputs, 1)
    out_grid = out_flat.reshape(row_count, col_count, channels)
    both_padded = close_poles(
        extended(jnp.stack([weighted, out_grid]), (("lat", 1), ("lon", 2)), 1),
        1,
        band_index,
        band_count,
    )
    grad_padded = both_padded[0]
    out_padded = both_padded[1]
    out_grad = spread_taps(weighted, grad_padded, conv_taps)
    tap_sum = lax.psum(tap_terms(weighted, out_padded), ("lat", "lon"))
    tap_update = tap_sum / jnp.sqrt(jnp.mean(tap_sum * tap_sum) + 1e-06)
    grad_flat = out_grad.reshape(token_count, channels)
    query_parts = []
    key_parts = []
    value_parts = []
    for group_index in range(group_count):
        col_start = group_index * group_width
        col_stop = col_start + group_width
        query_heads = split_heads(query_flat[:, col_start:col_stop])
        key_heads = split_heads(key_all[:, col_start:col_stop])
        logits = jnp.einsum("qhd,khd->hqk", query_heads, key_heads, precision=HIGH) * HD ** (-0.5)
        soft_weights = jnp.exp(logits - peaks[group_index]) / sums_soft[group_index]
        grad_heads = split_heads(grad_flat[:, col_start:col_stop])
        value_parts.append(
            jnp.einsum("hqk,qhd->khd", soft_weights, grad_heads, precision=HIGH).reshape(
                key_count, group_width
            )
        )
        prob_grad = jnp.einsum(
            "qhd,khd->hqk",
            grad_heads,
            split_heads(value_all[:, col_start:col_stop]),
            precision=HIGH,
        )
        row_dot = jnp.transpose(
            jnp.sum(grad_heads * split_heads(out_flat[:, col_start:col_stop]), -1)
        )[:, :, None]
        logit_grad = soft_weights * (prob_grad - row_dot)
        query_parts.append(
            (
                jnp.einsum("hqk,khd->qhd", logit_grad, key_heads, precision=HIGH) * HD ** (-0.5)
            ).reshape(token_count, group_width)
        )
        key_parts.append(
            (
                jnp.einsum("hqk,qhd->khd", logit_grad, query_heads, precision=HIGH) * HD ** (-0.5)
            ).reshape(key_count, group_width)
        )
    paired_terms = jnp.concatenate(key_parts + value_parts, 1)
    paired_band = lax.psum_scatter(paired_terms, "lat", scatter_dimension=0, tiled=True)
    paired_grad = lax.psum_scatter(paired_band, "lon", scatter_dimension=0, tiled=True)
    key_grad = paired_grad[:, :channels]
    value_grad = paired_grad[:, channels:]
    query_grad = jnp.concatenate(query_parts, 1).reshape(row_count, col_count, channels)
    return (query_grad, key_grad, value_grad, tap_update)


def body(queries, key_rows, value_rows, cotangent, conv_taps):
    bands = lax.axis_size("lat")
    sectors = lax.axis_size("lon")
    rows, columns, channels = queries.shape
    whole_heads = channels % (bands * LANES) == 0
    whole_tiles = columns % SUBLANES == 0 and (rows * columns) % LANES == 0
    if whole_heads and whole_tiles and sectors > 2:
        return split_heads_body(queries, key_rows, value_rows, cotangent, conv_taps)
    return whole_rows_body(queries, key_rows, value_rows, cotangent, conv_taps)


def solution(mesh):
    placed = (
        P("lat", "lon", None),
        P(("lat", "lon"), None),
        P(("lat", "lon"), None),
        P("lat", "lon", None),
        P(),
    )
    return jax.shard_map(
        body,
        mesh=mesh,
        in_specs=placed,
        out_specs=(P("lat", "lon", None), P(("lat", "lon"), None), P(("lat", "lon"), None), P()),
        check_vma=False,
    )
```

```python
import functools

import jax
import jax.numpy as jnp
import numpy as np
from jax import lax
from jax.experimental import pallas as pl
from jax.experimental.pallas import tpu as pltpu
from jax.sharding import PartitionSpec as P

HD = 64
LANES = 128
SUBLANES = 8
VMEM_LIMIT = 16 * 1024 * 1024

HIGH = lax.Precision.HIGHEST
OFFSETS = ((-1, -1), (-1, 0), (-1, 1), (0, -1), (0, 0), (0, 1), (1, -1), (1, 0), (1, 1))


def partner(index, step, peers):
    if peers & (peers - 1) == 0:
        return index ^ (peers - 1 - step if 0 < step < peers - 1 else step)
    return lax.rem(index + step, peers) if not isinstance(index, int) else (index + step) % peers


def source(index, step, peers):
    return partner(index, step if peers & (peers - 1) == 0 else peers - step, peers)


def exchange(value, step, peers):
    return lax.ppermute(value, "lat", [(i, partner(i, step, peers)) for i in range(peers)])


def to_all(blocks, devices):
    rows, width = blocks.shape
    blocks = blocks.reshape(devices, rows // devices, 1, width)
    return lax.all_to_all(blocks, ("lat", "lon"), 0, 0, tiled=True).reshape(rows, width)


def row_weights(line_total):
    cosine = np.sin((np.arange(line_total, dtype=np.float64) + 0.5) * (np.pi / line_total))
    return [float(w) for w in cosine / np.mean(cosine)]


def vmem_call(kernel, out_shapes, scratch=()):
    return pl.pallas_call(
        kernel,
        out_shape=[jax.ShapeDtypeStruct(s, jnp.float32) for s in out_shapes],
        scratch_shapes=[pltpu.VMEM(s, jnp.float32) for s in scratch],
        compiler_params=pltpu.CompilerParams(vmem_limit_bytes=VMEM_LIMIT),
    )


def arrival_kernel(part_ref, out_ref):
    out_ref[...] = part_ref[...]


def exchange_all(parts, bands, ahead):
    last = exchange(parts[-1], bands - 1, bands)
    cost = pl.CostEstimate(flops=10**10, bytes_accessed=10**6, transcendentals=0)
    (last,) = pl.pallas_call(
        arrival_kernel,
        out_shape=[jax.ShapeDtypeStruct(last.shape, jnp.float32)],
        cost_estimate=cost if ahead else None,
        compiler_params=pltpu.CompilerParams(vmem_limit_bytes=VMEM_LIMIT),
    )(last)
    return [parts[0]] + [exchange(parts[s], s, bands) for s in range(1, bands - 1)] + [last]


def block_rows(bands, keys, rows):
    return 2 * keys + rows


def term_rows(keys):
    return 2 * keys + len(OFFSETS)


def in_hbm(array):
    return pltpu.with_memory_space_constraint(array, pltpu.HBM)


def pack_kernel(bands, sectors, width, keys, *refs):
    key_ref, value_ref, query_ref, cotangent_ref, sent_ref = refs[:5]
    part_refs = refs[5 : 5 + bands]
    key_own, value_own, first_own, last_own, block_ref, sems = refs[5 + bands :]
    band = lax.axis_index("lat")
    sector = lax.axis_index("lon")
    rows, columns = query_ref.shape[:2]
    sent = block_rows(bands, keys, rows)

    small = [
        pltpu.make_async_copy(source_ref, target_ref, sems.at[i])
        for i, (source_ref, target_ref) in enumerate(
            (
                (key_ref, key_own),
                (value_ref, value_own),
                (cotangent_ref.at[:, 0:1, :], first_own),
                (cotangent_ref.at[:, columns - 1 : columns, :], last_own),
            )
        )
    ]
    for copy in small:
        copy.start()
    large = []
    for step, part_ref in enumerate(part_refs):
        lanes = pl.ds(pl.multiple_of(partner(band, step, bands) * width, width), width)
        for i, array_ref in enumerate((query_ref, cotangent_ref)):
            large.append(
                pltpu.make_async_copy(
                    array_ref.at[:, :, lanes], part_ref.at[i], sems.at[len(small) + len(large)]
                )
            )
    for copy in large:
        copy.start()
    for copy in small:
        copy.wait()
    sends = []
    for to_band in range(bands):
        lanes = slice(to_band * width, (to_band + 1) * width)
        key = key_own[:, lanes]
        value = value_own[:, lanes]
        first = first_own[:, 0, lanes]
        last = last_own[:, 0, lanes]
        for to_sector in range(sectors):
            device = to_band * sectors + to_sector
            is_next = lax.rem(to_sector - sector + sectors, sectors) == 1
            start = device * sent
            block_ref[start : start + keys, :] = key
            start = start + keys
            block_ref[start : start + keys, :] = value
            block_ref[start + keys : start + keys + rows, :] = jnp.where(is_next, last, first)
        group = pl.ds(to_band * sectors * sent, sectors * sent)
        sends.append(
            pltpu.make_async_copy(
                block_ref.at[group],
                sent_ref.at[group],
                sems.at[len(small) + len(large) + to_band],
            )
        )
        sends[-1].start()
    for copy in large + sends:
        copy.wait()


def heads_of(matrix, width):
    lane = lax.broadcasted_iota(jnp.int32, matrix.shape, 1)
    return jnp.concatenate(
        [
            jnp.where((lane >= h * HD) & (lane < (h + 1) * HD), matrix, 0.0)
            for h in range(width // HD)
        ],
        0,
    )


def own_heads(matrix, width, keys):
    lane = lax.broadcasted_iota(jnp.int32, (keys, width), 1)
    result = matrix[0:keys]
    for h in range(1, width // HD):
        result = jnp.where(lane >= h * HD, matrix[h * keys : (h + 1) * keys], result)
    return result


def rows_from_all(rows_ref, first, keys, devices, sent):
    return jnp.concatenate(
        [rows_ref[pl.ds(first + k, devices, stride=sent), :] for k in range(keys)], 0
    )


def dot(left, right, left_dim, right_dim):
    return lax.dot_general(
        left,
        right,
        (((left_dim,), (right_dim,)), ((), ())),
        preferred_element_type=jnp.float32,
    )


def split(value, terms):
    result = []
    for _ in range(terms):
        result.append(value.astype(jnp.bfloat16))
        value = value - result[-1].astype(jnp.float32)
    return result


def rows_by_tokens(rows, tokens):
    count = rows.shape[0]
    large, middle, small = split(rows, 3)
    token_large, token_middle, token_small = split(tokens, 3)
    left = jnp.concatenate(
        [
            jnp.concatenate([large, large], 1),
            jnp.concatenate([middle, middle], 1),
            jnp.concatenate([small, jnp.zeros_like(small)], 1),
        ],
        0,
    )
    main = dot(left, jnp.concatenate([token_large, token_middle], 1), 1, 1)
    rest = dot(large, token_small, 1, 1)
    return main[0:count] + (main[count : 2 * count] + (main[2 * count :] + rest))


def sum_over_tokens(left, right):
    count, width = left.shape[0], right.shape[1]
    every = dot(jnp.concatenate(split(left, 2), 0), jnp.concatenate(split(right, 2), 1), 1, 0)
    top, bottom = every[0:count], every[count:]
    return top[:, 0:width] + (top[:, width:] + bottom[:, 0:width] + bottom[:, width:])


def mix_rows(weights, rows):
    width = rows.shape[1]
    right = jnp.concatenate(split(rows, 2), 1)
    every = dot(jnp.concatenate(split(weights, 2), 0), jnp.concatenate([right, right], 0), 0, 0)
    return every[:, 0:width] + every[:, width:]


def mix_rows_exactly(weights, rows):
    width = rows.shape[1]
    large, middle, small = split(weights, 3)
    row_large, row_middle, row_small = split(rows, 3)
    zero = jnp.zeros_like(row_large)
    right = jnp.concatenate(
        [
            jnp.concatenate([row_large, row_large, row_large, zero], 0),
            jnp.concatenate([row_middle, row_middle, zero, row_small], 0),
        ],
        1,
    )
    every = dot(jnp.concatenate([large, middle, small, large], 0), right, 0, 0)
    return every[:, 0:width] + every[:, width:]


def attention_kernel(bands, sectors, width, keys, *refs):
    part_refs = refs[:bands]
    rows_ref, taps_ref, terms_ref = refs[bands : bands + 3]
    query_grad_refs = refs[bands + 3 : 2 * bands + 3]
    query_ref, weighted_ref, grad_ref, out_ref = refs[2 * bands + 3 :]
    band = lax.axis_index("lat")
    sector = lax.axis_index("lon")
    rows, columns = part_refs[0].shape[1:3]
    lines = rows * bands
    tokens = lines * columns
    edge = SUBLANES
    scale = HD ** (-0.5)
    weights = row_weights(lines)
    heads = width // HD
    devices = bands * sectors
    key_total = devices * keys
    sent = block_rows(bands, keys, rows)

    for step, part_ref in enumerate(part_refs):
        start = source(band, step, bands) * rows
        query_ref[pl.ds(start, rows)] = part_ref[0]
        weighted_ref[pl.ds(start + 1, rows), edge : edge + columns, :] = part_ref[1]
    before = lax.rem(sector + sectors - 1, sectors)
    after = lax.rem(sector + 1, sectors)
    for line in range(lines):
        b, r = divmod(line, rows)
        r = 2 * keys + r
        inner = weighted_ref[1 + line, edge : edge + columns, :]
        weighted_ref[1 + line, edge : edge + columns, :] = inner * weights[line]
        left = rows_ref[pl.ds((b * sectors + before) * sent + r, 1), :]
        right = rows_ref[pl.ds((b * sectors + after) * sent + r, 1), :]
        weighted_ref[1 + line, edge - 1 : edge, :] = left * weights[line]
        weighted_ref[1 + line, edge + columns : edge + columns + 1, :] = right * weights[line]
    zeros = jnp.zeros(weighted_ref.shape[1:], jnp.float32)
    weighted_ref[0] = zeros
    weighted_ref[lines + 1] = zeros

    own_lanes = pl.ds(pl.multiple_of(band * width, width), width)
    taps = [taps_ref[t : t + 1, own_lanes] for t in range(len(OFFSETS))]

    def shifted(line, offset):
        a, b = offset
        return weighted_ref[1 + line - a, edge - b : edge - b + columns, :]

    for line in range(lines):
        total = shifted(line, (0, 0))
        for tap, offset in zip(taps, OFFSETS):
            total = total + tap * shifted(line, offset)
        grad_ref[line] = total

    key_heads = heads_of(rows_from_all(rows_ref, 0, keys, devices, sent), width)
    value_heads = heads_of(rows_from_all(rows_ref, keys, keys, devices, sent), width)
    query = query_ref[...].reshape(tokens, width)
    grad = grad_ref[...].reshape(tokens, width)

    logits = rows_by_tokens(key_heads, query) * scale
    prob_list = []
    for h in range(heads):
        part = logits[h * key_total : (h + 1) * key_total]
        raised = jnp.exp(part - jnp.max(part, 0, keepdims=True))
        prob_list.append(raised / jnp.sum(raised, 0, keepdims=True))
    probs = jnp.concatenate(prob_list, 0)
    out_ref[...] = mix_rows(probs, value_heads).reshape(lines, columns, width)
    prob_grad = rows_by_tokens(value_heads, grad)
    logit_grad_list = []
    for h in range(heads):
        part = prob_grad[h * key_total : (h + 1) * key_total]
        row_dot = jnp.sum(prob_list[h] * part, 0, keepdims=True)
        logit_grad_list.append(prob_list[h] * (part - row_dot))
    logit_grad = jnp.concatenate(logit_grad_list, 0)

    key_grad = own_heads(sum_over_tokens(logit_grad, query), width, key_total) * scale
    value_grad = own_heads(sum_over_tokens(probs, grad), width, key_total)

    sums = [jnp.zeros((SUBLANES, width), jnp.float32) for _ in OFFSETS]
    for line in range(lines):
        out_line = out_ref[line]
        for t, offset in enumerate(OFFSETS):
            product = out_line * shifted(line, offset)
            for c in range(0, columns, SUBLANES):
                sums[t] = sums[t] + product[c : c + SUBLANES]
    tap_sum = jnp.concatenate([jnp.sum(s, 0, keepdims=True) for s in sums], 0)
    used = term_rows(keys)
    for k in range(keys):
        mine = slice(k * devices, (k + 1) * devices)
        terms_ref[pl.ds(k, devices, stride=used), :] = key_grad[mine]
        terms_ref[pl.ds(keys + k, devices, stride=used), :] = value_grad[mine]
    for device in range(devices):
        terms_ref[device * used + 2 * keys : (device + 1) * used, :] = tap_sum

    out_ref[...] = (mix_rows_exactly(logit_grad, key_heads) * scale).reshape(out_ref.shape)
    for step, part_ref in enumerate(query_grad_refs):
        part_ref[...] = out_ref[pl.ds(partner(band, step, bands) * rows, rows)]


def finish_kernel(bands, sectors, width, keys, *refs):
    part_refs = refs[:bands]
    terms_ref, query_ref, key_ref, value_ref, taps_ref = refs[bands:]
    band = lax.axis_index("lat")
    devices = bands * sectors
    rows, columns = query_ref.shape[:2]
    for step, part_ref in enumerate(part_refs):
        lanes = pl.ds(pl.multiple_of(source(band, step, bands) * width, width), width)
        query_ref[:, :, lanes] = part_ref[...]
    used = term_rows(keys)
    parts = []
    for to_band in range(bands):
        lanes = slice(to_band * width, (to_band + 1) * width)
        part = jnp.zeros((used, width), jnp.float32)
        for sector in range(sectors):
            start = (to_band * sectors + sector) * used
            part = part + terms_ref[start : start + used, :]
        key_ref[:, lanes] = part[0:keys]
        value_ref[:, lanes] = part[keys : 2 * keys]
        parts.append(part[2 * keys : used])
    tap_sum = jnp.concatenate(parts, 1)
    mean = jnp.sum(tap_sum * tap_sum, keepdims=True) / (len(OFFSETS) * width * bands)
    taps_ref[...] = tap_sum / jnp.sqrt(mean + 1e-06)


def split_heads_body(queries, key_rows, value_rows, cotangent, conv_taps):
    rows, columns, channels = queries.shape
    bands = lax.axis_size("lat")
    sectors = lax.axis_size("lon")
    devices = bands * sectors
    keys = key_rows.shape[0]
    width = channels // bands
    lines = rows * bands

    sent_rows = block_rows(bands, keys, rows)
    part_shape = (2, rows, columns, width)
    anywhere = pl.BlockSpec(memory_space=pl.ANY)
    here = pl.BlockSpec(memory_space=pltpu.VMEM)
    row_blocks, *parts = pl.pallas_call(
        functools.partial(pack_kernel, bands, sectors, width, keys),
        out_shape=[
            jax.ShapeDtypeStruct(s, jnp.float32)
            for s in [(devices * sent_rows, width)] + [part_shape] * bands
        ],
        in_specs=[anywhere] * 4,
        out_specs=[anywhere] + [here] * bands,
        scratch_shapes=[
            pltpu.VMEM((keys, channels), jnp.float32),
            pltpu.VMEM((keys, channels), jnp.float32),
            pltpu.VMEM((rows, 1, channels), jnp.float32),
            pltpu.VMEM((rows, 1, channels), jnp.float32),
            pltpu.VMEM((devices * sent_rows, width), jnp.float32),
            pltpu.SemaphoreType.DMA((4 + 3 * bands,)),
        ],
        compiler_params=pltpu.CompilerParams(vmem_limit_bytes=VMEM_LIMIT),
    )(*[in_hbm(x) for x in (key_rows, value_rows, queries, cotangent)])
    row_blocks = to_all(row_blocks, devices)
    parts = exchange_all(parts, bands, ahead=True)

    grid = (lines, columns, width)
    heads = width // HD
    terms, *grad_parts = vmem_call(
        functools.partial(attention_kernel, bands, sectors, width, keys),
        [(devices * term_rows(keys), width)] + [(rows, columns, width)] * bands,
        [
            grid,
            (lines + 2, columns + 2 * SUBLANES, width),
            grid,
            grid,
        ],
    )(*parts, row_blocks, conv_taps)

    terms = to_all(terms, devices)
    grad_parts = exchange_all(grad_parts, bands, ahead=False)
    query_grad, key_grad, value_grad, tap_update = pl.pallas_call(
        functools.partial(finish_kernel, bands, sectors, width, keys),
        out_shape=[
            jax.ShapeDtypeStruct(s, jnp.float32)
            for s in (queries.shape, key_rows.shape, value_rows.shape, conv_taps.shape)
        ],
        compiler_params=pltpu.CompilerParams(vmem_limit_bytes=VMEM_LIMIT),
    )(*grad_parts, terms)
    return (query_grad, key_grad, value_grad, tap_update)


def extended(value, sides, width):
    for axis, dim in sides:
        peers, length = (lax.axis_size(axis), value.shape[dim])
        up = [(i, (i + 1) % peers) for i in range(peers)]
        down = [(j, i) for i, j in up]
        last = lax.slice_in_dim(value, length - width, length, axis=dim)
        initial = lax.slice_in_dim(value, 0, width, axis=dim)
        before = lax.ppermute(last, axis, up)
        after = lax.ppermute(initial, axis, down)
        value = jnp.concatenate([before, value, after], axis=dim)
    return value


def split_heads(matrix):
    return matrix.reshape(matrix.shape[0], -1, HD)


def latitude_weights(row_count, band_index, band_count):
    line_total = row_count * band_count
    centres = (jnp.arange(line_total, dtype=jnp.float32) + 0.5) * (jnp.pi / line_total)
    mean_cosine = jnp.sum(jnp.sin(centres)) / line_total
    mine = (band_index * row_count + jnp.arange(row_count, dtype=jnp.int32)).astype(jnp.float32)
    return jnp.sin((mine + 0.5) * (jnp.pi / line_total)) / mean_cosine


def close_poles(padded, row_dim, band_index, band_count):
    height = padded.shape[row_dim]
    positions = jnp.arange(height)
    outside = (positions == 0) & (band_index == 0) | (positions == height - 1) & (
        band_index == band_count - 1
    )
    shape_mask = [1] * padded.ndim
    shape_mask[row_dim] = height
    return jnp.where(outside.reshape(shape_mask), 0.0, padded)


def spread_taps(weighted, grad_padded, conv_taps):
    row_count, col_count = (weighted.shape[0], weighted.shape[1])
    result = weighted
    for tap_index, (shift_row, shift_col) in enumerate(OFFSETS):
        result = (
            result
            + conv_taps[tap_index]
            * grad_padded[
                1 - shift_row : 1 - shift_row + row_count, 1 - shift_col : 1 - shift_col + col_count
            ]
        )
    return result


def tap_terms(weighted, out_padded):
    row_count, col_count = (weighted.shape[0], weighted.shape[1])
    term_list = []
    for shift_row, shift_col in OFFSETS:
        term_list.append(
            jnp.sum(
                out_padded[
                    1 + shift_row : 1 + shift_row + row_count,
                    1 + shift_col : 1 + shift_col + col_count,
                ]
                * weighted,
                axis=(0, 1),
            )
        )
    return jnp.stack(term_list)


def group_logits(query_part, key_part):
    return jnp.einsum(
        "qhd,khd->hqk", split_heads(query_part), split_heads(key_part), precision=HIGH
    ) * HD ** (-0.5)


def whole_rows_body(queries, key_rows, value_rows, cotangent, conv_taps):
    row_count, col_count, channels = queries.shape
    band_count = lax.axis_size("lat")
    band_index = lax.axis_index("lat")
    weighted = cotangent * latitude_weights(row_count, band_index, band_count)[:, None, None]
    paired_rows = jnp.concatenate([key_rows, value_rows], 1)
    paired_all = lax.all_gather(paired_rows, ("lat", "lon"), axis=0, tiled=True)
    key_all = paired_all[:, :channels]
    value_all = paired_all[:, channels:]
    token_count = row_count * col_count
    key_count = key_all.shape[0]
    query_flat = queries.reshape(token_count, channels)
    group_width = 2 * HD
    group_count = channels // group_width
    outputs = []
    peaks = []
    sums_soft = []
    for group_index in range(group_count):
        col_start = group_index * group_width
        col_stop = col_start + group_width
        logits = group_logits(query_flat[:, col_start:col_stop], key_all[:, col_start:col_stop])
        row_peak = jnp.max(logits, -1, keepdims=True)
        raised = jnp.exp(logits - row_peak)
        normaliser = jnp.sum(raised, -1, keepdims=True)
        soft_weights = raised / normaliser
        outputs.append(
            jnp.einsum(
                "hqk,khd->qhd",
                soft_weights,
                split_heads(value_all[:, col_start:col_stop]),
                precision=HIGH,
            ).reshape(token_count, group_width)
        )
        peaks.append(row_peak)
        sums_soft.append(normaliser)
    out_flat = jnp.concatenate(outputs, 1)
    out_grid = out_flat.reshape(row_count, col_count, channels)
    both_padded = close_poles(
        extended(jnp.stack([weighted, out_grid]), (("lat", 1), ("lon", 2)), 1),
        1,
        band_index,
        band_count,
    )
    grad_padded = both_padded[0]
    out_padded = both_padded[1]
    out_grad = spread_taps(weighted, grad_padded, conv_taps)
    tap_sum = lax.psum(tap_terms(weighted, out_padded), ("lat", "lon"))
    tap_update = tap_sum / jnp.sqrt(jnp.mean(tap_sum * tap_sum) + 1e-06)
    grad_flat = out_grad.reshape(token_count, channels)
    query_parts = []
    key_parts = []
    value_parts = []
    for group_index in range(group_count):
        col_start = group_index * group_width
        col_stop = col_start + group_width
        query_heads = split_heads(query_flat[:, col_start:col_stop])
        key_heads = split_heads(key_all[:, col_start:col_stop])
        logits = jnp.einsum("qhd,khd->hqk", query_heads, key_heads, precision=HIGH) * HD ** (-0.5)
        soft_weights = jnp.exp(logits - peaks[group_index]) / sums_soft[group_index]
        grad_heads = split_heads(grad_flat[:, col_start:col_stop])
        value_parts.append(
            jnp.einsum("hqk,qhd->khd", soft_weights, grad_heads, precision=HIGH).reshape(
                key_count, group_width
            )
        )
        prob_grad = jnp.einsum(
            "qhd,khd->hqk",
            grad_heads,
            split_heads(value_all[:, col_start:col_stop]),
            precision=HIGH,
        )
        row_dot = jnp.transpose(
            jnp.sum(grad_heads * split_heads(out_flat[:, col_start:col_stop]), -1)
        )[:, :, None]
        logit_grad = soft_weights * (prob_grad - row_dot)
        query_parts.append(
            (
                jnp.einsum("hqk,khd->qhd", logit_grad, key_heads, precision=HIGH) * HD ** (-0.5)
            ).reshape(token_count, group_width)
        )
        key_parts.append(
            (
                jnp.einsum("hqk,qhd->khd", logit_grad, query_heads, precision=HIGH) * HD ** (-0.5)
            ).reshape(key_count, group_width)
        )
    paired_terms = jnp.concatenate(key_parts + value_parts, 1)
    paired_band = lax.psum_scatter(paired_terms, "lat", scatter_dimension=0, tiled=True)
    paired_grad = lax.psum_scatter(paired_band, "lon", scatter_dimension=0, tiled=True)
    key_grad = paired_grad[:, :channels]
    value_grad = paired_grad[:, channels:]
    query_grad = jnp.concatenate(query_parts, 1).reshape(row_count, col_count, channels)
    return (query_grad, key_grad, value_grad, tap_update)


def body(queries, key_rows, value_rows, cotangent, conv_taps):
    bands = lax.axis_size("lat")
    sectors = lax.axis_size("lon")
    rows, columns, channels = queries.shape
    whole_heads = channels % (bands * LANES) == 0
    whole_tiles = columns % SUBLANES == 0 and (rows * columns) % LANES == 0
    if whole_heads and whole_tiles and sectors > 2:
        return split_heads_body(queries, key_rows, value_rows, cotangent, conv_taps)
    return whole_rows_body(queries, key_rows, value_rows, cotangent, conv_taps)


def solution(mesh):
    placed = (
        P("lat", "lon", None),
        P(("lat", "lon"), None),
        P(("lat", "lon"), None),
        P("lat", "lon", None),
        P(),
    )
    return jax.shard_map(
        body,
        mesh=mesh,
        in_specs=placed,
        out_specs=(P("lat", "lon", None), P(("lat", "lon"), None), P(("lat", "lon"), None), P()),
        check_vma=False,
    )
```

```python
import functools

import jax
import jax.numpy as jnp
import numpy as np
from jax import lax
from jax.experimental import pallas as pl
from jax.experimental.pallas import tpu as pltpu
from jax.sharding import PartitionSpec as P

HD = 64
LANES = 128
SUBLANES = 8
VMEM_LIMIT = 16 * 1024 * 1024

HIGH = lax.Precision.HIGHEST
OFFSETS = ((-1, -1), (-1, 0), (-1, 1), (0, -1), (0, 0), (0, 1), (1, -1), (1, 0), (1, 1))


def partner(index, step, peers):
    if peers & (peers - 1) == 0:
        return index ^ (peers - 1 - step if 0 < step < peers - 1 else step)
    return lax.rem(index + step, peers) if not isinstance(index, int) else (index + step) % peers


def source(index, step, peers):
    return partner(index, step if peers & (peers - 1) == 0 else peers - step, peers)


def exchange(value, step, peers):
    return lax.ppermute(value, "lat", [(i, partner(i, step, peers)) for i in range(peers)])


def to_all(blocks, devices):
    rows, width = blocks.shape
    blocks = blocks.reshape(devices, rows // devices, 1, width)
    return lax.all_to_all(blocks, ("lat", "lon"), 0, 0, tiled=True).reshape(rows, width)


def row_weights(line_total):
    cosine = np.sin((np.arange(line_total, dtype=np.float64) + 0.5) * (np.pi / line_total))
    return [float(w) for w in cosine / np.mean(cosine)]


def vmem_call(kernel, out_shapes, scratch=()):
    return pl.pallas_call(
        kernel,
        out_shape=[jax.ShapeDtypeStruct(s, jnp.float32) for s in out_shapes],
        scratch_shapes=[pltpu.VMEM(s, jnp.float32) for s in scratch],
        compiler_params=pltpu.CompilerParams(vmem_limit_bytes=VMEM_LIMIT),
    )


def arrival_kernel(part_ref, out_ref):
    out_ref[...] = part_ref[...]


def exchange_all(parts, bands, ahead):
    last = exchange(parts[-1], bands - 1, bands)
    cost = pl.CostEstimate(flops=10**10, bytes_accessed=10**6, transcendentals=0)
    (last,) = pl.pallas_call(
        arrival_kernel,
        out_shape=[jax.ShapeDtypeStruct(last.shape, jnp.float32)],
        cost_estimate=cost if ahead else None,
        compiler_params=pltpu.CompilerParams(vmem_limit_bytes=VMEM_LIMIT),
    )(last)
    return [parts[0]] + [exchange(parts[s], s, bands) for s in range(1, bands - 1)] + [last]


def block_rows(bands, keys, rows):
    return 2 * keys + rows


def term_rows(keys):
    return 2 * keys + len(OFFSETS)


def in_hbm(array):
    return pltpu.with_memory_space_constraint(array, pltpu.HBM)


def pack_kernel(bands, sectors, width, keys, *refs):
    key_ref, value_ref, query_ref, cotangent_ref, sent_ref = refs[:5]
    part_refs = refs[5 : 5 + bands]
    key_own, value_own, first_own, last_own, block_ref, sems = refs[5 + bands :]
    band = lax.axis_index("lat")
    sector = lax.axis_index("lon")
    rows, columns = query_ref.shape[:2]
    sent = block_rows(bands, keys, rows)

    small = [
        pltpu.make_async_copy(source_ref, target_ref, sems.at[i])
        for i, (source_ref, target_ref) in enumerate(
            (
                (key_ref, key_own),
                (value_ref, value_own),
                (cotangent_ref.at[:, 0:1, :], first_own),
                (cotangent_ref.at[:, columns - 1 : columns, :], last_own),
            )
        )
    ]
    for copy in small:
        copy.start()
    large = []
    for step, part_ref in enumerate(part_refs):
        lanes = pl.ds(pl.multiple_of(partner(band, step, bands) * width, width), width)
        for i, array_ref in enumerate((query_ref, cotangent_ref)):
            large.append(
                pltpu.make_async_copy(
                    array_ref.at[:, :, lanes], part_ref.at[i], sems.at[len(small) + len(large)]
                )
            )
    for copy in large:
        copy.start()
    for copy in small:
        copy.wait()
    sends = []
    for to_band in range(bands):
        lanes = slice(to_band * width, (to_band + 1) * width)
        key = key_own[:, lanes]
        value = value_own[:, lanes]
        first = first_own[:, 0, lanes]
        last = last_own[:, 0, lanes]
        for to_sector in range(sectors):
            device = to_band * sectors + to_sector
            is_next = lax.rem(to_sector - sector + sectors, sectors) == 1
            start = device * sent
            block_ref[start : start + keys, :] = key
            start = start + keys
            block_ref[start : start + keys, :] = value
            block_ref[start + keys : start + keys + rows, :] = jnp.where(is_next, last, first)
        group = pl.ds(to_band * sectors * sent, sectors * sent)
        sends.append(
            pltpu.make_async_copy(
                block_ref.at[group],
                sent_ref.at[group],
                sems.at[len(small) + len(large) + to_band],
            )
        )
        sends[-1].start()
    for copy in large + sends:
        copy.wait()


def heads_of(matrix, width):
    lane = lax.broadcasted_iota(jnp.int32, matrix.shape, 1)
    return jnp.concatenate(
        [
            jnp.where((lane >= h * HD) & (lane < (h + 1) * HD), matrix, 0.0)
            for h in range(width // HD)
        ],
        0,
    )


def own_heads(matrix, width, keys):
    lane = lax.broadcasted_iota(jnp.int32, (keys, width), 1)
    result = matrix[0:keys]
    for h in range(1, width // HD):
        result = jnp.where(lane >= h * HD, matrix[h * keys : (h + 1) * keys], result)
    return result


def rows_from_all(rows_ref, first, keys, devices, sent):
    return jnp.concatenate(
        [rows_ref[pl.ds(first + k, devices, stride=sent), :] for k in range(keys)], 0
    )


def dot(left, right, left_dim, right_dim):
    return lax.dot_general(
        left,
        right,
        (((left_dim,), (right_dim,)), ((), ())),
        preferred_element_type=jnp.float32,
    )


def split(value, terms):
    result = []
    for _ in range(terms):
        result.append(value.astype(jnp.bfloat16))
        value = value - result[-1].astype(jnp.float32)
    return result


def rows_by_tokens(rows, tokens):
    count = rows.shape[0]
    large, middle, small = split(rows, 3)
    token_large, token_middle, token_small = split(tokens, 3)
    left = jnp.concatenate(
        [
            jnp.concatenate([large, large], 1),
            jnp.concatenate([middle, middle], 1),
            jnp.concatenate([small, jnp.zeros_like(small)], 1),
        ],
        0,
    )
    main = dot(left, jnp.concatenate([token_large, token_middle], 1), 1, 1)
    rest = dot(large, token_small, 1, 1)
    return main[0:count] + (main[count : 2 * count] + (main[2 * count :] + rest))


def sum_over_tokens(left, right):
    count, width = left.shape[0], right.shape[1]
    every = dot(jnp.concatenate(split(left, 2), 0), jnp.concatenate(split(right, 2), 1), 1, 0)
    top, bottom = every[0:count], every[count:]
    return top[:, 0:width] + (top[:, width:] + bottom[:, 0:width] + bottom[:, width:])


def mix_rows(weights, rows):
    width = rows.shape[1]
    right = jnp.concatenate(split(rows, 2), 1)
    every = dot(jnp.concatenate(split(weights, 2), 0), jnp.concatenate([right, right], 0), 0, 0)
    return every[:, 0:width] + every[:, width:]


def mix_rows_exactly(weights, rows):
    width = rows.shape[1]
    large, middle, small = split(weights, 3)
    row_large, row_middle, row_small = split(rows, 3)
    zero = jnp.zeros_like(row_large)
    right = jnp.concatenate(
        [
            jnp.concatenate([row_large, row_large, row_large, zero], 0),
            jnp.concatenate([row_middle, row_middle, zero, row_small], 0),
        ],
        1,
    )
    every = dot(jnp.concatenate([large, middle, small, large], 0), right, 0, 0)
    return every[:, 0:width] + every[:, width:]


def attention_kernel(bands, sectors, width, keys, *refs):
    part_refs = refs[:bands]
    rows_ref, taps_ref, terms_ref = refs[bands : bands + 3]
    query_grad_refs = refs[bands + 3 : 2 * bands + 3]
    query_ref, weighted_ref, grad_ref, out_ref = refs[2 * bands + 3 :]
    band = lax.axis_index("lat")
    sector = lax.axis_index("lon")
    rows, columns = part_refs[0].shape[1:3]
    lines = rows * bands
    tokens = lines * columns
    edge = SUBLANES
    scale = HD ** (-0.5)
    weights = row_weights(lines)
    heads = width // HD
    devices = bands * sectors
    key_total = devices * keys
    sent = block_rows(bands, keys, rows)

    for step, part_ref in enumerate(part_refs):
        start = source(band, step, bands) * rows
        query_ref[pl.ds(start, rows)] = part_ref[0]
        weighted_ref[pl.ds(start + 1, rows), edge : edge + columns, :] = part_ref[1]
    before = lax.rem(sector + sectors - 1, sectors)
    after = lax.rem(sector + 1, sectors)
    for line in range(lines):
        b, r = divmod(line, rows)
        r = 2 * keys + r
        inner = weighted_ref[1 + line, edge : edge + columns, :]
        weighted_ref[1 + line, edge : edge + columns, :] = inner * weights[line]
        left = rows_ref[pl.ds((b * sectors + before) * sent + r, 1), :]
        right = rows_ref[pl.ds((b * sectors + after) * sent + r, 1), :]
        weighted_ref[1 + line, edge - 1 : edge, :] = left * weights[line]
        weighted_ref[1 + line, edge + columns : edge + columns + 1, :] = right * weights[line]
    zeros = jnp.zeros(weighted_ref.shape[1:], jnp.float32)
    weighted_ref[0] = zeros
    weighted_ref[lines + 1] = zeros

    own_lanes = pl.ds(pl.multiple_of(band * width, width), width)
    taps = [taps_ref[t : t + 1, own_lanes] for t in range(len(OFFSETS))]

    def shifted(line, offset):
        a, b = offset
        return weighted_ref[1 + line - a, edge - b : edge - b + columns, :]

    for line in range(lines):
        total = shifted(line, (0, 0))
        for tap, offset in zip(taps, OFFSETS):
            total = total + tap * shifted(line, offset)
        grad_ref[line] = total

    key_heads = heads_of(rows_from_all(rows_ref, 0, keys, devices, sent), width)
    value_heads = heads_of(rows_from_all(rows_ref, keys, keys, devices, sent), width)
    query = query_ref[...].reshape(tokens, width)
    grad = grad_ref[...].reshape(tokens, width)

    logits = rows_by_tokens(key_heads, query) * scale
    prob_list = []
    for h in range(heads):
        part = logits[h * key_total : (h + 1) * key_total]
        raised = jnp.exp(part - jnp.max(part, 0, keepdims=True))
        prob_list.append(raised * (1.0 / jnp.sum(raised, 0, keepdims=True)))
    probs = jnp.concatenate(prob_list, 0)
    out_ref[...] = mix_rows(probs, value_heads).reshape(lines, columns, width)
    prob_grad = rows_by_tokens(value_heads, grad)
    logit_grad_list = []
    for h in range(heads):
        part = prob_grad[h * key_total : (h + 1) * key_total]
        row_dot = jnp.sum(prob_list[h] * part, 0, keepdims=True)
        logit_grad_list.append(prob_list[h] * (part - row_dot))
    logit_grad = jnp.concatenate(logit_grad_list, 0)

    key_grad = own_heads(sum_over_tokens(logit_grad, query), width, key_total) * scale
    value_grad = own_heads(sum_over_tokens(probs, grad), width, key_total)

    sums = [jnp.zeros((SUBLANES, width), jnp.float32) for _ in OFFSETS]
    for line in range(lines):
        out_line = out_ref[line]
        for t, offset in enumerate(OFFSETS):
            product = out_line * shifted(line, offset)
            for c in range(0, columns, SUBLANES):
                sums[t] = sums[t] + product[c : c + SUBLANES]
    tap_sum = jnp.concatenate([jnp.sum(s, 0, keepdims=True) for s in sums], 0)
    used = term_rows(keys)
    for k in range(keys):
        mine = slice(k * devices, (k + 1) * devices)
        terms_ref[pl.ds(k, devices, stride=used), :] = key_grad[mine]
        terms_ref[pl.ds(keys + k, devices, stride=used), :] = value_grad[mine]
    for device in range(devices):
        terms_ref[device * used + 2 * keys : (device + 1) * used, :] = tap_sum

    out_ref[...] = (mix_rows_exactly(logit_grad, key_heads) * scale).reshape(out_ref.shape)
    for step, part_ref in enumerate(query_grad_refs):
        part_ref[...] = out_ref[pl.ds(partner(band, step, bands) * rows, rows)]


def finish_kernel(bands, sectors, width, keys, *refs):
    part_refs = refs[:bands]
    terms_ref, query_ref, key_ref, value_ref, taps_ref = refs[bands:]
    band = lax.axis_index("lat")
    devices = bands * sectors
    rows, columns = query_ref.shape[:2]
    for step, part_ref in enumerate(part_refs):
        lanes = pl.ds(pl.multiple_of(source(band, step, bands) * width, width), width)
        query_ref[:, :, lanes] = part_ref[...]
    used = term_rows(keys)
    parts = []
    for to_band in range(bands):
        lanes = slice(to_band * width, (to_band + 1) * width)
        rows_of = [
            terms_ref[(to_band * sectors + sector) * used : (to_band * sectors + sector + 1) * used, :]
            for sector in range(sectors)
        ]
        while len(rows_of) > 1:
            rows_of = [sum(rows_of[i : i + 2]) for i in range(0, len(rows_of), 2)]
        part = rows_of[0]
        key_ref[:, lanes] = part[0:keys]
        value_ref[:, lanes] = part[keys : 2 * keys]
        parts.append(part[2 * keys : used])
    tap_sum = jnp.concatenate(parts, 1)
    mean = jnp.sum(tap_sum * tap_sum, keepdims=True) / (len(OFFSETS) * width * bands)
    taps_ref[...] = tap_sum / jnp.sqrt(mean + 1e-06)


def split_heads_body(queries, key_rows, value_rows, cotangent, conv_taps):
    rows, columns, channels = queries.shape
    bands = lax.axis_size("lat")
    sectors = lax.axis_size("lon")
    devices = bands * sectors
    keys = key_rows.shape[0]
    width = channels // bands
    lines = rows * bands

    sent_rows = block_rows(bands, keys, rows)
    part_shape = (2, rows, columns, width)
    anywhere = pl.BlockSpec(memory_space=pl.ANY)
    here = pl.BlockSpec(memory_space=pltpu.VMEM)
    row_blocks, *parts = pl.pallas_call(
        functools.partial(pack_kernel, bands, sectors, width, keys),
        out_shape=[
            jax.ShapeDtypeStruct(s, jnp.float32)
            for s in [(devices * sent_rows, width)] + [part_shape] * bands
        ],
        in_specs=[anywhere] * 4,
        out_specs=[anywhere] + [here] * bands,
        scratch_shapes=[
            pltpu.VMEM((keys, channels), jnp.float32),
            pltpu.VMEM((keys, channels), jnp.float32),
            pltpu.VMEM((rows, 1, channels), jnp.float32),
            pltpu.VMEM((rows, 1, channels), jnp.float32),
            pltpu.VMEM((devices * sent_rows, width), jnp.float32),
            pltpu.SemaphoreType.DMA((4 + 3 * bands,)),
        ],
        compiler_params=pltpu.CompilerParams(vmem_limit_bytes=VMEM_LIMIT),
    )(*[in_hbm(x) for x in (key_rows, value_rows, queries, cotangent)])
    row_blocks = to_all(row_blocks, devices)
    parts = exchange_all(parts, bands, ahead=True)

    grid = (lines, columns, width)
    heads = width // HD
    terms, *grad_parts = vmem_call(
        functools.partial(attention_kernel, bands, sectors, width, keys),
        [(devices * term_rows(keys), width)] + [(rows, columns, width)] * bands,
        [
            grid,
            (lines + 2, columns + 2 * SUBLANES, width),
            grid,
            grid,
        ],
    )(*parts, row_blocks, conv_taps)

    terms = to_all(terms, devices)
    grad_parts = exchange_all(grad_parts, bands, ahead=False)
    query_grad, key_grad, value_grad, tap_update = pl.pallas_call(
        functools.partial(finish_kernel, bands, sectors, width, keys),
        out_shape=[
            jax.ShapeDtypeStruct(s, jnp.float32)
            for s in (queries.shape, key_rows.shape, value_rows.shape, conv_taps.shape)
        ],
        compiler_params=pltpu.CompilerParams(vmem_limit_bytes=VMEM_LIMIT),
    )(*grad_parts, terms)
    return (query_grad, key_grad, value_grad, tap_update)


def extended(value, sides, width):
    for axis, dim in sides:
        peers, length = (lax.axis_size(axis), value.shape[dim])
        up = [(i, (i + 1) % peers) for i in range(peers)]
        down = [(j, i) for i, j in up]
        last = lax.slice_in_dim(value, length - width, length, axis=dim)
        initial = lax.slice_in_dim(value, 0, width, axis=dim)
        before = lax.ppermute(last, axis, up)
        after = lax.ppermute(initial, axis, down)
        value = jnp.concatenate([before, value, after], axis=dim)
    return value


def split_heads(matrix):
    return matrix.reshape(matrix.shape[0], -1, HD)


def latitude_weights(row_count, band_index, band_count):
    line_total = row_count * band_count
    centres = (jnp.arange(line_total, dtype=jnp.float32) + 0.5) * (jnp.pi / line_total)
    mean_cosine = jnp.sum(jnp.sin(centres)) / line_total
    mine = (band_index * row_count + jnp.arange(row_count, dtype=jnp.int32)).astype(jnp.float32)
    return jnp.sin((mine + 0.5) * (jnp.pi / line_total)) / mean_cosine


def close_poles(padded, row_dim, band_index, band_count):
    height = padded.shape[row_dim]
    positions = jnp.arange(height)
    outside = (positions == 0) & (band_index == 0) | (positions == height - 1) & (
        band_index == band_count - 1
    )
    shape_mask = [1] * padded.ndim
    shape_mask[row_dim] = height
    return jnp.where(outside.reshape(shape_mask), 0.0, padded)


def spread_taps(weighted, grad_padded, conv_taps):
    row_count, col_count = (weighted.shape[0], weighted.shape[1])
    result = weighted
    for tap_index, (shift_row, shift_col) in enumerate(OFFSETS):
        result = (
            result
            + conv_taps[tap_index]
            * grad_padded[
                1 - shift_row : 1 - shift_row + row_count, 1 - shift_col : 1 - shift_col + col_count
            ]
        )
    return result


def tap_terms(weighted, out_padded):
    row_count, col_count = (weighted.shape[0], weighted.shape[1])
    term_list = []
    for shift_row, shift_col in OFFSETS:
        term_list.append(
            jnp.sum(
                out_padded[
                    1 + shift_row : 1 + shift_row + row_count,
                    1 + shift_col : 1 + shift_col + col_count,
                ]
                * weighted,
                axis=(0, 1),
            )
        )
    return jnp.stack(term_list)


def group_logits(query_part, key_part):
    return jnp.einsum(
        "qhd,khd->hqk", split_heads(query_part), split_heads(key_part), precision=HIGH
    ) * HD ** (-0.5)


def whole_rows_body(queries, key_rows, value_rows, cotangent, conv_taps):
    row_count, col_count, channels = queries.shape
    band_count = lax.axis_size("lat")
    band_index = lax.axis_index("lat")
    weighted = cotangent * latitude_weights(row_count, band_index, band_count)[:, None, None]
    paired_rows = jnp.concatenate([key_rows, value_rows], 1)
    paired_all = lax.all_gather(paired_rows, ("lat", "lon"), axis=0, tiled=True)
    key_all = paired_all[:, :channels]
    value_all = paired_all[:, channels:]
    token_count = row_count * col_count
    key_count = key_all.shape[0]
    query_flat = queries.reshape(token_count, channels)
    group_width = 2 * HD
    group_count = channels // group_width
    outputs = []
    peaks = []
    sums_soft = []
    for group_index in range(group_count):
        col_start = group_index * group_width
        col_stop = col_start + group_width
        logits = group_logits(query_flat[:, col_start:col_stop], key_all[:, col_start:col_stop])
        row_peak = jnp.max(logits, -1, keepdims=True)
        raised = jnp.exp(logits - row_peak)
        normaliser = jnp.sum(raised, -1, keepdims=True)
        soft_weights = raised / normaliser
        outputs.append(
            jnp.einsum(
                "hqk,khd->qhd",
                soft_weights,
                split_heads(value_all[:, col_start:col_stop]),
                precision=HIGH,
            ).reshape(token_count, group_width)
        )
        peaks.append(row_peak)
        sums_soft.append(normaliser)
    out_flat = jnp.concatenate(outputs, 1)
    out_grid = out_flat.reshape(row_count, col_count, channels)
    both_padded = close_poles(
        extended(jnp.stack([weighted, out_grid]), (("lat", 1), ("lon", 2)), 1),
        1,
        band_index,
        band_count,
    )
    grad_padded = both_padded[0]
    out_padded = both_padded[1]
    out_grad = spread_taps(weighted, grad_padded, conv_taps)
    tap_sum = lax.psum(tap_terms(weighted, out_padded), ("lat", "lon"))
    tap_update = tap_sum / jnp.sqrt(jnp.mean(tap_sum * tap_sum) + 1e-06)
    grad_flat = out_grad.reshape(token_count, channels)
    query_parts = []
    key_parts = []
    value_parts = []
    for group_index in range(group_count):
        col_start = group_index * group_width
        col_stop = col_start + group_width
        query_heads = split_heads(query_flat[:, col_start:col_stop])
        key_heads = split_heads(key_all[:, col_start:col_stop])
        logits = jnp.einsum("qhd,khd->hqk", query_heads, key_heads, precision=HIGH) * HD ** (-0.5)
        soft_weights = jnp.exp(logits - peaks[group_index]) / sums_soft[group_index]
        grad_heads = split_heads(grad_flat[:, col_start:col_stop])
        value_parts.append(
            jnp.einsum("hqk,qhd->khd", soft_weights, grad_heads, precision=HIGH).reshape(
                key_count, group_width
            )
        )
        prob_grad = jnp.einsum(
            "qhd,khd->hqk",
            grad_heads,
            split_heads(value_all[:, col_start:col_stop]),
            precision=HIGH,
        )
        row_dot = jnp.transpose(
            jnp.sum(grad_heads * split_heads(out_flat[:, col_start:col_stop]), -1)
        )[:, :, None]
        logit_grad = soft_weights * (prob_grad - row_dot)
        query_parts.append(
            (
                jnp.einsum("hqk,khd->qhd", logit_grad, key_heads, precision=HIGH) * HD ** (-0.5)
            ).reshape(token_count, group_width)
        )
        key_parts.append(
            (
                jnp.einsum("hqk,qhd->khd", logit_grad, query_heads, precision=HIGH) * HD ** (-0.5)
            ).reshape(key_count, group_width)
        )
    paired_terms = jnp.concatenate(key_parts + value_parts, 1)
    paired_band = lax.psum_scatter(paired_terms, "lat", scatter_dimension=0, tiled=True)
    paired_grad = lax.psum_scatter(paired_band, "lon", scatter_dimension=0, tiled=True)
    key_grad = paired_grad[:, :channels]
    value_grad = paired_grad[:, channels:]
    query_grad = jnp.concatenate(query_parts, 1).reshape(row_count, col_count, channels)
    return (query_grad, key_grad, value_grad, tap_update)


def body(queries, key_rows, value_rows, cotangent, conv_taps):
    bands = lax.axis_size("lat")
    sectors = lax.axis_size("lon")
    rows, columns, channels = queries.shape
    whole_heads = channels % (bands * LANES) == 0
    whole_tiles = columns % SUBLANES == 0 and (rows * columns) % LANES == 0
    if whole_heads and whole_tiles and sectors > 2:
        return split_heads_body(queries, key_rows, value_rows, cotangent, conv_taps)
    return whole_rows_body(queries, key_rows, value_rows, cotangent, conv_taps)


def solution(mesh):
    placed = (
        P("lat", "lon", None),
        P(("lat", "lon"), None),
        P(("lat", "lon"), None),
        P("lat", "lon", None),
        P(),
    )
    return jax.shard_map(
        body,
        mesh=mesh,
        in_specs=placed,
        out_specs=(P("lat", "lon", None), P(("lat", "lon"), None), P(("lat", "lon"), None), P()),
        check_vma=False,
    )
```
